32 devices in a mesh: rows: 4 (over y, x), tp: 8 (over z, core).
Axes of the slice: x: 2, y: 2, z: 4, core: 2. Of those that a mesh axis runs over, the one named last changes fastest.
Arguments:
- hidden_in: bfloat16 [4, 2048, 2048], P('rows', 'tp'), may hold values from -6 to 6
- segment_ids: int32 [4, 2048], P('rows', 'tp'), may hold values from 0 to 7, never falling along the last dimension, each value on 1 to 1024 neighbouring positions
- ln_gain: float32 [2048], replicated, may hold values from 0.5 to 1.5
- ln_bias: float32 [2048], replicated, may hold values from -3 to 3
- w_qkv: bfloat16 [2048, 3, 2048], P(None, None, 'tp'), may hold values from -0.125 to 0.125
- b_qkv: float32 [3, 2048], P(None, 'tp'), may hold values from -3 to 3
- w_out: bfloat16 [2048, 2048], P('tp'), may hold values from -0.5 to 0.5
- out_bias: float32 [2048], replicated, may hold values from -3 to 3
- w_up: bfloat16 [2048, 8192], P(None, 'tp'), may hold values from -0.125 to 0.125
- b_up: float32 [8192], P('tp'), may hold values from -3 to 3
- w_down: bfloat16 [8192, 2048], P('tp'), may hold values from -0.0625 to 0.0625
- cotangent: bfloat16 [4, 2048, 2048], P('rows', 'tp'), may hold values from -6 to 6
Outputs:
- hidden_out: bfloat16 [4, 2048, 2048], P('rows', 'tp')
- grad_input: bfloat16 [4, 2048, 2048], P('rows', 'tp')
- grad_ln_gain: float32 [2048], replicated
- grad_ln_bias: float32 [2048], replicated
- grad_w_qkv: float32 [2048, 3, 2048], P(None, None, 'tp')
- grad_b_qkv: float32 [3, 2048], P(None, 'tp')
- grad_w_out: float32 [2048, 2048], P('tp')
- grad_out_bias: float32 [2048], replicated
- grad_w_up: float32 [2048, 8192], P(None, 'tp')
- grad_b_up: float32 [8192], P('tp')
- grad_w_down: float32 [8192, 2048], P('tp')
The draws below stay inside these ranges and needn't reach their ends.
Inputs may be any that keep to these rules, and one draw needn't show every extreme that they name: `segment_ids`: within a row the ids never fall; every document has 1 to 1024 tokens, and one has exactly 1024.
All inputs are finite; a program needn't handle non-finite values.
Results may differ from the reference program's by a relative error of at most 0.012.
The reference program's roundings to bfloat16 on the way count: a program that leaves them out, or rounds other values in their place, can miss the bound.
Values may be sent and summed in bfloat16 or wider, within the bound.
No kernel may reach another device: no remote copies, remote signals or barrier semaphores. Data moves between devices by JAX's collectives and lax.ppermute only.
A program may use at most 256 MiB of HBM per device.

```python
import math
from functools import partial
import jax
import jax.numpy as jnp
import numpy as np
from jax import lax

D = 2048
HEADS = 32
HEAD_DIM = 64
ROT = 32
FF = 8192
LENGTH = 2048
DOCS = 8
BATCH = 4


def block_levels(key, extent, cuts, smallest, high):
    loudness = 1.0
    for dim, parts in cuts:
        draws = jax.random.uniform(jax.random.fold_in(jax.random.fold_in(key, 6), dim), (parts,), jnp.float32, smallest / len(cuts), high / len(cuts))
        loudness = loudness * jnp.repeat(jnp.exp(draws), extent[dim] // parts).reshape((-1,) + (1,) * (len(extent) - 1 - dim))
    return loudness


def length_profile(count, total, most, skew):
    loads = [(1 << 20) // math.isqrt(grade ** skew) + 1 for grade in range(2, count + 1)]
    surplus, holding = total - most - (count - 1), [1] * (count - 1)
    while surplus > 0:
        movable = [i for i in range(count - 1) if holding[i] < most]
        pool, budget = sum([loads[i] for i in movable]), surplus
        for i in movable:
            addition = min(most - holding[i], max(1, budget * loads[i] // pool), surplus)
            holding[i] = holding[i] + addition
            surplus = surplus - addition
    return np.array([most] + holding)


def ragged(stream_key, amount, total, most, lean):
    if amount == 2:
        one = jax.random.randint(stream_key, (), max(1, total - most), min(most, total - 1) + 1)
        return jnp.stack([one, total - one])
    lengths = jnp.asarray(length_profile(amount, total, most, lean), jnp.int32)
    couples = (amount - 1) // 2
    giver, taker = lengths[1:1 + 2 * couples:2], lengths[2:2 + 2 * couples:2]
    slack = jnp.minimum(giver - 1, most - taker)
    moved = jax.random.randint(jax.random.fold_in(stream_key, 1), (couples,), 0, 1 << 20) % (slack + 1)
    lengths = lengths.at[1:1 + 2 * couples:2].set(giver - moved).at[2:2 + 2 * couples:2].set(taker + moved)
    return lengths[jax.random.permutation(jax.random.fold_in(stream_key, 2), amount)]


def gaussian(stream_key, dims, spread, most, cuts=(), held_as=jnp.bfloat16):
    array = jax.random.normal(stream_key, dims, jnp.float32) * spread
    if len(cuts) > 0:
        array = block_levels(stream_key, dims, cuts, -0.22, 0.18) * array
    return jnp.clip(array, min=-most, max=most).astype(held_as)


def setup_inputs(seed: int = 0) -> dict:
    arg_keys = jax.random.split(jax.random.key(seed), 13)
    return {
        "hidden_in": gaussian(arg_keys[0], (BATCH, LENGTH, D), 1.0, 6.0, ((0, 4), (1, 8))),
        "segment_ids": jax.vmap(lambda own: jnp.searchsorted(jnp.cumsum(ragged(own, DOCS, LENGTH, LENGTH // 2, 2)), jnp.arange(LENGTH), side="right"))(jax.random.split(arg_keys[1], BATCH)).reshape((BATCH, LENGTH)).astype(jnp.int32),
        "ln_gain": jnp.clip(1.0 + 0.1 * jax.random.normal(arg_keys[2], (D,), jnp.float32), 0.5, 1.5),
        "ln_bias": gaussian(arg_keys[3], (D,), 0.5, 3.0, (), jnp.float32),
        "w_qkv": gaussian(arg_keys[4], (D, 3, D), D ** -0.5, 0.125, ((2, 8),)),
        "b_qkv": gaussian(arg_keys[5], (3, D), 0.5, 3.0, ((1, 8),), jnp.float32),
        "w_out": gaussian(arg_keys[6], (D, D), (D // 16) ** -0.5, 0.5, ((0, 8),)),
        "out_bias": gaussian(arg_keys[7], (D,), 0.5, 3.0, (), jnp.float32),
        "w_up": gaussian(arg_keys[8], (D, FF), D ** -0.5, 0.125, ((1, 8),)),
        "b_up": gaussian(arg_keys[9], (FF,), 0.5, 3.0, ((0, 8),), jnp.float32),
        "w_down": gaussian(arg_keys[10], (FF, D), FF ** -0.5, 0.0625, ((0, 8),)),
        "cotangent": gaussian(arg_keys[11], (BATCH, LENGTH, D), 1.0, 6.0, ((0, 4), (1, 8))),
    }


EPSILON = 1e-05
NEGATIVE = -1e+30
HIGH = lax.Precision.HIGHEST

@jax.custom_vjp
def low(v):
    return lax.optimization_barrier(v.astype(jnp.bfloat16)).astype(jnp.float32)

@jax.custom_vjp
def low_back(v):
    return v

def low_keep(v):
    return (low(v), None)

def low_pass(kept, grad):
    return (grad,)

def back_keep(v):
    return (v, None)

def back_low(kept, grad):
    return (low(grad),)
low.defvjp(low_keep, low_pass)
low_back.defvjp(back_keep, back_low)

def doc_positions(segments):
    length = segments.shape[-1]
    index_row = jnp.arange(length, dtype=jnp.int32)
    previous = jnp.concatenate([segments[..., :1], segments[..., :-1]], axis=-1)
    marks = jnp.where((index_row == 0) | (segments != previous), index_row, jnp.zeros_like(index_row))
    return index_row - lax.cummax(marks, axis=segments.ndim - 1)

def rotary_tables(positions):
    ladder = jnp.arange(ROT // 2, dtype=jnp.float32)
    inverse = jnp.exp(ladder * (-2.0 * math.log(10000.0) / ROT))
    angles = positions.astype(jnp.float32)[..., None] * inverse
    return (jnp.cos(angles)[..., None, :], jnp.sin(angles)[..., None, :])

def rotate(vectors, cosine, sine):
    quarter = ROT // 2
    first = vectors[..., :quarter]
    second = vectors[..., quarter:ROT]
    remainder = vectors[..., ROT:]
    return jnp.concatenate([first * cosine - second * sine, second * cosine + first * sine, remainder], axis=-1)

def row_forward(params, row_input, row_segments):
    gain, norm_bias, weight_qkv, bias_qkv, weight_out, bias_out, weight_up, bias_up, weight_down = params
    average = lax.optimization_barrier(jnp.mean(row_input, axis=-1, keepdims=True))
    centred = row_input - average
    variance = lax.optimization_barrier(jnp.mean(centred * centred, axis=-1, keepdims=True))
    normed = low(centred * lax.rsqrt(variance + EPSILON) * gain + norm_bias)
    mixed = jnp.dot(normed, weight_qkv.reshape(D, 3 * D), precision=HIGH) + bias_qkv.reshape(3 * D)
    mixed = low_back(mixed).reshape(LENGTH, 3, HEADS, HEAD_DIM)
    cosine, sine = rotary_tables(doc_positions(row_segments))
    queries = low(rotate(mixed[:, 0], cosine, sine))
    key_vecs = low(rotate(mixed[:, 1], cosine, sine))
    value_vecs = low(mixed[:, 2])
    block_rows = min(512, LENGTH)
    key_index = jnp.arange(LENGTH, dtype=jnp.int32)

    def one_block(block_index):
        start = (block_index * block_rows).astype(jnp.int32)
        query_block = lax.dynamic_slice_in_dim(queries, start, block_rows, 0)
        seg_block = lax.dynamic_slice_in_dim(row_segments, start, block_rows, 0)
        query_index = start + jnp.arange(block_rows, dtype=jnp.int32)
        scores = jnp.einsum('qhe,khe->hqk', query_block, key_vecs, precision=HIGH) * 0.125
        scores = low_back(scores)
        allowed = (seg_block[:, None] == row_segments[None, :]) & (key_index[None, :] <= query_index[:, None])
        scores = jnp.where(allowed[None], scores, NEGATIVE)
        probs = low(jax.nn.softmax(scores, axis=-1))
        return jnp.einsum('hqk,khe->qhe', probs, value_vecs, precision=HIGH)
    contexts = lax.map(jax.checkpoint(one_block), jnp.arange(LENGTH // block_rows, dtype=jnp.int32))
    context = low(low_back(contexts.reshape(LENGTH, D)))
    attention = jnp.dot(context, weight_out, precision=HIGH)
    upward = low_back(jnp.dot(normed, weight_up, precision=HIGH) + bias_up)
    activated = low(jax.nn.gelu(upward, approximate=True))
    return row_input + attention + jnp.dot(activated, weight_down, precision=HIGH) + bias_out

def reference(hidden_in, segment_ids, ln_gain, ln_bias, w_qkv, b_qkv, w_out, out_bias, w_up, b_up, w_down, cotangent):
    params = tuple((item.astype(jnp.float32) for item in (ln_gain, ln_bias, w_qkv, b_qkv, w_out, out_bias, w_up, b_up, w_down)))
    inputs = hidden_in.astype(jnp.float32)

    def forward(layer_in, layer_params):
        stepper = jax.checkpoint(partial(row_forward, layer_params))

        def scan_step(carry, pair):
            return (carry, stepper(pair[0], pair[1]))
        return lax.scan(scan_step, jnp.zeros((), jnp.float32), (layer_in, segment_ids))[1]
    outputs, pullback = jax.vjp(forward, inputs, params)
    grad_in, grads = pullback(cotangent.astype(jnp.float32))
    return (outputs.astype(jnp.bfloat16), grad_in.astype(jnp.bfloat16), grads[0], grads[1], grads[2], grads[3], grads[4], grads[5], grads[6], grads[7], grads[8])
```

```python
from functools import partial
import math

import jax
import jax.numpy as jnp
from jax import lax
from jax.experimental import pallas as pl
from jax.experimental.pallas import tpu as pltpu
from jax.sharding import PartitionSpec as P

HEAD_DIM = 64
ROT = 32
EPSILON = 1e-05
NEGATIVE = -1e30
VMEM_BYTES = 56 * 2**20


def lane_heads(rows, width):
    return lax.broadcasted_iota(jnp.int32, (rows, width), 1) // HEAD_DIM


def swap_pairs(x):
    width = x.shape[1]
    lane = lax.broadcasted_iota(jnp.int32, x.shape, 1) % HEAD_DIM
    up = pltpu.roll(x, width - ROT // 2, 1)
    down = pltpu.roll(x, ROT // 2, 1)
    return jnp.where(lane < ROT // 2, up, down)


def mask_bias(starts, key_first, query_first, block):
    key_index = key_first + lax.broadcasted_iota(jnp.int32, (block, block), 0)
    query_index = query_first + lax.broadcasted_iota(jnp.int32, (block, block), 1)
    allowed = (key_index >= starts) & (key_index <= query_index)
    return jnp.where(allowed, 0.0, NEGATIVE).astype(jnp.float32)


NT = (((1,), (1,)), ((), ()))


def forward_kernel(lows, starts, q, k, v, context, lse, v_t, acc):
    block, width = q.shape
    heads = width // HEAD_DIM
    length = k.shape[0]
    i = pl.program_id(0)

    @pl.when(i == 0)
    def _():
        for j in range(length // block):
            rows = pl.ds(j * block, block)
            v_t[:, rows] = v[rows, :].T

    row_heads = lane_heads(block, width)
    scaled = q[...] * 0.125
    masked = [jnp.where(row_heads == h, scaled, 0).astype(jnp.bfloat16) for h in range(heads)]
    acc[...] = jnp.zeros_like(acc)

    def step(j, carry):
        tops, sums = carry
        first = pl.multiple_of(j * block, block)
        keys = k[pl.ds(first, block), :]
        bias = mask_bias(starts[0:1, :], first, i * block, block)
        new_tops, new_sums = [], []
        for h in range(heads):
            rows = pl.ds(h * HEAD_DIM, HEAD_DIM)
            scores = lax.dot_general(keys, masked[h], NT, preferred_element_type=jnp.float32) + bias
            top = jnp.maximum(tops[h], jnp.max(scores, axis=0, keepdims=True))
            weights = jnp.exp(scores - top)
            keep = jnp.exp(tops[h] - top)
            new_tops.append(top)
            new_sums.append(sums[h] * keep + jnp.sum(weights, axis=0, keepdims=True))
            acc[rows, :] = acc[rows, :] * keep + jnp.dot(
                v_t[rows, pl.ds(first, block)],
                weights.astype(jnp.bfloat16),
                preferred_element_type=jnp.float32,
            )
        return tuple(new_tops), tuple(new_sums)

    empty = tuple(jnp.full((1, block), NEGATIVE, jnp.float32) for _ in range(heads))
    nothing = tuple(jnp.zeros((1, block), jnp.float32) for _ in range(heads))
    tops, sums = lax.fori_loop(lows[i], i + 1, step, (empty, nothing))
    for h in range(heads):
        rows = pl.ds(h * HEAD_DIM, HEAD_DIM)
        acc[rows, :] = acc[rows, :] / sums[h]
        lse[h : h + 1, :] = tops[h] + jnp.log(sums[h])
    context[...] = acc[...].T.astype(jnp.bfloat16)


def attend_forward(lows, starts, mixed, block):
    length, triple = mixed.shape
    width = triple // 3
    blocks = length // block
    return pl.pallas_call(
        forward_kernel,
        grid_spec=pltpu.PrefetchScalarGridSpec(
            num_scalar_prefetch=1,
            grid=(blocks,),
            in_specs=[
                pl.BlockSpec((8, block), lambda i, lows: (0, i)),
                pl.BlockSpec((block, width), lambda i, lows: (i, 0)),
                pl.BlockSpec((length, width), lambda i, lows: (0, 1)),
                pl.BlockSpec((length, width), lambda i, lows: (0, 2)),
            ],
            out_specs=[
                pl.BlockSpec((block, width), lambda i, lows: (i, 0)),
                pl.BlockSpec((8, block), lambda i, lows: (0, i)),
            ],
            scratch_shapes=[
                pltpu.VMEM((width, length), jnp.bfloat16),
                pltpu.VMEM((width, block), jnp.float32),
            ],
        ),
        out_shape=[
            jax.ShapeDtypeStruct((length, width), jnp.bfloat16),
            jax.ShapeDtypeStruct((8, length), jnp.float32),
        ],
        compiler_params=pltpu.CompilerParams(vmem_limit_bytes=VMEM_BYTES),
        cost_estimate=pl.CostEstimate(
            flops=2 * length * length * width * 8,
            bytes_accessed=length * width * 8,
            transcendentals=0,
        ),
        name="attend_forward",
    )(lows, starts, mixed, mixed, mixed)


def backward_kernel(
    lows, starts, lse, q, k, v, context, grad, cosine, sine, grad_mixed, k_t, grad_q, grad_k, grad_v
):
    block, width = q.shape
    heads = width // HEAD_DIM
    length = k.shape[0]
    i = pl.program_id(0)
    blocks = length // block

    @pl.when(i == 0)
    def _():
        grad_k[...] = jnp.zeros_like(grad_k)
        grad_v[...] = jnp.zeros_like(grad_v)
        for j in range(blocks):
            rows = pl.ds(j * block, block)
            k_t[:, rows] = k[rows, :].T

    row_heads = lane_heads(block, width)
    scaled = q[...] * 0.125
    grads = grad[...]
    masked_q = [jnp.where(row_heads == h, scaled, 0).astype(jnp.bfloat16) for h in range(heads)]
    masked_g = [jnp.where(row_heads == h, grads, 0).astype(jnp.bfloat16) for h in range(heads)]
    products = (grads.astype(jnp.float32) * context[...].astype(jnp.float32)).T
    inner = [
        jnp.sum(products[h * HEAD_DIM : (h + 1) * HEAD_DIM, :], axis=0, keepdims=True)
        for h in range(heads)
    ]
    grad_q[...] = jnp.zeros_like(grad_q)

    def step(j, carry):
        first = pl.multiple_of(j * block, block)
        here = pl.ds(first, block)
        keys = k[here, :]
        values = v[here, :]
        bias = mask_bias(starts[0:1, :], first, i * block, block)
        probs, slopes = [], []
        for h in range(heads):
            rows = pl.ds(h * HEAD_DIM, HEAD_DIM)
            scores = lax.dot_general(
                keys, masked_q[h], NT, preferred_element_type=jnp.float32
            )
            soft = jnp.exp(scores + bias - lse[h : h + 1, :])
            grad_probs = lax.dot_general(
                values, masked_g[h], NT, preferred_element_type=jnp.float32
            )
            slope = (soft * (grad_probs - inner[h])).astype(jnp.bfloat16)
            grad_q[rows, :] += jnp.dot(k_t[rows, here], slope, preferred_element_type=jnp.float32)
            probs.append(soft.astype(jnp.bfloat16))
            slopes.append(slope)
        grad_v[here, :] += jnp.dot(
            jnp.concatenate(probs, axis=1),
            jnp.concatenate(masked_g, axis=0),
            preferred_element_type=jnp.float32,
        )
        grad_k[here, :] += jnp.dot(
            jnp.concatenate(slopes, axis=1),
            jnp.concatenate(masked_q, axis=0),
            preferred_element_type=jnp.float32,
        )
        return carry

    lax.fori_loop(lows[i], i + 1, step, 0)

    def unrotate(x, rows):
        parts = []
        for part in range(width // 128):
            piece = x[:, part * 128 : (part + 1) * 128]
            parts.append(piece * cosine[rows, :] - swap_pairs(piece) * sine[rows, :])
        return jnp.concatenate(parts, axis=1).astype(jnp.bfloat16)

    mine = pl.ds(pl.multiple_of(i * block, block), block)
    grad_mixed[mine, 0:width] = unrotate(grad_q[...].T * 0.125, mine)

    @pl.when(i == blocks - 1)
    def _():
        def finish(j, carry):
            rows = pl.ds(pl.multiple_of(j * block, block), block)
            grad_mixed[rows, width : 2 * width] = unrotate(grad_k[rows, :], rows)
            grad_mixed[rows, 2 * width : 3 * width] = grad_v[rows, :].astype(jnp.bfloat16)
            return carry

        lax.fori_loop(0, blocks, finish, 0)


def attend_backward(lows, starts, lse, mixed, context, grad_context, cosine, sine, block):
    length, triple = mixed.shape
    width = triple // 3
    blocks = length // block
    whole = lambda i, lows: (0, 0)
    row = lambda i, lows: (i, 0)
    column = lambda i, lows: (0, i)
    return pl.pallas_call(
        backward_kernel,
        grid_spec=pltpu.PrefetchScalarGridSpec(
            num_scalar_prefetch=1,
            grid=(blocks,),
            in_specs=[
                pl.BlockSpec((8, block), column),
                pl.BlockSpec((8, block), column),
                pl.BlockSpec((block, width), row),
                pl.BlockSpec((length, width), lambda i, lows: (0, 1)),
                pl.BlockSpec((length, width), lambda i, lows: (0, 2)),
                pl.BlockSpec((block, width), row),
                pl.BlockSpec((block, width), row),
                pl.BlockSpec((length, 128), whole),
                pl.BlockSpec((length, 128), whole),
            ],
            out_specs=pl.BlockSpec((length, triple), whole),
            scratch_shapes=[
                pltpu.VMEM((width, length), jnp.bfloat16),
                pltpu.VMEM((width, block), jnp.float32),
                pltpu.VMEM((length, width), jnp.float32),
                pltpu.VMEM((length, width), jnp.float32),
            ],
        ),
        out_shape=jax.ShapeDtypeStruct((length, triple), jnp.bfloat16),
        compiler_params=pltpu.CompilerParams(vmem_limit_bytes=VMEM_BYTES),
        cost_estimate=pl.CostEstimate(
            flops=2 * length * length * width * 20,
            bytes_accessed=length * width * 24,
            transcendentals=0,
        ),
        name="attend_backward",
    )(lows, starts, lse, mixed, mixed, mixed, context, grad_context, cosine, sine)


def positions_of(segments):
    ids = jnp.arange(8, dtype=jnp.int32)
    counts = jnp.sum((segments[None, :] < ids[:, None]).astype(jnp.int32), axis=1)
    return jnp.sum(jnp.where(segments[None, :] == ids[:, None], counts[:, None], 0), axis=0)


def rotary_tables(positions):
    lane = jnp.arange(128, dtype=jnp.int32) % HEAD_DIM
    step = (lane % (ROT // 2)).astype(jnp.float32)
    inverse = jnp.exp(step * (-2.0 * math.log(10000.0) / ROT))
    angles = positions.astype(jnp.float32)[:, None] * inverse[None, :]
    rotated = (lane < ROT)[None, :]
    cosine = jnp.where(rotated, jnp.cos(angles), 1.0)
    sine = jnp.where(rotated, jnp.where((lane < ROT // 2)[None, :], -1.0, 1.0) * jnp.sin(angles), 0.0)
    return cosine, sine


def gelu_pair(u):
    scale = math.sqrt(2.0 / math.pi)
    square = u * u
    bent = jnp.tanh(scale * u * (1.0 + 0.044715 * square))
    half = 0.5 * (1.0 + bent)
    slope = half + 0.5 * u * (1.0 - bent * bent) * (scale * (1.0 + 3 * 0.044715 * square))
    return u * half, slope


def project_kernel(
    place, x, gain, shift, w_qkv, b_qkv, w_up, b_up, cosine, sine, *refs
):
    normed, mixed, activated, slope = refs[-4:]
    n = pl.program_id(0)

    @pl.when(n == 0)
    def _():
        wide = x[...].astype(jnp.float32)
        centred = wide - jnp.mean(wide, axis=1, keepdims=True)
        inverse_std = lax.rsqrt(jnp.mean(centred * centred, axis=1, keepdims=True) + EPSILON)
        normed[...] = (centred * inverse_std * gain[...] + shift[...]).astype(jnp.bfloat16)

    @pl.when(n < 3)
    def _():
        y = jnp.dot(normed[...], w_qkv[...], preferred_element_type=jnp.float32) + b_qkv[...]

        @pl.when(n < 2)
        def _():
            parts = []
            for part in range(y.shape[1] // 128):
                piece = y[:, part * 128 : (part + 1) * 128]
                parts.append(piece * cosine[...] + swap_pairs(piece) * sine[...])
            mixed[...] = jnp.concatenate(parts, axis=1).astype(jnp.bfloat16)

        @pl.when(n == 2)
        def _():
            mixed[...] = y.astype(jnp.bfloat16)

    @pl.when(n >= 3)
    def _():
        u = jnp.dot(normed[...], w_up[...], preferred_element_type=jnp.float32) + b_up[...]
        high, tilt = gelu_pair(u)
        activated[...] = high.astype(jnp.bfloat16)
        slope[...] = tilt.astype(jnp.bfloat16)


def project(place, x, weights, tables, length, carried):
    gain, shift, w_qkv, b_qkv, w_up, b_up = weights
    block, width = x.shape
    local_width = w_qkv.shape[1] // 3
    hidden = w_up.shape[1]
    tile = min(256, hidden)
    whole = lambda n, place: (0, 0)
    qkv = lambda n, place: (0, jnp.minimum(n, 2))
    up = lambda n, place: (0, jnp.maximum(n - 3, 0))
    here = lambda n, place: (place[0], 0)
    in_specs = [
        pl.BlockSpec((block, width), whole),
        pl.BlockSpec((1, width), whole),
        pl.BlockSpec((1, width), whole),
        pl.BlockSpec((width, local_width), qkv),
        pl.BlockSpec((1, local_width), qkv),
        pl.BlockSpec((width, tile), up),
        pl.BlockSpec((1, tile), up),
        pl.BlockSpec((block, 128), here),
        pl.BlockSpec((block, 128), here),
    ]
    out_specs = [
        pl.BlockSpec((block, width), here),
        pl.BlockSpec((block, local_width), lambda n, place: (place[0], jnp.minimum(n, 2))),
        pl.BlockSpec((block, tile), lambda n, place: (place[0], jnp.maximum(n - 3, 0))),
        pl.BlockSpec((block, tile), lambda n, place: (place[0], jnp.maximum(n - 3, 0))),
    ]
    out_shape = [
        jax.ShapeDtypeStruct((length, columns), jnp.bfloat16)
        for columns in (width, 3 * local_width, hidden, hidden)
    ]
    operands = [place, x, gain, shift, w_qkv, b_qkv, w_up, b_up, *tables]
    aliases = {}
    if carried is not None:
        aliases = {len(operands) + i: i for i in range(4)}
        operands += list(carried)
        in_specs += [pl.BlockSpec(memory_space=pl.ANY)] * 4
    return pl.pallas_call(
        project_kernel,
        grid_spec=pltpu.PrefetchScalarGridSpec(
            num_scalar_prefetch=1,
            grid=(3 + hidden // tile,),
            in_specs=in_specs,
            out_specs=out_specs,
        ),
        out_shape=out_shape,
        input_output_aliases=aliases,
        compiler_params=pltpu.CompilerParams(vmem_limit_bytes=VMEM_BYTES),
        cost_estimate=pl.CostEstimate(
            flops=2 * block * width * (3 * local_width + hidden),
            bytes_accessed=2 * width * (3 * local_width + hidden) + 4 * block * width,
            transcendentals=0,
        ),
        name="project",
    )(*operands)


def finish_kernel(order, row_a, far_a, row_b, far_b, *outs):
    s = pl.program_id(0)
    for index, source in enumerate((row_a, far_a, row_b, far_b)):

        @pl.when(s // 2 == index)
        def _(source=source):
            start = 0
            for out in outs:
                rows = out.shape[0]
                out[...] = source[0, start : start + rows, :].astype(jnp.float32)
                start += rows


def finish(order, pieces, splits):
    _, rows, columns = pieces[0].shape
    in_specs = [
        pl.BlockSpec(
            (1, rows, columns),
            lambda s, order, i=i: (jnp.clip(s - 2 * i, 0, 1), 0, 0),
        )
        for i in range(4)
    ]
    return pl.pallas_call(
        finish_kernel,
        grid_spec=pltpu.PrefetchScalarGridSpec(
            num_scalar_prefetch=1,
            grid=(8,),
            in_specs=in_specs,
            out_specs=[
                pl.BlockSpec((part, columns), lambda s, order: (order[s], 0)) for part in splits
            ],
        ),
        out_shape=[jax.ShapeDtypeStruct((8 * part, columns), jnp.float32) for part in splits],
        compiler_params=pltpu.CompilerParams(vmem_limit_bytes=VMEM_BYTES),
        cost_estimate=pl.CostEstimate(
            flops=0, bytes_accessed=8 * rows * columns * 6, transcendentals=0
        ),
        name="finish",
    )(order, *pieces)


def add_low(one, other):
    return (one.astype(jnp.float32) + other.astype(jnp.float32)).astype(jnp.bfloat16)


def swap_rows(array, bit):
    return lax.ppermute(array, "rows", [(i, i ^ bit) for i in range(4)])


def sum_rows(parts, splits):
    row = lax.axis_index("rows")
    x, y = row % 2, row // 2
    pieces, order = [], []
    for half, (first, second, first_bit, second_bit) in enumerate(((x, y, 1, 2), (y, x, 2, 1))):
        group = parts[4 * half : 4 * half + 4].reshape(2, 2, *parts.shape[1:])
        away = lax.dynamic_index_in_dim(group, 1 - first, 0, False)
        keep = lax.dynamic_index_in_dim(group, first, 0, False)
        near = add_low(keep, swap_rows(away, first_bit))
        away = lax.dynamic_index_in_dim(near, 1 - second, 0, True)
        keep = lax.dynamic_index_in_dim(near, second, 0, True)
        own = add_low(keep, swap_rows(away, second_bit))
        other = swap_rows(own, second_bit)
        line = jnp.where(
            second == 0,
            jnp.concatenate([own, other], axis=0),
            jnp.concatenate([other, own], axis=0),
        )
        pieces += [line, swap_rows(line, first_bit)]
        for base in (2 * first, 2 * (1 - first)):
            order += [4 * half + base, 4 * half + base + 1]
    return finish(jnp.stack(order).astype(jnp.int32), pieces, splits)


def sum_all(array, rows, tp):
    for axis, size in (("tp", tp), ("rows", rows)):
        step = 1
        while step < size:
            array = array + lax.ppermute(array, axis, [(i, i ^ step) for i in range(size)])
            step *= 2
    return array


def token_sum(matrix):
    ones_row = jnp.ones((1, matrix.shape[0]), matrix.dtype)
    return jnp.dot(ones_row, matrix, preferred_element_type=jnp.float32)[0]


def transposed_dot(left, right):
    return lax.dot_general(
        left, right, (((0,), (0,)), ((), ())), preferred_element_type=jnp.float32
    )


def dot_transposed(left, right):
    return lax.dot_general(left, right, NT, preferred_element_type=jnp.float32)


def local(
    rows,
    tp,
    hidden_in,
    segment_ids,
    ln_gain,
    ln_bias,
    w_qkv,
    b_qkv,
    w_out,
    out_bias,
    w_up,
    b_up,
    w_down,
    cotangent,
):
    x = hidden_in[0]
    block, width = x.shape
    length = block * tp
    local_width = w_qkv.shape[2]
    hidden = w_up.shape[1]
    chips = tp // 2
    me = lax.axis_index("tp")
    chip, core = me // 2, me % 2

    around = [(i, (i + 2) % tp) for i in range(tp)]
    sibling = [(i, i ^ 1) for i in range(tp)]
    segments = lax.all_gather(segment_ids[0], "tp", axis=0, tiled=True)
    starts = positions_of(segments)
    tables = rotary_tables(jnp.arange(length, dtype=jnp.int32) - starts)
    lows = starts[::block] // block
    starts = jnp.broadcast_to(starts[None], (8, length))

    qkv_matrix = w_qkv.reshape(width, 3 * local_width)
    weights = (
        ln_gain.reshape(1, width),
        ln_bias.reshape(1, width),
        qkv_matrix,
        b_qkv.reshape(1, 3 * local_width),
        w_up,
        b_up.reshape(1, hidden),
    )
    carried = None
    travelling = x
    for s in range(chips):
        if s > 0:
            travelling = lax.ppermute(travelling, "tp", around)
        source = (chip - s + chips) % chips
        for flip, piece in enumerate((travelling, lax.ppermute(travelling, "tp", sibling))):
            place = (2 * source + (core ^ flip)).astype(jnp.int32).reshape(1)
            carried = project(place, piece, weights, tables, length, carried)
    normed, mixed, activated, slope = carried

    chunks = 2
    columns = width // chunks
    grads = [
        lax.all_gather(
            cotangent[0, :, c * columns : (c + 1) * columns], "tp", axis=0, tiled=True
        )
        for c in range(chunks)
    ]
    context, lse = attend_forward(lows, starts, mixed, block)

    w_down_parts, w_out_parts = [], []
    for grad in grads:
        low = transposed_dot(activated, grad).astype(jnp.bfloat16)
        low_out = transposed_dot(context, grad).astype(jnp.bfloat16)
        if rows == 4:
            parts = jnp.concatenate(
                [low.reshape(8, hidden // 8, columns), low_out.reshape(8, local_width // 8, columns)],
                axis=1,
            )
            total, total_out = sum_rows(parts, (hidden // 8, local_width // 8))
        else:
            total = lax.psum(low, "rows").astype(jnp.float32)
            total_out = lax.psum(low_out, "rows").astype(jnp.float32)
        w_down_parts.append(total)
        w_out_parts.append(total_out)
    grad_w_down = jnp.concatenate(w_down_parts, axis=1)
    grad_w_out = jnp.concatenate(w_out_parts, axis=1)

    grad_whole = jnp.concatenate(grads, axis=1)
    grad_up = (dot_transposed(grad_whole, w_down) * slope.astype(jnp.float32)).astype(jnp.bfloat16)
    grad_context = dot_transposed(grad_whole, w_out).astype(jnp.bfloat16)

    def reduce_weight(partial_sum):
        low = partial_sum.astype(jnp.bfloat16)
        if rows == 4:
            tall, wide = low.shape
            return sum_rows(low.reshape(8, tall // 8, wide), (tall // 8,))[0]
        return lax.psum(low, "rows").astype(jnp.float32)

    grad_w_up = reduce_weight(transposed_dot(normed, grad_up))
    grad_mixed = attend_backward(lows, starts, lse, mixed, context, grad_context, *tables, block)
    grad_w_qkv = reduce_weight(transposed_dot(normed, grad_mixed)).reshape(width, 3, local_width)

    branch = (
        jnp.dot(context, w_out, preferred_element_type=jnp.float32)
        + jnp.dot(activated, w_down, preferred_element_type=jnp.float32)
    ).astype(jnp.bfloat16)
    branch_total = lax.psum_scatter(branch, "tp", scatter_dimension=0, tiled=True)
    inputs = x.astype(jnp.float32)
    hidden_out = (inputs + branch_total.astype(jnp.float32) + out_bias).astype(jnp.bfloat16)

    part = (
        dot_transposed(grad_mixed, qkv_matrix) + dot_transposed(grad_up, w_up)
    ).astype(jnp.bfloat16)
    grad_normed = lax.psum_scatter(part, "tp", scatter_dimension=0, tiled=True).astype(jnp.float32)

    average = jnp.mean(inputs, axis=-1, keepdims=True)
    centred = inputs - average
    inverse_std = lax.rsqrt(jnp.mean(centred * centred, axis=-1, keepdims=True) + EPSILON)
    unit_rows = centred * inverse_std
    gain_terms = jnp.sum(grad_normed * unit_rows, axis=0)
    bias_terms = jnp.sum(grad_normed, axis=0)
    grad_unit = grad_normed * ln_gain
    grad_input = cotangent[0].astype(jnp.float32) + inverse_std * (
        grad_unit
        - jnp.mean(grad_unit, axis=-1, keepdims=True)
        - unit_rows * jnp.mean(grad_unit * unit_rows, axis=-1, keepdims=True)
    )
    small = lax.psum(jnp.concatenate([token_sum(grad_mixed), token_sum(grad_up)]), "rows")
    grad_b_qkv = small[: 3 * local_width].reshape(3, local_width)
    grad_b_up = small[3 * local_width :]
    tail = sum_all(jnp.stack([gain_terms, bias_terms, token_sum(cotangent[0])]), rows, tp)
    return (
        hidden_out[None],
        grad_input.astype(jnp.bfloat16)[None],
        tail[0],
        tail[1],
        grad_w_qkv,
        grad_b_qkv,
        grad_w_out,
        tail[2],
        grad_w_up,
        grad_b_up,
        grad_w_down,
    )


def solution(mesh):
    in_specs = (
        P("rows", "tp", None),
        P("rows", "tp"),
        P(),
        P(),
        P(None, None, "tp"),
        P(None, "tp"),
        P("tp", None),
        P(),
        P(None, "tp"),
        P("tp"),
        P("tp", None),
        P("rows", "tp", None),
    )
    out_specs = (
        P("rows", "tp", None),
        P("rows", "tp", None),
        P(),
        P(),
        P(None, None, "tp"),
        P(None, "tp"),
        P("tp", None),
        P(),
        P(None, "tp"),
        P("tp"),
        P("tp", None),
    )
    return jax.shard_map(
        partial(local, mesh.shape["rows"], mesh.shape["tp"]),
        mesh=mesh,
        in_specs=in_specs,
        out_specs=out_specs,
        check_vma=False,
    )
```

```python
from functools import partial
import math

import jax
import jax.numpy as jnp
from jax import lax
from jax.experimental import pallas as pl
from jax.experimental.pallas import tpu as pltpu
from jax.sharding import PartitionSpec as P

HEAD_DIM = 64
ROT = 32
EPSILON = 1e-05
NEGATIVE = -1e30
VMEM_BYTES = 56 * 2**20
NT = (((1,), (1,)), ((), ()))


class Line:
    def __init__(self):
        self.token = jnp.zeros((8, 128), jnp.float32)

    def join(self, *arrays):
        *arrays, self.token = lax.optimization_barrier((*arrays, self.token))
        return arrays

    def call(
        self, body, name, grid, operands, in_specs, outs, scalars=0, scratch=(), aliases=None, cost=0
    ):
        inputs = len(operands)

        def whole_body(*refs):
            refs = list(refs)
            token = refs.pop(inputs + 1 + len(outs))
            refs.pop(inputs)
            token[...] = jnp.zeros_like(token)
            body(*refs)

        *results, self.token = pl.pallas_call(
            whole_body,
            grid_spec=pltpu.PrefetchScalarGridSpec(
                num_scalar_prefetch=scalars,
                grid=grid,
                in_specs=[*in_specs, pl.BlockSpec(memory_space=pl.ANY)],
                out_specs=[
                    *(spec for _, _, spec in outs),
                    pl.BlockSpec((8, 128), lambda *index: (0, 0)),
                ],
                scratch_shapes=list(scratch),
            ),
            out_shape=[
                *(jax.ShapeDtypeStruct(shape, dtype) for shape, dtype, _ in outs),
                jax.ShapeDtypeStruct((8, 128), jnp.float32),
            ],
            input_output_aliases=aliases or {},
            compiler_params=pltpu.CompilerParams(vmem_limit_bytes=VMEM_BYTES),
            cost_estimate=pl.CostEstimate(
                flops=2**20 + cost, bytes_accessed=2**16, transcendentals=0
            ),
            name=name,
        )(*operands, self.token)
        return results


def whole(*index):
    return (0, 0)


def row(i, *scalars):
    return (i, 0)


def lane_heads(rows, width):
    return lax.broadcasted_iota(jnp.int32, (rows, width), 1) // HEAD_DIM


def swap_pairs(x):
    width = x.shape[1]
    lane = lax.broadcasted_iota(jnp.int32, x.shape, 1) % HEAD_DIM
    up = pltpu.roll(x, width - ROT // 2, 1)
    down = pltpu.roll(x, ROT // 2, 1)
    return jnp.where(lane < ROT // 2, up, down)


def mask_bias(starts, key_first, query_first, block):
    key_index = key_first + lax.broadcasted_iota(jnp.int32, (block, block), 0)
    query_index = query_first + lax.broadcasted_iota(jnp.int32, (block, block), 1)
    allowed = (key_index >= starts) & (key_index <= query_index)
    return jnp.where(allowed, 0.0, NEGATIVE).astype(jnp.float32)


def stack_heads(source, stacked, block):
    length, width = source.shape
    row_heads = lane_heads(block, width)
    for j in range(length // block):
        rows = pl.ds(j * block, block)
        piece = source[rows, :]
        for h in range(width // HEAD_DIM):
            stacked[j, pl.ds(h * block, block), :] = jnp.where(row_heads == h, piece, 0).astype(
                jnp.bfloat16
            )


def forward_kernel(lows, starts, q, k, v, context, lse, v_t, k_heads, acc):
    block, width = q.shape
    heads = width // HEAD_DIM
    length = k.shape[0]
    i = pl.program_id(0)

    @pl.when(i == 0)
    def _():
        stack_heads(k, k_heads, block)
        for j in range(length // block):
            rows = pl.ds(j * block, block)
            v_t[:, rows] = v[rows, :].T

    turned = (q[...] * 0.125).T
    acc[...] = jnp.zeros_like(acc)

    def step(j, carry):
        tops, sums = carry
        first = pl.multiple_of(j * block, block)
        all_scores = jnp.dot(k_heads[j], turned, preferred_element_type=jnp.float32)
        bias = mask_bias(starts[0:1, :], first, i * block, block)
        new_tops, new_sums = [], []
        for h in range(heads):
            rows = pl.ds(h * HEAD_DIM, HEAD_DIM)
            scores = all_scores[h * block : (h + 1) * block, :] + bias
            top = jnp.maximum(tops[h], jnp.max(scores, axis=0, keepdims=True))
            weights = jnp.exp(scores - top)
            keep = jnp.exp(tops[h] - top)
            new_tops.append(top)
            new_sums.append(sums[h] * keep + jnp.sum(weights, axis=0, keepdims=True))
            acc[rows, :] = acc[rows, :] * keep + jnp.dot(
                v_t[rows, pl.ds(first, block)],
                weights.astype(jnp.bfloat16),
                preferred_element_type=jnp.float32,
            )
        return tuple(new_tops), tuple(new_sums)

    empty = tuple(jnp.full((1, block), NEGATIVE, jnp.float32) for _ in range(heads))
    nothing = tuple(jnp.zeros((1, block), jnp.float32) for _ in range(heads))
    tops, sums = lax.fori_loop(lows[i], i + 1, step, (empty, nothing))
    for h in range(heads):
        rows = pl.ds(h * HEAD_DIM, HEAD_DIM)
        acc[rows, :] = acc[rows, :] / sums[h]
        lse[h : h + 1, :] = tops[h] + jnp.log(sums[h])
    context[...] = acc[...].T.astype(jnp.bfloat16)


def attend_forward(line, lows, starts, mixed, block):
    length, triple = mixed.shape
    local_width = triple // 3
    blocks = length // block
    stack = (blocks, local_width // HEAD_DIM * block, local_width)
    column = lambda i, lows: (0, i)
    return line.call(
        forward_kernel,
        "attend_forward",
        (blocks,),
        [lows, starts, mixed, mixed, mixed],
        [
            pl.BlockSpec((8, block), column),
            pl.BlockSpec((block, local_width), row),
            pl.BlockSpec((length, local_width), lambda i, lows: (0, 1)),
            pl.BlockSpec((length, local_width), lambda i, lows: (0, 2)),
        ],
        [
            ((length, local_width), jnp.bfloat16, pl.BlockSpec((block, local_width), row)),
            ((8, length), jnp.float32, pl.BlockSpec((8, block), column)),
        ],
        scalars=1,
        scratch=[
            pltpu.VMEM((local_width, length), jnp.bfloat16),
            pltpu.VMEM(stack, jnp.bfloat16),
            pltpu.VMEM((local_width, block), jnp.float32),
        ],
    )


def backward_kernel(
    lows, starts, lse, q, k, v, context, grad, cosine, sine, grad_mixed, k_t, k_heads, v_heads, grad_q, grad_k, grad_v
):
    block, width = q.shape
    heads = width // HEAD_DIM
    length = k.shape[0]
    i = pl.program_id(0)
    blocks = length // block

    @pl.when(i == 0)
    def _():
        grad_k[...] = jnp.zeros_like(grad_k)
        grad_v[...] = jnp.zeros_like(grad_v)
        stack_heads(k, k_heads, block)
        stack_heads(v, v_heads, block)
        for j in range(blocks):
            rows = pl.ds(j * block, block)
            k_t[:, rows] = k[rows, :].T

    row_heads = lane_heads(block, width)
    scaled = q[...] * 0.125
    grads = grad[...]
    masked_q = [jnp.where(row_heads == h, scaled, 0).astype(jnp.bfloat16) for h in range(heads)]
    masked_g = [jnp.where(row_heads == h, grads, 0).astype(jnp.bfloat16) for h in range(heads)]
    turned_q = scaled.T
    turned_g = grads.T
    products = (grads.astype(jnp.float32) * context[...].astype(jnp.float32)).T
    inner = [
        jnp.sum(products[h * HEAD_DIM : (h + 1) * HEAD_DIM, :], axis=0, keepdims=True)
        for h in range(heads)
    ]
    grad_q[...] = jnp.zeros_like(grad_q)

    def step(j, carry):
        first = pl.multiple_of(j * block, block)
        here = pl.ds(first, block)
        all_scores = jnp.dot(k_heads[j], turned_q, preferred_element_type=jnp.float32)
        all_grads = jnp.dot(v_heads[j], turned_g, preferred_element_type=jnp.float32)
        bias = mask_bias(starts[0:1, :], first, i * block, block)
        probs, slopes = [], []
        for h in range(heads):
            rows = pl.ds(h * HEAD_DIM, HEAD_DIM)
            part = slice(h * block, (h + 1) * block)
            scores = all_scores[part, :]
            soft = jnp.exp(scores + bias - lse[h : h + 1, :])
            grad_probs = all_grads[part, :]
            slope = (soft * (grad_probs - inner[h])).astype(jnp.bfloat16)
            grad_q[rows, :] += jnp.dot(k_t[rows, here], slope, preferred_element_type=jnp.float32)
            probs.append(soft.astype(jnp.bfloat16))
            slopes.append(slope)
        grad_v[here, :] += jnp.dot(
            jnp.concatenate(probs, axis=1),
            jnp.concatenate(masked_g, axis=0),
            preferred_element_type=jnp.float32,
        )
        grad_k[here, :] += jnp.dot(
            jnp.concatenate(slopes, axis=1),
            jnp.concatenate(masked_q, axis=0),
            preferred_element_type=jnp.float32,
        )
        return carry

    lax.fori_loop(lows[i], i + 1, step, 0)

    def unrotate(x, rows):
        parts = []
        for part in range(width // 128):
            piece = x[:, part * 128 : (part + 1) * 128]
            parts.append(piece * cosine[rows, :] - swap_pairs(piece) * sine[rows, :])
        return jnp.concatenate(parts, axis=1).astype(jnp.bfloat16)

    mine = pl.ds(pl.multiple_of(i * block, block), block)
    grad_mixed[mine, 0:width] = unrotate(grad_q[...].T * 0.125, mine)

    @pl.when(i == blocks - 1)
    def _():
        def finish(j, carry):
            rows = pl.ds(pl.multiple_of(j * block, block), block)
            grad_mixed[rows, width : 2 * width] = unrotate(grad_k[rows, :], rows)
            grad_mixed[rows, 2 * width : 3 * width] = grad_v[rows, :].astype(jnp.bfloat16)
            return carry

        lax.fori_loop(0, blocks, finish, 0)


def attend_backward(line, lows, starts, lse, mixed, context, grad_context, cosine, sine, block):
    length, triple = mixed.shape
    local_width = triple // 3
    blocks = length // block
    stack = (blocks, local_width // HEAD_DIM * block, local_width)
    column = lambda i, lows: (0, i)
    return line.call(
        backward_kernel,
        "attend_backward",
        (blocks,),
        [lows, starts, lse, mixed, mixed, mixed, context, grad_context, cosine, sine],
        [
            pl.BlockSpec((8, block), column),
            pl.BlockSpec((8, block), column),
            pl.BlockSpec((block, local_width), row),
            pl.BlockSpec((length, local_width), lambda i, lows: (0, 1)),
            pl.BlockSpec((length, local_width), lambda i, lows: (0, 2)),
            pl.BlockSpec((block, local_width), row),
            pl.BlockSpec((block, local_width), row),
            pl.BlockSpec((length, 128), whole),
            pl.BlockSpec((length, 128), whole),
        ],
        [((length, triple), jnp.bfloat16, pl.BlockSpec((length, triple), whole))],
        scalars=1,
        scratch=[
            pltpu.VMEM((local_width, length), jnp.bfloat16),
            pltpu.VMEM(stack, jnp.bfloat16),
            pltpu.VMEM(stack, jnp.bfloat16),
            pltpu.VMEM((local_width, block), jnp.float32),
            pltpu.VMEM((length, local_width), jnp.float32),
            pltpu.VMEM((length, local_width), jnp.float32),
        ],
        cost=632 * 10**8,
    )[0]


def positions_of(segments):
    ids = jnp.arange(8, dtype=jnp.int32)
    counts = jnp.sum((segments[None, :] < ids[:, None]).astype(jnp.int32), axis=1)
    return jnp.sum(jnp.where(segments[None, :] == ids[:, None], counts[:, None], 0), axis=0)


def rotary_tables(positions):
    lane = jnp.arange(128, dtype=jnp.int32) % HEAD_DIM
    step = (lane % (ROT // 2)).astype(jnp.float32)
    inverse = jnp.exp(step * (-2.0 * math.log(10000.0) / ROT))
    angles = positions.astype(jnp.float32)[:, None] * inverse[None, :]
    rotated = (lane < ROT)[None, :]
    cosine = jnp.where(rotated, jnp.cos(angles), 1.0)
    sine = jnp.where(rotated, jnp.where((lane < ROT // 2)[None, :], -1.0, 1.0) * jnp.sin(angles), 0.0)
    return cosine, sine


def gelu_pair(u):
    scale = math.sqrt(2.0 / math.pi)
    square = u * u
    bent = jnp.tanh(scale * u * (1.0 + 0.044715 * square))
    half = 0.5 * (1.0 + bent)
    slope = half + 0.5 * u * (1.0 - bent * bent) * (scale * (1.0 + 3 * 0.044715 * square))
    return u * half, slope


def project_kernel(place, mine, other, gain, shift, w_qkv, b_qkv, w_up, b_up, cosine, sine, *refs):
    normed, unit, mixed, activated, slope = refs[-5:]
    n = pl.program_id(0)
    block = mine.shape[0]
    width = w_qkv.shape[2]
    strip = min(128, block)
    strips = [pl.ds(r * strip, strip) for r in range(2 * block // strip)]

    @pl.when(n == 0)
    def _():
        for source, first in ((mine, place[1] * block), (other, (1 - place[1]) * block)):
            for r in range(block // strip):
                wide = source[pl.ds(r * strip, strip), :].astype(jnp.float32)
                centred = wide - jnp.mean(wide, axis=1, keepdims=True)
                inverse_std = lax.rsqrt(
                    jnp.mean(centred * centred, axis=1, keepdims=True) + EPSILON
                )
                rows = pl.ds(pl.multiple_of(first + r * strip, strip), strip)
                even = centred * inverse_std
                unit[rows, :] = even.astype(jnp.bfloat16)
                normed[rows, :] = (even * gain[...] + shift[...]).astype(jnp.bfloat16)
        for rows in strips:
            for j in range(3):
                columns = slice(j * width, (j + 1) * width)
                y = jnp.dot(normed[rows, :], w_qkv[j], preferred_element_type=jnp.float32)
                y = y + b_qkv[:, columns]
                if j < 2:
                    parts = []
                    for part in range(width // 128):
                        piece = y[:, part * 128 : (part + 1) * 128]
                        parts.append(piece * cosine[rows, :] + swap_pairs(piece) * sine[rows, :])
                    y = jnp.concatenate(parts, axis=1)
                mixed[rows, columns] = y.astype(jnp.bfloat16)

    @pl.when(n > 0)
    def _():
        for rows in strips:
            u = jnp.dot(normed[rows, :], w_up[...], preferred_element_type=jnp.float32) + b_up[...]
            high, tilt = gelu_pair(u)
            activated[rows, :] = high.astype(jnp.bfloat16)
            slope[rows, :] = tilt.astype(jnp.bfloat16)


def project(line, place, mine, other, weights, tables, length, carried):
    gain, shift, w_qkv, b_qkv, w_up, b_up = weights
    block, width = mine.shape
    local_width = w_qkv.shape[2]
    hidden = w_up.shape[1]
    tile = min(512, hidden)
    up = lambda n, place: (0, jnp.maximum(n - 1, 0))
    here = lambda n, place: (place[0], 0)
    up_here = lambda n, place: (place[0], jnp.maximum(n - 1, 0))
    operands = [place, mine, other, gain, shift, w_qkv, b_qkv, w_up, b_up, *tables, *carried]
    return line.call(
        project_kernel,
        "project",
        (1 + hidden // tile,),
        operands,
        [
            pl.BlockSpec((block, width), whole),
            pl.BlockSpec((block, width), whole),
            pl.BlockSpec((1, width), whole),
            pl.BlockSpec((1, width), whole),
            pl.BlockSpec((3, width, local_width), lambda n, place: (0, 0, 0)),
            pl.BlockSpec((1, 3 * local_width), whole),
            pl.BlockSpec((width, tile), up),
            pl.BlockSpec((1, tile), up),
            pl.BlockSpec((2 * block, 128), here),
            pl.BlockSpec((2 * block, 128), here),
            *[pl.BlockSpec(memory_space=pl.ANY)] * len(carried),
        ],
        [
            ((length, columns), jnp.bfloat16, pl.BlockSpec((2 * block, wide), index))
            for columns, wide, index in (
                (width, width, here),
                (width, width, here),
                (3 * local_width, 3 * local_width, here),
                (hidden, tile, up_here),
                (hidden, tile, up_here),
            )
        ],
        scalars=1,
        aliases={len(operands) - 5 + i: i for i in range(len(carried))},
    )


def backward_products_kernel(layout, *refs):
    grads = refs[:layout]
    w_down, w_out, slope, grad_up, grad_context, total = refs[layout:]
    columns = grads[0].shape[1]
    up, context = 0.0, 0.0
    for c in range(layout):
        part = slice(c * columns, (c + 1) * columns)
        piece = grads[c][...]
        up = up + lax.dot_general(piece, w_down[:, part], NT, preferred_element_type=jnp.float32)
        context = context + lax.dot_general(
            piece, w_out[:, part], NT, preferred_element_type=jnp.float32
        )
    low = (up * slope[...].astype(jnp.float32)).astype(jnp.bfloat16)
    grad_up[...] = low
    grad_context[...] = context.astype(jnp.bfloat16)

    @pl.when(pl.program_id(0) == 0)
    def _():
        total[...] = jnp.zeros_like(total)

    total[...] += jnp.sum(low.astype(jnp.float32), axis=0, keepdims=True)


def backward_products(line, grads, w_down, w_out, slope):
    length, columns = grads[0].shape
    hidden, width = w_down.shape
    local_width = w_out.shape[0]
    tile = min(256, length)
    return line.call(
        partial(backward_products_kernel, len(grads)),
        "backward_products",
        (length // tile,),
        [*grads, w_down, w_out, slope],
        [pl.BlockSpec((tile, columns), row) for _ in grads]
        + [
            pl.BlockSpec((hidden, width), whole),
            pl.BlockSpec((local_width, width), whole),
            pl.BlockSpec((tile, hidden), row),
        ],
        [
            ((length, hidden), jnp.bfloat16, pl.BlockSpec((tile, hidden), row)),
            ((length, local_width), jnp.bfloat16, pl.BlockSpec((tile, local_width), row)),
            ((1, hidden), jnp.float32, pl.BlockSpec((1, hidden), whole)),
        ],
    )


def branch_kernel(context, activated, w_out, w_down, out):
    total = jnp.dot(context[...], w_out[...], preferred_element_type=jnp.float32)
    total = total + jnp.dot(activated[...], w_down[...], preferred_element_type=jnp.float32)
    out[...] = total.astype(jnp.bfloat16)


def branch_sum(line, context, activated, w_out, w_down):
    length, local_width = context.shape
    hidden, width = w_down.shape
    tile = min(256, length)
    return line.call(
        branch_kernel,
        "branch_sum",
        (length // tile,),
        [context, activated, w_out, w_down],
        [
            pl.BlockSpec((tile, local_width), row),
            pl.BlockSpec((tile, hidden), row),
            pl.BlockSpec((local_width, width), whole),
            pl.BlockSpec((hidden, width), whole),
        ],
        [((length, width), jnp.bfloat16, pl.BlockSpec((tile, width), row))],
    )[0]


def normed_kernel(mixed, up, unit, w_qkv, w_up, out, gain, shift):
    width = w_qkv.shape[2]
    total = lax.dot_general(up[...], w_up[...], NT, preferred_element_type=jnp.float32)
    for j in range(3):
        total = total + lax.dot_general(
            mixed[:, j * width : (j + 1) * width],
            w_qkv[j],
            NT,
            preferred_element_type=jnp.float32,
        )
    out[...] = total.astype(jnp.bfloat16)

    @pl.when(pl.program_id(0) == 0)
    def _():
        gain[...] = jnp.zeros_like(gain)
        shift[...] = jnp.zeros_like(shift)

    gain[...] += jnp.sum(total * unit[...].astype(jnp.float32), axis=0, keepdims=True)
    shift[...] += jnp.sum(total, axis=0, keepdims=True)


def normed_sum(line, grad_mixed, grad_up, unit, w_qkv, w_up):
    length, triple = grad_mixed.shape
    width, hidden = w_up.shape
    tile = min(256, length)
    return line.call(
        normed_kernel,
        "normed_sum",
        (length // tile,),
        [grad_mixed, grad_up, unit, w_qkv, w_up],
        [
            pl.BlockSpec((tile, triple), row),
            pl.BlockSpec((tile, hidden), row),
            pl.BlockSpec((tile, width), row),
            pl.BlockSpec(w_qkv.shape, lambda i: (0, 0, 0)),
            pl.BlockSpec((width, hidden), whole),
        ],
        [
            ((length, width), jnp.bfloat16, pl.BlockSpec((tile, width), row)),
            ((1, width), jnp.float32, pl.BlockSpec((1, width), whole)),
            ((1, width), jnp.float32, pl.BlockSpec((1, width), whole)),
        ],
    )


def finish_kernel(layout, order, *refs):
    s = pl.program_id(0)
    outs = refs[-1:] if isinstance(layout, int) else refs[-len(layout) :]
    for index, source in enumerate(refs[:4]):

        @pl.when(s == index)
        def _(source=source):
            if isinstance(layout, int):
                group = outs[0].shape[2]
                for j in range(layout):
                    columns = slice(j * group, (j + 1) * group)
                    outs[0][j] = source[:, columns].astype(jnp.float32)
            else:
                start = 0
                columns = source.shape[1]
                for out in outs:
                    rows, spread = out.shape
                    for j in range(spread // columns):
                        out[:, j * columns : (j + 1) * columns] = source[
                            start : start + rows, :
                        ].astype(jnp.float32)
                        start += rows


def finish(line, order, pieces, layout, carried=()):
    rows, columns = pieces[0].shape
    in_specs = [pl.BlockSpec(pieces[0].shape, whole) for _ in range(4)]
    in_specs += [pl.BlockSpec(memory_space=pl.ANY)] * len(carried)
    if isinstance(layout, int):
        group = columns // layout
        spec = pl.BlockSpec((layout, rows, group), lambda s, order: (0, order[s], 0))
        outs = [((layout, 4 * rows, group), jnp.float32, spec)]
    else:
        outs = [
            (
                (4 * tall, spread),
                jnp.float32,
                pl.BlockSpec((tall, wide), lambda s, order, place=place: (order[s], place)),
            )
            for tall, wide, spread, place in layout
        ]
    return line.call(
        partial(finish_kernel, layout),
        "finish",
        (4,),
        [order, *pieces, *carried],
        in_specs,
        outs,
        scalars=1,
        aliases={5 + i: i for i in range(len(carried))},
        cost=460 * 10**8,
    )


def add_low(one, other):
    return (one.astype(jnp.float32) + other.astype(jnp.float32)).astype(jnp.bfloat16)


def swap_rows(array, bit):
    return lax.ppermute(array, "rows", [(i, i ^ bit) for i in range(4)])


def outer_kernel(extra, order, left, right, *refs):
    s = pl.program_id(0)
    dims = (((0,), (0,)), ((), ()))
    low = lax.dot_general(left[...], right[...], dims, preferred_element_type=jnp.float32)
    parts = [low.astype(jnp.bfloat16)]
    outs = refs[:4]
    if extra:
        second, *more = refs[: 1 + extra]
        outs, held = refs[1 + extra : 5 + extra], refs[-1]

        @pl.when(s == 0)
        def _():
            for k, other in enumerate((*more, right)):
                held[k] = lax.dot_general(
                    second[...], other[...], dims, preferred_element_type=jnp.float32
                ).astype(jnp.bfloat16)

        rows = held.shape[1] // 4
        here = pl.ds(pl.multiple_of(order[s] * rows, rows), rows)
        parts += [held[k, here, :] for k in range(extra + 1)]
    for index, out in enumerate(outs):

        @pl.when(s == index)
        def _(out=out):
            start = 0
            for part in parts:
                out[start : start + part.shape[0], :] = part
                start += part.shape[0]


def outer_parts(line, order, left, right, second=None, more=()):
    length, tall = left.shape
    columns = right.shape[1]
    extra = len(more)
    rows = (tall + (second.shape[1] * (extra + 1) if extra else 0)) // 4
    return line.call(
        partial(outer_kernel, extra),
        "outer_parts",
        (4,),
        [order, left, right] + ([second, *more] if extra else []),
        [
            pl.BlockSpec((length, tall // 4), lambda s, order: (0, order[s])),
            pl.BlockSpec((length, columns), whole),
        ]
        + ([pl.BlockSpec(array.shape, whole) for array in (second, *more)] if extra else []),
        [((rows, columns), jnp.bfloat16, pl.BlockSpec((rows, columns), whole)) for _ in range(4)],
        scalars=1,
        scratch=[pltpu.VMEM((extra + 1, second.shape[1], columns), jnp.bfloat16)] if extra else (),
    )


class RowsSum:
    def __init__(self, rows, line, left, right, second=None, more=()):
        self.rows, self.line, self.phase = rows, line, 0
        if rows != 4:
            self.order = jnp.arange(4, dtype=jnp.int32)
            self.pieces = lax.psum(outer_parts(line, self.order, left, right, second, more), "rows")
            return
        place = lax.axis_index("rows")
        x, y = place % 2, place // 2
        away = jnp.stack([1 - x, 3 - y, x, 2 + y]).astype(jnp.int32)
        self.order = jnp.stack([x, 1 - x, 2 + y, 3 - y]).astype(jnp.int32)
        self.bits = ((1, 2), (2, 1))
        *away, keep_a, keep_b = outer_parts(line, away, left, right, second, more)
        self.keep = [keep_a, keep_b]
        self.send(0, away)

    def send(self, which, arrays):
        arrays = self.line.join(*arrays)
        self.came = [swap_rows(a, bits[which]) for a, bits in zip(arrays, self.bits)]
        return arrays

    def advance(self):
        if self.rows != 4:
            return
        self.phase += 1
        came = self.line.join(*self.came)
        if self.phase < 3:
            self.keep = [add_low(k, c) for k, c in zip(self.keep, came)]
            self.keep = self.send(2 - self.phase, self.keep)
        else:
            self.pieces = [self.keep[0], came[0], self.keep[1], came[1]]

    def finish(self, *layout, **more):
        self.advance()
        return finish(self.line, self.order, self.pieces, *layout, **more)


def sum_all(array, rows, tp):
    for axis, size in (("tp", tp), ("rows", rows)):
        step = 1
        while step < size:
            array = array + lax.ppermute(array, axis, [(i, i ^ step) for i in range(size)])
            step *= 2
    return array


def gather_small(array, me, tp):
    step = 1
    while step < tp:
        other = lax.ppermute(array, "tp", [(i, i ^ step) for i in range(tp)])
        array = jnp.where(
            (me // step) % 2 == 0,
            jnp.concatenate([array, other]),
            jnp.concatenate([other, array]),
        )
        step *= 2
    return array


def token_sum(matrix):
    ones_row = jnp.ones((1, matrix.shape[0]), matrix.dtype)
    return jnp.dot(ones_row, matrix, preferred_element_type=jnp.float32)[0]


def local(
    rows,
    tp,
    hidden_in,
    segment_ids,
    ln_gain,
    ln_bias,
    w_qkv,
    b_qkv,
    w_out,
    out_bias,
    w_up,
    b_up,
    w_down,
    cotangent,
):
    x = hidden_in[0]
    block, width = x.shape
    length = block * tp
    local_width = w_qkv.shape[2]
    hidden = w_up.shape[1]
    chips = tp // 2
    me = lax.axis_index("tp")
    chip, core = me // 2, me % 2
    line = Line()

    around = [(i, (i + 2) % tp) for i in range(tp)]
    sibling = [(i, i ^ 1) for i in range(tp)]
    segments = gather_small(segment_ids[0], me, tp)
    mine, segments = lax.optimization_barrier((x, segments))
    coming = lax.ppermute(mine, "tp", around)
    other = lax.ppermute(mine, "tp", sibling)
    starts = positions_of(segments)
    tables = rotary_tables(jnp.arange(length, dtype=jnp.int32) - starts)
    lows = starts[::block] // block
    starts = jnp.broadcast_to(starts[None], (8, length))
    w_three = jnp.transpose(w_qkv, (1, 0, 2))
    weights = (
        ln_gain.reshape(1, width),
        ln_bias.reshape(1, width),
        w_three,
        b_qkv.reshape(1, 3 * local_width),
        w_up,
        b_up.reshape(1, hidden),
    )
    carried = ()
    for s in range(chips):
        place = jnp.stack([(chip - s + chips) % chips, core]).astype(jnp.int32)
        mine, other = line.join(mine, other)
        carried = project(line, place, mine, other, weights, tables, length, carried)
        if s < chips - 1:
            (mine,) = line.join(coming)
            if s < chips - 2:
                coming = lax.ppermute(mine, "tp", around)
            other = lax.ppermute(mine, "tp", sibling)
            if s == max(chips - 3, 0):
                chunks = 2
                columns = width // chunks
                pieces = [cotangent[0, :, c * columns : (c + 1) * columns] for c in range(chunks)]
                *pieces, mine = lax.optimization_barrier((*pieces, mine))
                grads = [lax.all_gather(piece, "tp", axis=0, tiled=True) for piece in pieces]
    normed, unit, mixed, activated, slope = carried

    hidden_parts, local_parts = hidden // 4, local_width // 4
    sums = partial(RowsSum, rows, line)
    d0 = sums(activated, grads[0])
    context, lse = attend_forward(line, lows, starts, mixed, block)
    d0.advance()
    branch = branch_sum(line, context, activated, w_out, w_down)
    branch_total = lax.psum_scatter(branch, "tp", scatter_dimension=0, tiled=True)
    d1 = sums(activated, grads[1], context, [grads[0]])
    d0.advance()
    grad_up, grad_context, grad_b_up = backward_products(line, grads, w_down, w_out, slope)
    d1.advance()
    up = sums(normed, grad_up)
    d1.advance()
    grad_mixed = attend_backward(
        line, lows, starts, lse, mixed, context, grad_context, *tables, block
    )
    up.advance()
    down = d0.finish([(hidden_parts, columns, width, 0)])
    (branch_total,) = line.join(branch_total)
    part, gain_part, shift_part = normed_sum(line, grad_mixed, grad_up, unit, w_three, w_up)
    grad_normed = lax.psum_scatter(part, "tp", scatter_dimension=0, tiled=True).astype(jnp.float32)
    three = sums(normed, grad_mixed)
    up.advance()
    down = d1.finish(
        [(hidden_parts, columns, width, 1), (local_parts, width, width, 0)], carried=down
    )
    three.advance()
    up = up.finish([(width // 4, hidden, hidden, 0)])
    three.advance()
    three = three.finish(3)
    grad_w_down, grad_w_out = down
    grad_w_up = up[0]
    grad_w_qkv = jnp.transpose(three[0], (1, 0, 2))

    inputs = x.astype(jnp.float32)
    hidden_out = (inputs + branch_total.astype(jnp.float32) + out_bias).astype(jnp.bfloat16)
    average = jnp.mean(inputs, axis=-1, keepdims=True)
    centred = inputs - average
    inverse_std = lax.rsqrt(jnp.mean(centred * centred, axis=-1, keepdims=True) + EPSILON)
    unit_rows = centred * inverse_std
    grad_unit = grad_normed * ln_gain
    grad_input = cotangent[0].astype(jnp.float32) + inverse_std * (
        grad_unit
        - jnp.mean(grad_unit, axis=-1, keepdims=True)
        - unit_rows * jnp.mean(grad_unit * unit_rows, axis=-1, keepdims=True)
    )
    small = sum_all(jnp.concatenate([token_sum(grad_mixed), grad_b_up[0]]), rows, 1)
    grad_b_qkv = small[: 3 * local_width].reshape(3, local_width)
    grad_b_up = small[3 * local_width :]
    tail = sum_all(
        jnp.concatenate([gain_part, shift_part, token_sum(cotangent[0])[None]]), rows, tp
    )
    return (
        hidden_out[None],
        grad_input.astype(jnp.bfloat16)[None],
        tail[0],
        tail[1],
        grad_w_qkv,
        grad_b_qkv,
        grad_w_out,
        tail[2],
        grad_w_up,
        grad_b_up,
        grad_w_down,
    )


def solution(mesh):
    in_specs = (
        P("rows", "tp", None),
        P("rows", "tp"),
        P(),
        P(),
        P(None, None, "tp"),
        P(None, "tp"),
        P("tp", None),
        P(),
        P(None, "tp"),
        P("tp"),
        P("tp", None),
        P("rows", "tp", None),
    )
    out_specs = (
        P("rows", "tp", None),
        P("rows", "tp", None),
        P(),
        P(),
        P(None, None, "tp"),
        P(None, "tp"),
        P("tp", None),
        P(),
        P(None, "tp"),
        P("tp"),
        P("tp", None),
    )
    return jax.shard_map(
        partial(local, mesh.shape["rows"], mesh.shape["tp"]),
        mesh=mesh,
        in_specs=in_specs,
        out_specs=out_specs,
        check_vma=False,
    )
```

```python
from functools import partial
import math

import jax
import jax.numpy as jnp
from jax import lax
from jax.experimental import pallas as pl
from jax.experimental.pallas import tpu as pltpu
from jax.sharding import PartitionSpec as P

HEAD_DIM = 64
ROT = 32
EPSILON = 1e-05
NEGATIVE = -1e30
VMEM_BYTES = 56 * 2**20
NT = (((1,), (1,)), ((), ()))


class Line:
    def __init__(self):
        self.token = jnp.zeros((8, 128), jnp.float32)

    def join(self, *arrays):
        *arrays, self.token = lax.optimization_barrier((*arrays, self.token))
        return arrays

    def call(
        self, body, name, grid, operands, in_specs, outs, scalars=0, scratch=(), aliases=None, cost=0
    ):
        inputs = len(operands)

        def whole_body(*refs):
            refs = list(refs)
            token = refs.pop(inputs + 1 + len(outs))
            refs.pop(inputs)
            token[...] = jnp.zeros_like(token)
            body(*refs)

        *results, self.token = pl.pallas_call(
            whole_body,
            grid_spec=pltpu.PrefetchScalarGridSpec(
                num_scalar_prefetch=scalars,
                grid=grid,
                in_specs=[*in_specs, pl.BlockSpec(memory_space=pl.ANY)],
                out_specs=[
                    *(spec for _, _, spec in outs),
                    pl.BlockSpec((8, 128), lambda *index: (0, 0)),
                ],
                scratch_shapes=list(scratch),
            ),
            out_shape=[
                *(jax.ShapeDtypeStruct(shape, dtype) for shape, dtype, _ in outs),
                jax.ShapeDtypeStruct((8, 128), jnp.float32),
            ],
            input_output_aliases=aliases or {},
            compiler_params=pltpu.CompilerParams(vmem_limit_bytes=VMEM_BYTES),
            cost_estimate=pl.CostEstimate(
                flops=2**20 + cost, bytes_accessed=2**16, transcendentals=0
            ),
            name=name,
        )(*operands, self.token)
        return results


def whole(*index):
    return (0, 0)


def row(i, *scalars):
    return (i, 0)


def lane_heads(rows, width):
    return lax.broadcasted_iota(jnp.int32, (rows, width), 1) // HEAD_DIM


def swap_pairs(x):
    width = x.shape[1]
    lane = lax.broadcasted_iota(jnp.int32, x.shape, 1) % HEAD_DIM
    up = pltpu.roll(x, width - ROT // 2, 1)
    down = pltpu.roll(x, ROT // 2, 1)
    return jnp.where(lane < ROT // 2, up, down)


def mask_bias(starts, key_first, query_first, block):
    key_index = key_first + lax.broadcasted_iota(jnp.int32, (block, block), 0)
    query_index = query_first + lax.broadcasted_iota(jnp.int32, (block, block), 1)
    allowed = (key_index >= starts) & (key_index <= query_index)
    return jnp.where(allowed, 0.0, NEGATIVE).astype(jnp.float32)


def stack_heads(source, stacked, block):
    length, width = source.shape
    row_heads = lane_heads(block, width)
    for j in range(length // block):
        rows = pl.ds(j * block, block)
        piece = source[rows, :]
        for h in range(width // HEAD_DIM):
            stacked[j, pl.ds(h * block, block), :] = jnp.where(row_heads == h, piece, 0).astype(
                jnp.bfloat16
            )


def forward_kernel(lows, starts, q, k, v, context, lse, v_t, k_heads, acc):
    block, width = q.shape
    heads = width // HEAD_DIM
    length = k.shape[0]
    i = pl.program_id(0)

    @pl.when(i == 0)
    def _():
        stack_heads(k, k_heads, block)
        for j in range(length // block):
            rows = pl.ds(j * block, block)
            v_t[:, rows] = v[rows, :].T

    turned = (q[...] * 0.125).T
    acc[...] = jnp.zeros_like(acc)

    def step(j, carry):
        tops, sums = carry
        first = pl.multiple_of(j * block, block)
        all_scores = jnp.dot(k_heads[j], turned, preferred_element_type=jnp.float32)
        bias = mask_bias(starts[0:1, :], first, i * block, block)
        new_tops, new_sums = [], []
        for h in range(heads):
            rows = pl.ds(h * HEAD_DIM, HEAD_DIM)
            scores = all_scores[h * block : (h + 1) * block, :] + bias
            top = jnp.maximum(tops[h], jnp.max(scores, axis=0, keepdims=True))
            weights = jnp.exp(scores - top)
            keep = jnp.exp(tops[h] - top)
            new_tops.append(top)
            new_sums.append(sums[h] * keep + jnp.sum(weights, axis=0, keepdims=True))
            acc[rows, :] = acc[rows, :] * keep + jnp.dot(
                v_t[rows, pl.ds(first, block)],
                weights.astype(jnp.bfloat16),
                preferred_element_type=jnp.float32,
            )
        return tuple(new_tops), tuple(new_sums)

    empty = tuple(jnp.full((1, block), NEGATIVE, jnp.float32) for _ in range(heads))
    nothing = tuple(jnp.zeros((1, block), jnp.float32) for _ in range(heads))
    tops, sums = lax.fori_loop(lows[i], i + 1, step, (empty, nothing))
    for h in range(heads):
        rows = pl.ds(h * HEAD_DIM, HEAD_DIM)
        acc[rows, :] = acc[rows, :] / sums[h]
        lse[h : h + 1, :] = tops[h] + jnp.log(sums[h])
    context[...] = acc[...].astype(jnp.bfloat16).T


def attend_forward(line, lows, starts, mixed, block):
    length, triple = mixed.shape
    local_width = triple // 3
    blocks = length // block
    stack = (blocks, local_width // HEAD_DIM * block, local_width)
    column = lambda i, lows: (0, i)
    return line.call(
        forward_kernel,
        "attend_forward",
        (blocks,),
        [lows, starts, mixed, mixed, mixed],
        [
            pl.BlockSpec((8, block), column),
            pl.BlockSpec((block, local_width), row),
            pl.BlockSpec((length, local_width), lambda i, lows: (0, 1)),
            pl.BlockSpec((length, local_width), lambda i, lows: (0, 2)),
        ],
        [
            ((length, local_width), jnp.bfloat16, pl.BlockSpec((block, local_width), row)),
            ((8, length), jnp.float32, pl.BlockSpec((8, block), column)),
        ],
        scalars=1,
        scratch=[
            pltpu.VMEM((local_width, length), jnp.bfloat16),
            pltpu.VMEM(stack, jnp.bfloat16),
            pltpu.VMEM((local_width, block), jnp.float32),
        ],
    )


def backward_kernel(
    lows, starts, lse, q, k, v, context, grad, cosine, sine, turned_tables, grad_mixed, k_t, k_heads, v_heads, grad_q, grad_k, grad_v
):
    block, width = q.shape
    heads = width // HEAD_DIM
    length = k.shape[0]
    i = pl.program_id(0)
    blocks = length // block

    @pl.when(i == 0)
    def _():
        grad_k[...] = jnp.zeros_like(grad_k)
        grad_v[...] = jnp.zeros_like(grad_v)
        stack_heads(k, k_heads, block)
        stack_heads(v, v_heads, block)
        for j in range(blocks):
            rows = pl.ds(j * block, block)
            k_t[:, rows] = k[rows, :].T

    row_heads = lane_heads(block, width)
    scaled = q[...] * 0.125
    grads = grad[...]
    masked_q = [jnp.where(row_heads == h, scaled, 0).astype(jnp.bfloat16) for h in range(heads)]
    masked_g = [jnp.where(row_heads == h, grads, 0).astype(jnp.bfloat16) for h in range(heads)]
    turned_q = scaled.T
    turned_g = grads.T
    products = grads.astype(jnp.float32) * context[...].astype(jnp.float32)
    high = products.astype(jnp.bfloat16)
    low = (products - high.astype(jnp.float32)).astype(jnp.bfloat16)
    chooser = lax.broadcasted_iota(jnp.int32, (8, width), 0) == lane_heads(8, width)
    chooser = jnp.where(chooser, 1.0, 0.0).astype(jnp.bfloat16)
    sums = lax.dot_general(chooser, high, NT, preferred_element_type=jnp.float32)
    sums = sums + lax.dot_general(chooser, low, NT, preferred_element_type=jnp.float32)
    inner = [sums[h : h + 1, :] for h in range(heads)]
    grad_q[...] = jnp.zeros_like(grad_q)

    def step(j, carry):
        first = pl.multiple_of(j * block, block)
        here = pl.ds(first, block)
        all_scores = jnp.dot(k_heads[j], turned_q, preferred_element_type=jnp.float32)
        all_grads = jnp.dot(v_heads[j], turned_g, preferred_element_type=jnp.float32)
        bias = mask_bias(starts[0:1, :], first, i * block, block)
        probs, slopes = [], []
        for h in range(heads):
            rows = pl.ds(h * HEAD_DIM, HEAD_DIM)
            part = slice(h * block, (h + 1) * block)
            scores = all_scores[part, :]
            soft = jnp.exp(scores + bias - lse[h : h + 1, :])
            grad_probs = all_grads[part, :]
            slope = (soft * (grad_probs - inner[h])).astype(jnp.bfloat16)
            grad_q[rows, :] += jnp.dot(k_t[rows, here], slope, preferred_element_type=jnp.float32)
            probs.append(soft.astype(jnp.bfloat16))
            slopes.append(slope)
        grad_v[here, :] += jnp.dot(
            jnp.concatenate(probs, axis=1),
            jnp.concatenate(masked_g, axis=0),
            preferred_element_type=jnp.float32,
        )
        grad_k[here, :] += jnp.dot(
            jnp.concatenate(slopes, axis=1),
            jnp.concatenate(masked_q, axis=0),
            preferred_element_type=jnp.float32,
        )
        return carry

    lax.fori_loop(lows[i], i + 1, step, 0)

    def unrotate(x, rows):
        parts = []
        for part in range(width // 128):
            piece = x[:, part * 128 : (part + 1) * 128]
            parts.append(piece * cosine[rows, :] - swap_pairs(piece) * sine[rows, :])
        return jnp.concatenate(parts, axis=1).astype(jnp.bfloat16)

    mine = pl.ds(pl.multiple_of(i * block, block), block)
    cos_t, sin_t = turned_tables[0 : ROT // 2, :], turned_tables[ROT // 2 : ROT, :]
    for h in range(heads):
        top = pl.ds(h * HEAD_DIM, ROT // 2)
        bottom = pl.ds(h * HEAD_DIM + ROT // 2, ROT // 2)
        one, two = grad_q[top, :], grad_q[bottom, :]
        grad_q[top, :] = one * cos_t + two * sin_t
        grad_q[bottom, :] = two * cos_t - one * sin_t
    grad_mixed[mine, 0:width] = (grad_q[...] * 0.125).astype(jnp.bfloat16).T

    @pl.when(i == blocks - 1)
    def _():
        def finish(j, carry):
            rows = pl.ds(pl.multiple_of(j * block, block), block)
            grad_mixed[rows, width : 2 * width] = unrotate(grad_k[rows, :], rows)
            grad_mixed[rows, 2 * width : 3 * width] = grad_v[rows, :].astype(jnp.bfloat16)
            return carry

        lax.fori_loop(0, blocks, finish, 0)


def attend_backward(line, lows, starts, lse, mixed, context, grad_context, cosine, sine, turned, block):
    length, triple = mixed.shape
    local_width = triple // 3
    blocks = length // block
    stack = (blocks, local_width // HEAD_DIM * block, local_width)
    column = lambda i, lows: (0, i)
    return line.call(
        backward_kernel,
        "attend_backward",
        (blocks,),
        [lows, starts, lse, mixed, mixed, mixed, context, grad_context, cosine, sine, turned],
        [
            pl.BlockSpec((8, block), column),
            pl.BlockSpec((8, block), column),
            pl.BlockSpec((block, local_width), row),
            pl.BlockSpec((length, local_width), lambda i, lows: (0, 1)),
            pl.BlockSpec((length, local_width), lambda i, lows: (0, 2)),
            pl.BlockSpec((block, local_width), row),
            pl.BlockSpec((block, local_width), row),
            pl.BlockSpec((length, 128), whole),
            pl.BlockSpec((length, 128), whole),
            pl.BlockSpec((ROT, block), column),
        ],
        [((length, triple), jnp.bfloat16, pl.BlockSpec((length, triple), whole))],
        scalars=1,
        scratch=[
            pltpu.VMEM((local_width, length), jnp.bfloat16),
            pltpu.VMEM(stack, jnp.bfloat16),
            pltpu.VMEM(stack, jnp.bfloat16),
            pltpu.VMEM((local_width, block), jnp.float32),
            pltpu.VMEM((length, local_width), jnp.float32),
            pltpu.VMEM((length, local_width), jnp.float32),
        ],
        cost=632 * 10**8,
    )[0]


def positions_of(segments):
    ids = jnp.arange(8, dtype=jnp.int32)
    counts = jnp.sum((segments[None, :] < ids[:, None]).astype(jnp.int32), axis=1)
    return jnp.sum(jnp.where(segments[None, :] == ids[:, None], counts[:, None], 0), axis=0)


def rotary_tables(positions):
    lane = jnp.arange(128, dtype=jnp.int32) % HEAD_DIM
    step = (lane % (ROT // 2)).astype(jnp.float32)
    inverse = jnp.exp(step * (-2.0 * math.log(10000.0) / ROT))
    angles = positions.astype(jnp.float32)[:, None] * inverse[None, :]
    rotated = (lane < ROT)[None, :]
    cosine = jnp.where(rotated, jnp.cos(angles), 1.0)
    sine = jnp.where(rotated, jnp.where((lane < ROT // 2)[None, :], -1.0, 1.0) * jnp.sin(angles), 0.0)
    turned = jnp.concatenate([cosine[:, : ROT // 2], sine[:, ROT // 2 : ROT]], axis=1).T
    return cosine, sine, turned


def gelu_pair(u):
    scale = math.sqrt(2.0 / math.pi)
    square = u * u
    bent = jnp.tanh(scale * u * (1.0 + 0.044715 * square))
    half = 0.5 * (1.0 + bent)
    slope = half + 0.5 * u * (1.0 - bent * bent) * (scale * (1.0 + 3 * 0.044715 * square))
    return u * half, slope


def project_kernel(place, mine, other, gain, shift, w_qkv, b_qkv, w_up, b_up, cosine, sine, *refs):
    normed, unit, mixed, activated, slope = refs[-5:]
    n = pl.program_id(0)
    block = mine.shape[0]
    width = w_qkv.shape[2]
    strip = min(128, block)
    strips = [pl.ds(r * strip, strip) for r in range(2 * block // strip)]

    @pl.when(n == 0)
    def _():
        for source, first in ((mine, place[1] * block), (other, (1 - place[1]) * block)):
            for r in range(block // strip):
                wide = source[pl.ds(r * strip, strip), :].astype(jnp.float32)
                centred = wide - jnp.mean(wide, axis=1, keepdims=True)
                inverse_std = lax.rsqrt(
                    jnp.mean(centred * centred, axis=1, keepdims=True) + EPSILON
                )
                rows = pl.ds(pl.multiple_of(first + r * strip, strip), strip)
                even = centred * inverse_std
                unit[rows, :] = even.astype(jnp.bfloat16)
                normed[rows, :] = (even * gain[...] + shift[...]).astype(jnp.bfloat16)
        for rows in strips:
            for j in range(3):
                columns = slice(j * width, (j + 1) * width)
                y = jnp.dot(normed[rows, :], w_qkv[j], preferred_element_type=jnp.float32)
                y = y + b_qkv[:, columns]
                if j < 2:
                    parts = []
                    for part in range(width // 128):
                        piece = y[:, part * 128 : (part + 1) * 128]
                        parts.append(piece * cosine[rows, :] + swap_pairs(piece) * sine[rows, :])
                    y = jnp.concatenate(parts, axis=1)
                mixed[rows, columns] = y.astype(jnp.bfloat16)

    @pl.when(n > 0)
    def _():
        for rows in strips:
            u = jnp.dot(normed[rows, :], w_up[...], preferred_element_type=jnp.float32) + b_up[...]
            high, tilt = gelu_pair(u)
            activated[rows, :] = high.astype(jnp.bfloat16)
            slope[rows, :] = tilt.astype(jnp.bfloat16)


def project(line, place, mine, other, weights, tables, length, carried):
    gain, shift, w_qkv, b_qkv, w_up, b_up = weights
    block, width = mine.shape
    local_width = w_qkv.shape[2]
    hidden = w_up.shape[1]
    tile = min(512, hidden)
    up = lambda n, place: (0, jnp.maximum(n - 1, 0))
    here = lambda n, place: (place[0], 0)
    up_here = lambda n, place: (place[0], jnp.maximum(n - 1, 0))
    operands = [place, mine, other, gain, shift, w_qkv, b_qkv, w_up, b_up, *tables, *carried]
    return line.call(
        project_kernel,
        "project",
        (1 + hidden // tile,),
        operands,
        [
            pl.BlockSpec((block, width), whole),
            pl.BlockSpec((block, width), whole),
            pl.BlockSpec((1, width), whole),
            pl.BlockSpec((1, width), whole),
            pl.BlockSpec((3, width, local_width), lambda n, place: (0, 0, 0)),
            pl.BlockSpec((1, 3 * local_width), whole),
            pl.BlockSpec((width, tile), up),
            pl.BlockSpec((1, tile), up),
            pl.BlockSpec((2 * block, 128), here),
            pl.BlockSpec((2 * block, 128), here),
            *[pl.BlockSpec(memory_space=pl.ANY)] * len(carried),
        ],
        [
            ((length, columns), jnp.bfloat16, pl.BlockSpec((2 * block, wide), index))
            for columns, wide, index in (
                (width, width, here),
                (width, width, here),
                (3 * local_width, 3 * local_width, here),
                (hidden, tile, up_here),
                (hidden, tile, up_here),
            )
        ],
        scalars=1,
        aliases={len(operands) - 5 + i: i for i in range(len(carried))},
    )


def backward_products_kernel(layout, *refs):
    grads = refs[:layout]
    w_down, w_out, slope, grad_up, grad_context, total = refs[layout:]
    columns = grads[0].shape[1]
    up, context = 0.0, 0.0
    for c in range(layout):
        part = slice(c * columns, (c + 1) * columns)
        piece = grads[c][...]
        up = up + lax.dot_general(piece, w_down[:, part], NT, preferred_element_type=jnp.float32)
        context = context + lax.dot_general(
            piece, w_out[:, part], NT, preferred_element_type=jnp.float32
        )
    low = (up * slope[...].astype(jnp.float32)).astype(jnp.bfloat16)
    grad_up[...] = low
    grad_context[...] = context.astype(jnp.bfloat16)

    @pl.when(pl.program_id(0) == 0)
    def _():
        total[...] = jnp.zeros_like(total)

    total[...] += jnp.sum(low.astype(jnp.float32), axis=0, keepdims=True)


def backward_products(line, grads, w_down, w_out, slope):
    length, columns = grads[0].shape
    hidden, width = w_down.shape
    local_width = w_out.shape[0]
    tile = min(256, length)
    return line.call(
        partial(backward_products_kernel, len(grads)),
        "backward_products",
        (length // tile,),
        [*grads, w_down, w_out, slope],
        [pl.BlockSpec((tile, columns), row) for _ in grads]
        + [
            pl.BlockSpec((hidden, width), whole),
            pl.BlockSpec((local_width, width), whole),
            pl.BlockSpec((tile, hidden), row),
        ],
        [
            ((length, hidden), jnp.bfloat16, pl.BlockSpec((tile, hidden), row)),
            ((length, local_width), jnp.bfloat16, pl.BlockSpec((tile, local_width), row)),
            ((1, hidden), jnp.float32, pl.BlockSpec((1, hidden), whole)),
        ],
    )


def branch_kernel(context, activated, w_out, w_down, out):
    total = jnp.dot(context[...], w_out[...], preferred_element_type=jnp.float32)
    total = total + jnp.dot(activated[...], w_down[...], preferred_element_type=jnp.float32)
    out[...] = total.astype(jnp.bfloat16)


def branch_sum(line, context, activated, w_out, w_down):
    length, local_width = context.shape
    hidden, width = w_down.shape
    tile = min(256, length)
    return line.call(
        branch_kernel,
        "branch_sum",
        (length // tile,),
        [context, activated, w_out, w_down],
        [
            pl.BlockSpec((tile, local_width), row),
            pl.BlockSpec((tile, hidden), row),
            pl.BlockSpec((local_width, width), whole),
            pl.BlockSpec((hidden, width), whole),
        ],
        [((length, width), jnp.bfloat16, pl.BlockSpec((tile, width), row))],
    )[0]


def normed_kernel(mixed, up, unit, w_qkv, w_up, out, gain, shift):
    width = w_qkv.shape[2]
    total = lax.dot_general(up[...], w_up[...], NT, preferred_element_type=jnp.float32)
    for j in range(3):
        total = total + lax.dot_general(
            mixed[:, j * width : (j + 1) * width],
            w_qkv[j],
            NT,
            preferred_element_type=jnp.float32,
        )
    out[...] = total.astype(jnp.bfloat16)

    @pl.when(pl.program_id(0) == 0)
    def _():
        gain[...] = jnp.zeros_like(gain)
        shift[...] = jnp.zeros_like(shift)

    gain[...] += jnp.sum(total * unit[...].astype(jnp.float32), axis=0, keepdims=True)
    shift[...] += jnp.sum(total, axis=0, keepdims=True)


def normed_sum(line, grad_mixed, grad_up, unit, w_qkv, w_up):
    length, triple = grad_mixed.shape
    width, hidden = w_up.shape
    tile = min(256, length)
    return line.call(
        normed_kernel,
        "normed_sum",
        (length // tile,),
        [grad_mixed, grad_up, unit, w_qkv, w_up],
        [
            pl.BlockSpec((tile, triple), row),
            pl.BlockSpec((tile, hidden), row),
            pl.BlockSpec((tile, width), row),
            pl.BlockSpec(w_qkv.shape, lambda i: (0, 0, 0)),
            pl.BlockSpec((width, hidden), whole),
        ],
        [
            ((length, width), jnp.bfloat16, pl.BlockSpec((tile, width), row)),
            ((1, width), jnp.float32, pl.BlockSpec((1, width), whole)),
            ((1, width), jnp.float32, pl.BlockSpec((1, width), whole)),
        ],
    )


def finish_kernel(layout, order, *refs):
    s = pl.program_id(0)
    outs = refs[-1:] if isinstance(layout, int) else refs[-len(layout) :]
    for index, source in enumerate(refs[:4]):

        @pl.when(s == index)
        def _(source=source):
            if isinstance(layout, int):
                group = outs[0].shape[2]
                for j in range(layout):
                    columns = slice(j * group, (j + 1) * group)
                    outs[0][j] = source[:, columns].astype(jnp.float32)
            else:
                start = 0
                columns = source.shape[1]
                for out in outs:
                    rows, spread = out.shape
                    for j in range(spread // columns):
                        out[:, j * columns : (j + 1) * columns] = source[
                            start : start + rows, :
                        ].astype(jnp.float32)
                        start += rows


def finish(line, order, pieces, layout, carried=(), cost=0):
    rows, columns = pieces[0].shape
    in_specs = [pl.BlockSpec(pieces[0].shape, whole) for _ in range(4)]
    in_specs += [pl.BlockSpec(memory_space=pl.ANY)] * len(carried)
    if isinstance(layout, int):
        group = columns // layout
        spec = pl.BlockSpec((layout, rows, group), lambda s, order: (0, order[s], 0))
        outs = [((layout, 4 * rows, group), jnp.float32, spec)]
    else:
        outs = [
            (
                (4 * tall, spread),
                jnp.float32,
                pl.BlockSpec((tall, wide), lambda s, order, place=place: (order[s], place)),
            )
            for tall, wide, spread, place in layout
        ]
    return line.call(
        partial(finish_kernel, layout),
        "finish",
        (4,),
        [order, *pieces, *carried],
        in_specs,
        outs,
        scalars=1,
        aliases={5 + i: i for i in range(len(carried))},
        cost=cost,
    )


def add_low(one, other):
    return (one.astype(jnp.float32) + other.astype(jnp.float32)).astype(jnp.bfloat16)


def swap_rows(array, bit):
    return lax.ppermute(array, "rows", [(i, i ^ bit) for i in range(4)])


def outer_kernel(extra, order, left, right, *refs):
    s = pl.program_id(0)
    dims = (((0,), (0,)), ((), ()))
    low = lax.dot_general(left[...], right[...], dims, preferred_element_type=jnp.float32)
    parts = [low.astype(jnp.bfloat16)]
    outs = refs[:4]
    if extra:
        second, *more = refs[: 1 + extra]
        outs, held = refs[1 + extra : 5 + extra], refs[-1]

        @pl.when(s == 0)
        def _():
            for k, other in enumerate((*more, right)):
                held[k] = lax.dot_general(
                    second[...], other[...], dims, preferred_element_type=jnp.float32
                ).astype(jnp.bfloat16)

        rows = held.shape[1] // 4
        here = pl.ds(pl.multiple_of(order[s] * rows, rows), rows)
        parts += [held[k, here, :] for k in range(extra + 1)]
    for index, out in enumerate(outs):

        @pl.when(s == index)
        def _(out=out):
            start = 0
            for part in parts:
                out[start : start + part.shape[0], :] = part
                start += part.shape[0]


def outer_parts(line, order, left, right, second=None, more=()):
    length, tall = left.shape
    columns = right.shape[1]
    extra = len(more)
    rows = (tall + (second.shape[1] * (extra + 1) if extra else 0)) // 4
    return line.call(
        partial(outer_kernel, extra),
        "outer_parts",
        (4,),
        [order, left, right] + ([second, *more] if extra else []),
        [
            pl.BlockSpec((length, tall // 4), lambda s, order: (0, order[s])),
            pl.BlockSpec((length, columns), whole),
        ]
        + ([pl.BlockSpec(array.shape, whole) for array in (second, *more)] if extra else []),
        [((rows, columns), jnp.bfloat16, pl.BlockSpec((rows, columns), whole)) for _ in range(4)],
        scalars=1,
        scratch=[pltpu.VMEM((extra + 1, second.shape[1], columns), jnp.bfloat16)] if extra else (),
    )


class RowsSum:
    def __init__(self, rows, line, left, right, second=None, more=()):
        self.rows, self.line, self.phase = rows, line, 0
        if rows != 4:
            self.order = jnp.arange(4, dtype=jnp.int32)
            self.pieces = lax.psum(outer_parts(line, self.order, left, right, second, more), "rows")
            return
        place = lax.axis_index("rows")
        x, y = place % 2, place // 2
        away = jnp.stack([1 - x, 3 - y, x, 2 + y]).astype(jnp.int32)
        self.order = jnp.stack([x, 1 - x, 2 + y, 3 - y]).astype(jnp.int32)
        self.bits = ((1, 2), (2, 1))
        *away, keep_a, keep_b = outer_parts(line, away, left, right, second, more)
        self.keep = [keep_a, keep_b]
        self.send(0, away)

    def send(self, which, arrays):
        arrays = self.line.join(*arrays)
        self.came = [swap_rows(a, bits[which]) for a, bits in zip(arrays, self.bits)]
        return arrays

    def advance(self):
        if self.rows != 4:
            return
        self.phase += 1
        came = self.line.join(*self.came)
        if self.phase < 3:
            self.keep = [add_low(k, c) for k, c in zip(self.keep, came)]
            self.keep = self.send(2 - self.phase, self.keep)
        else:
            self.pieces = [self.keep[0], came[0], self.keep[1], came[1]]

    def finish(self, *layout, **more):
        if self.phase < 3:
            self.advance()
        return finish(self.line, self.order, self.pieces, *layout, **more)


class SmallSum:
    def __init__(self, line, array, more, rows, tp):
        self.line, self.array, self.more = line, array, more
        self.steps = [("tp", 1 << i, tp) for i in range(tp.bit_length() - 1)]
        self.steps += [("rows", 1 << i, rows) for i in range(rows.bit_length() - 1)]
        self.send()

    def send(self):
        if self.steps:
            axis, step, size = self.steps.pop(0)
            if axis == "rows" and self.more is not None:
                self.array, self.more = jnp.concatenate([self.array, self.more]), None
            (self.array,) = self.line.join(self.array)
            self.came = lax.ppermute(self.array, axis, [(i, i ^ step) for i in range(size)])
        else:
            self.came = None

    def step(self):
        if self.came is not None:
            (came,) = self.line.join(self.came)
            self.array = self.array + came
            self.send()

    def rest(self):
        while self.came is not None:
            self.step()
        return self.array


class SmallGather:
    def __init__(self, line, array, me, tp):
        self.line, self.me, self.step = line, me, 1
        while 2 * self.step < tp:
            other = lax.ppermute(array, "tp", [(i, i ^ self.step) for i in range(tp)])
            array = self.laid(array, other)
            self.step *= 2
        (self.array,) = line.join(array)
        self.other = lax.ppermute(self.array, "tp", [(i, i ^ self.step) for i in range(tp)])

    def laid(self, array, other):
        return jnp.where(
            (self.me // self.step) % 2 == 0,
            jnp.concatenate([array, other]),
            jnp.concatenate([other, array]),
        )

    def whole(self):
        return self.line.join(self.laid(self.array, *self.line.join(self.other)))[0]


def token_sum(matrix):
    ones_row = jnp.ones((1, matrix.shape[0]), matrix.dtype)
    return jnp.dot(ones_row, matrix, preferred_element_type=jnp.float32)[0]


def local(
    rows,
    tp,
    hidden_in,
    segment_ids,
    ln_gain,
    ln_bias,
    w_qkv,
    b_qkv,
    w_out,
    out_bias,
    w_up,
    b_up,
    w_down,
    cotangent,
):
    x = hidden_in[0]
    block, width = x.shape
    length = block * tp
    local_width = w_qkv.shape[2]
    hidden = w_up.shape[1]
    chips = tp // 2
    me = lax.axis_index("tp")
    chip, core = me // 2, me % 2
    line = Line()

    around = [(i, (i + 2) % tp) for i in range(tp)]
    sibling = [(i, i ^ 1) for i in range(tp)]
    mine, others = [x], [lax.ppermute(x, "tp", sibling)]
    coming = lax.ppermute(x, "tp", around)
    ids = SmallGather(line, segment_ids[0], me, tp)
    grads = []

    def serve():
        nonlocal coming
        (arrived,) = line.join(coming)
        mine.append(arrived)
        if len(mine) < chips:
            coming = lax.ppermute(arrived, "tp", around)
        others.append(lax.ppermute(arrived, "tp", sibling))
        if len(mine) == max(chips - 1, 2):
            halves = [cotangent[0, :, :columns], cotangent[0, :, columns:]]
            *halves, mine[-1] = lax.optimization_barrier((*halves, arrived))
            grads.extend(lax.all_gather(half, "tp", axis=0, tiled=True) for half in halves)

    columns = width // 2
    serve()
    segments = ids.whole()
    starts = positions_of(segments)
    tables = rotary_tables(jnp.arange(length, dtype=jnp.int32) - starts)
    lows = starts[::block] // block
    starts = jnp.broadcast_to(starts[None], (8, length))
    w_three = jnp.transpose(w_qkv, (1, 0, 2))
    weights = (
        ln_gain.reshape(1, width),
        ln_bias.reshape(1, width),
        w_three,
        b_qkv.reshape(1, 3 * local_width),
        w_up,
        b_up.reshape(1, hidden),
    )
    carried = ()

    def project_slot(s):
        place = jnp.stack([(chip - s + chips) % chips, core]).astype(jnp.int32)
        pair = line.join(mine[s], others[s])
        return project(line, place, *pair, weights, tables[:2], length, carried)

    carried = project_slot(0)
    for s in range(1, chips):
        if s > 1:
            serve()
        if s != 1 or chips == 2:
            for t in (1, 2) if s == 2 else (s,):
                carried = project_slot(t)
    normed, unit, mixed, activated, slope = carried

    hidden_parts, local_parts = hidden // 4, local_width // 4
    sums = partial(RowsSum, rows, line)
    d0 = sums(activated, grads[0])
    context, lse = attend_forward(line, lows, starts, mixed, block)
    d0.advance()
    branch = branch_sum(line, context, activated, w_out, w_down)
    branch_total = lax.psum_scatter(branch, "tp", scatter_dimension=0, tiled=True)
    d1 = sums(activated, grads[1], context, [grads[0]])
    d0.advance()
    grad_up, grad_context, grad_b_up = backward_products(line, grads, w_down, w_out, slope)
    d1.advance()
    up = sums(normed, grad_up)
    d1.advance()
    grad_mixed = attend_backward(
        line, lows, starts, lse, mixed, context, grad_context, *tables, block
    )
    d0.advance()
    up.advance()
    d1.advance()
    (branch_total,) = line.join(branch_total)
    part, gain_part, shift_part = normed_sum(line, grad_mixed, grad_up, unit, w_three, w_up)
    grad_normed = lax.psum_scatter(part, "tp", scatter_dimension=0, tiled=True).astype(jnp.float32)
    up.advance()
    three = sums(normed, grad_mixed)
    small = SmallSum(
        line,
        jnp.concatenate([gain_part, shift_part, token_sum(cotangent[0])[None]], axis=1)[0],
        jnp.concatenate([token_sum(grad_mixed), grad_b_up[0]]),
        rows,
        tp,
    )
    down = d0.finish([(hidden_parts, columns, width, 0)])
    small.step()
    down = d1.finish(
        [(hidden_parts, columns, width, 1), (local_parts, width, width, 0)], carried=down
    )
    up.advance()
    three.advance()
    small.step()
    up = up.finish([(width // 4, hidden, hidden, 0)], cost=1035 * 10**8)
    three.advance()
    small.step()
    small.step()
    three = three.finish(3, cost=230 * 10**8)
    small = small.rest()
    grad_w_down, grad_w_out = down
    grad_w_up = up[0]
    grad_w_qkv = jnp.transpose(three[0], (1, 0, 2))

    inputs = x.astype(jnp.float32)
    hidden_out = (inputs + branch_total.astype(jnp.float32) + out_bias).astype(jnp.bfloat16)
    average = jnp.mean(inputs, axis=-1, keepdims=True)
    centred = inputs - average
    inverse_std = lax.rsqrt(jnp.mean(centred * centred, axis=-1, keepdims=True) + EPSILON)
    unit_rows = centred * inverse_std
    grad_unit = grad_normed * ln_gain
    grad_input = cotangent[0].astype(jnp.float32) + inverse_std * (
        grad_unit
        - jnp.mean(grad_unit, axis=-1, keepdims=True)
        - unit_rows * jnp.mean(grad_unit * unit_rows, axis=-1, keepdims=True)
    )
    tail = small[: 3 * width].reshape(3, width)
    grad_b_qkv = small[3 * width : 3 * (width + local_width)].reshape(3, local_width)
    grad_b_up = small[3 * (width + local_width) :]
    return (
        hidden_out[None],
        grad_input.astype(jnp.bfloat16)[None],
        tail[0],
        tail[1],
        grad_w_qkv,
        grad_b_qkv,
        grad_w_out,
        tail[2],
        grad_w_up,
        grad_b_up,
        grad_w_down,
    )


def solution(mesh):
    in_specs = (
        P("rows", "tp", None),
        P("rows", "tp"),
        P(),
        P(),
        P(None, None, "tp"),
        P(None, "tp"),
        P("tp", None),
        P(),
        P(None, "tp"),
        P("tp"),
        P("tp", None),
        P("rows", "tp", None),
    )
    out_specs = (
        P("rows", "tp", None),
        P("rows", "tp", None),
        P(),
        P(),
        P(None, None, "tp"),
        P(None, "tp"),
        P("tp", None),
        P(),
        P(None, "tp"),
        P("tp"),
        P("tp", None),
    )
    return jax.shard_map(
        partial(local, mesh.shape["rows"], mesh.shape["tp"]),
        mesh=mesh,
        in_specs=in_specs,
        out_specs=out_specs,
        check_vma=False,
    )
```

```python
from functools import partial
import math

import jax
import jax.numpy as jnp
from jax import lax
from jax.experimental import pallas as pl
from jax.experimental.pallas import tpu as pltpu
from jax.sharding import PartitionSpec as P

HEAD_DIM = 64
ROT = 32
EPSILON = 1e-05
NEGATIVE = -1e30
VMEM_BYTES = 56 * 2**20
NT = (((1,), (1,)), ((), ()))


class Line:
    def __init__(self):
        self.token = jnp.zeros((8, 128), jnp.float32)

    def join(self, *arrays):
        *arrays, self.token = lax.optimization_barrier((*arrays, self.token))
        return arrays

    def call(
        self, body, name, grid, operands, in_specs, outs, scalars=0, scratch=(), aliases=None, cost=0
    ):
        inputs = len(operands)

        def whole_body(*refs):
            refs = list(refs)
            token = refs.pop(inputs + 1 + len(outs))
            refs.pop(inputs)
            token[...] = jnp.zeros_like(token)
            body(*refs)

        *results, self.token = pl.pallas_call(
            whole_body,
            grid_spec=pltpu.PrefetchScalarGridSpec(
                num_scalar_prefetch=scalars,
                grid=grid,
                in_specs=[*in_specs, pl.BlockSpec(memory_space=pl.ANY)],
                out_specs=[
                    *(spec for _, _, spec in outs),
                    pl.BlockSpec((8, 128), lambda *index: (0, 0)),
                ],
                scratch_shapes=list(scratch),
            ),
            out_shape=[
                *(jax.ShapeDtypeStruct(shape, dtype) for shape, dtype, _ in outs),
                jax.ShapeDtypeStruct((8, 128), jnp.float32),
            ],
            input_output_aliases=aliases or {},
            compiler_params=pltpu.CompilerParams(vmem_limit_bytes=VMEM_BYTES),
            cost_estimate=pl.CostEstimate(
                flops=2**20 + cost, bytes_accessed=2**16, transcendentals=0
            ),
            name=name,
        )(*operands, self.token)
        return results


def whole(*index):
    return (0, 0)


def row(i, *scalars):
    return (i, 0)


def lane_heads(rows, width):
    return lax.broadcasted_iota(jnp.int32, (rows, width), 1) // HEAD_DIM


def swap_pairs(x):
    width = x.shape[1]
    lane = lax.broadcasted_iota(jnp.int32, x.shape, 1) % HEAD_DIM
    up = pltpu.roll(x, width - ROT // 2, 1)
    down = pltpu.roll(x, ROT // 2, 1)
    return jnp.where(lane < ROT // 2, up, down)


def mask_bias(starts, key_first, query_first, block):
    key_index = key_first + lax.broadcasted_iota(jnp.int32, (block, block), 0)
    query_index = query_first + lax.broadcasted_iota(jnp.int32, (block, block), 1)
    allowed = (key_index >= starts) & (key_index <= query_index)
    return jnp.where(allowed, 0.0, NEGATIVE).astype(jnp.float32)


def stack_heads(source, stacked, block):
    length, width = source.shape
    row_heads = lane_heads(block, width)
    for j in range(length // block):
        rows = pl.ds(j * block, block)
        piece = source[rows, :]
        for h in range(width // HEAD_DIM):
            stacked[j, pl.ds(h * block, block), :] = jnp.where(row_heads == h, piece, 0).astype(
                jnp.bfloat16
            )


def forward_kernel(lows, starts, q, k, v, context, lse, v_t, k_heads, acc):
    block, width = q.shape
    heads = width // HEAD_DIM
    length = k.shape[0]
    i = pl.program_id(0)

    @pl.when(i == 0)
    def _():
        stack_heads(k, k_heads, block)
        for j in range(length // block):
            rows = pl.ds(j * block, block)
            v_t[:, rows] = v[rows, :].T

    turned = (q[...] * 0.125).T
    acc[...] = jnp.zeros_like(acc)

    def step(j, carry):
        tops, sums = carry
        first = pl.multiple_of(j * block, block)
        all_scores = jnp.dot(k_heads[j], turned, preferred_element_type=jnp.float32)
        bias = mask_bias(starts[0:1, :], first, i * block, block)
        new_tops, new_sums = [], []
        for h in range(heads):
            rows = pl.ds(h * HEAD_DIM, HEAD_DIM)
            scores = all_scores[h * block : (h + 1) * block, :] + bias
            top = jnp.maximum(tops[h], jnp.max(scores, axis=0, keepdims=True))
            weights = jnp.exp(scores - top)
            keep = jnp.exp(tops[h] - top)
            new_tops.append(top)
            new_sums.append(sums[h] * keep + jnp.sum(weights, axis=0, keepdims=True))
            acc[rows, :] = acc[rows, :] * keep + jnp.dot(
                v_t[rows, pl.ds(first, block)],
                weights.astype(jnp.bfloat16),
                preferred_element_type=jnp.float32,
            )
        return tuple(new_tops), tuple(new_sums)

    empty = tuple(jnp.full((1, block), NEGATIVE, jnp.float32) for _ in range(heads))
    nothing = tuple(jnp.zeros((1, block), jnp.float32) for _ in range(heads))
    tops, sums = lax.fori_loop(lows[i], i + 1, step, (empty, nothing))
    for h in range(heads):
        rows = pl.ds(h * HEAD_DIM, HEAD_DIM)
        acc[rows, :] = acc[rows, :] / sums[h]
        lse[h : h + 1, :] = tops[h] + jnp.log(sums[h])
    context[...] = acc[...].astype(jnp.bfloat16).T


def attend_forward(line, lows, starts, mixed, block):
    length, triple = mixed.shape
    local_width = triple // 3
    blocks = length // block
    stack = (blocks, local_width // HEAD_DIM * block, local_width)
    column = lambda i, lows: (0, i)
    return line.call(
        forward_kernel,
        "attend_forward",
        (blocks,),
        [lows, starts, mixed, mixed, mixed],
        [
            pl.BlockSpec((8, block), column),
            pl.BlockSpec((block, local_width), row),
            pl.BlockSpec((length, local_width), lambda i, lows: (0, 1)),
            pl.BlockSpec((length, local_width), lambda i, lows: (0, 2)),
        ],
        [
            ((length, local_width), jnp.bfloat16, pl.BlockSpec((block, local_width), row)),
            ((8, length), jnp.float32, pl.BlockSpec((8, block), column)),
        ],
        scalars=1,
        scratch=[
            pltpu.VMEM((local_width, length), jnp.bfloat16),
            pltpu.VMEM(stack, jnp.bfloat16),
            pltpu.VMEM((local_width, block), jnp.float32),
        ],
    )


def backward_kernel(
    lows, starts, lse, q, k, v, context, grad, cosine, sine, turned_tables, grad_mixed, k_t, k_heads, v_heads, grad_q, grad_k, grad_v
):
    block, width = q.shape
    heads = width // HEAD_DIM
    length = k.shape[0]
    i = pl.program_id(0)
    blocks = length // block

    @pl.when(i == 0)
    def _():
        grad_k[...] = jnp.zeros_like(grad_k)
        grad_v[...] = jnp.zeros_like(grad_v)
        stack_heads(k, k_heads, block)
        stack_heads(v, v_heads, block)
        for j in range(blocks):
            rows = pl.ds(j * block, block)
            k_t[:, rows] = k[rows, :].T

    row_heads = lane_heads(block, width)
    scaled = q[...] * 0.125
    grads = grad[...]
    masked_q = [jnp.where(row_heads == h, scaled, 0).astype(jnp.bfloat16) for h in range(heads)]
    masked_g = [jnp.where(row_heads == h, grads, 0).astype(jnp.bfloat16) for h in range(heads)]
    turned_q = scaled.T
    turned_g = grads.T
    products = grads.astype(jnp.float32) * context[...].astype(jnp.float32)
    high = products.astype(jnp.bfloat16)
    low = (products - high.astype(jnp.float32)).astype(jnp.bfloat16)
    chooser = lax.broadcasted_iota(jnp.int32, (8, width), 0) == lane_heads(8, width)
    chooser = jnp.where(chooser, 1.0, 0.0).astype(jnp.bfloat16)
    sums = lax.dot_general(chooser, high, NT, preferred_element_type=jnp.float32)
    sums = sums + lax.dot_general(chooser, low, NT, preferred_element_type=jnp.float32)
    inner = [sums[h : h + 1, :] for h in range(heads)]
    grad_q[...] = jnp.zeros_like(grad_q)

    def step(j, carry):
        first = pl.multiple_of(j * block, block)
        here = pl.ds(first, block)
        all_scores = jnp.dot(k_heads[j], turned_q, preferred_element_type=jnp.float32)
        all_grads = jnp.dot(v_heads[j], turned_g, preferred_element_type=jnp.float32)
        bias = mask_bias(starts[0:1, :], first, i * block, block)
        probs, slopes = [], []
        for h in range(heads):
            rows = pl.ds(h * HEAD_DIM, HEAD_DIM)
            part = slice(h * block, (h + 1) * block)
            scores = all_scores[part, :]
            soft = jnp.exp(scores + bias - lse[h : h + 1, :])
            grad_probs = all_grads[part, :]
            slope = (soft * (grad_probs - inner[h])).astype(jnp.bfloat16)
            grad_q[rows, :] += jnp.dot(k_t[rows, here], slope, preferred_element_type=jnp.float32)
            probs.append(soft.astype(jnp.bfloat16))
            slopes.append(slope)
        grad_v[here, :] += jnp.dot(
            jnp.concatenate(probs, axis=1),
            jnp.concatenate(masked_g, axis=0),
            preferred_element_type=jnp.float32,
        )
        grad_k[here, :] += jnp.dot(
            jnp.concatenate(slopes, axis=1),
            jnp.concatenate(masked_q, axis=0),
            preferred_element_type=jnp.float32,
        )
        return carry

    lax.fori_loop(lows[i], i + 1, step, 0)

    def unrotate(x, rows):
        parts = []
        for part in range(width // 128):
            piece = x[:, part * 128 : (part + 1) * 128]
            parts.append(piece * cosine[rows, :] - swap_pairs(piece) * sine[rows, :])
        return jnp.concatenate(parts, axis=1).astype(jnp.bfloat16)

    mine = pl.ds(pl.multiple_of(i * block, block), block)
    cos_t, sin_t = turned_tables[0 : ROT // 2, :], turned_tables[ROT // 2 : ROT, :]
    for h in range(heads):
        top = pl.ds(h * HEAD_DIM, ROT // 2)
        bottom = pl.ds(h * HEAD_DIM + ROT // 2, ROT // 2)
        one, two = grad_q[top, :], grad_q[bottom, :]
        grad_q[top, :] = one * cos_t + two * sin_t
        grad_q[bottom, :] = two * cos_t - one * sin_t
    grad_mixed[mine, 0:width] = (grad_q[...] * 0.125).astype(jnp.bfloat16).T

    @pl.when(i == blocks - 1)
    def _():
        def finish(j, carry):
            rows = pl.ds(pl.multiple_of(j * block, block), block)
            grad_mixed[rows, width : 2 * width] = unrotate(grad_k[rows, :], rows)
            grad_mixed[rows, 2 * width : 3 * width] = grad_v[rows, :].astype(jnp.bfloat16)
            return carry

        lax.fori_loop(0, blocks, finish, 0)


def attend_backward(line, lows, starts, lse, mixed, context, grad_context, cosine, sine, turned, block):
    length, triple = mixed.shape
    local_width = triple // 3
    blocks = length // block
    stack = (blocks, local_width // HEAD_DIM * block, local_width)
    column = lambda i, lows: (0, i)
    return line.call(
        backward_kernel,
        "attend_backward",
        (blocks,),
        [lows, starts, lse, mixed, mixed, mixed, context, grad_context, cosine, sine, turned],
        [
            pl.BlockSpec((8, block), column),
            pl.BlockSpec((8, block), column),
            pl.BlockSpec((block, local_width), row),
            pl.BlockSpec((length, local_width), lambda i, lows: (0, 1)),
            pl.BlockSpec((length, local_width), lambda i, lows: (0, 2)),
            pl.BlockSpec((block, local_width), row),
            pl.BlockSpec((block, local_width), row),
            pl.BlockSpec((length, 128), whole),
            pl.BlockSpec((length, 128), whole),
            pl.BlockSpec((ROT, block), column),
        ],
        [((length, triple), jnp.bfloat16, pl.BlockSpec((length, triple), whole))],
        scalars=1,
        scratch=[
            pltpu.VMEM((local_width, length), jnp.bfloat16),
            pltpu.VMEM(stack, jnp.bfloat16),
            pltpu.VMEM(stack, jnp.bfloat16),
            pltpu.VMEM((local_width, block), jnp.float32),
            pltpu.VMEM((length, local_width), jnp.float32),
            pltpu.VMEM((length, local_width), jnp.float32),
        ],
        cost=632 * 10**8,
    )[0]


def positions_of(segments):
    ids = jnp.arange(8, dtype=jnp.int32)
    counts = jnp.sum((segments[None, :] < ids[:, None]).astype(jnp.int32), axis=1)
    return jnp.sum(jnp.where(segments[None, :] == ids[:, None], counts[:, None], 0), axis=0)


def rotary_tables(positions):
    lane = jnp.arange(128, dtype=jnp.int32) % HEAD_DIM
    step = (lane % (ROT // 2)).astype(jnp.float32)
    inverse = jnp.exp(step * (-2.0 * math.log(10000.0) / ROT))
    angles = positions.astype(jnp.float32)[:, None] * inverse[None, :]
    rotated = (lane < ROT)[None, :]
    cosine = jnp.where(rotated, jnp.cos(angles), 1.0)
    sine = jnp.where(rotated, jnp.where((lane < ROT // 2)[None, :], -1.0, 1.0) * jnp.sin(angles), 0.0)
    turned = jnp.concatenate([cosine[:, : ROT // 2], sine[:, ROT // 2 : ROT]], axis=1).T
    return cosine, sine, turned


def gelu_pair(u):
    scale = math.sqrt(2.0 / math.pi)
    square = u * u
    bent = jnp.tanh(scale * u * (1.0 + 0.044715 * square))
    half = 0.5 * (1.0 + bent)
    slope = half + 0.5 * u * (1.0 - bent * bent) * (scale * (1.0 + 3 * 0.044715 * square))
    return u * half, slope


def project_kernel(place, mine, other, gain, shift, w_qkv, b_qkv, w_up, b_up, cosine, sine, *refs):
    normed, unit, mixed, activated, slope = refs[-5:]
    n = pl.program_id(0)
    block = mine.shape[0]
    width = w_qkv.shape[2]
    strip = min(128, block)
    strips = [pl.ds(r * strip, strip) for r in range(2 * block // strip)]

    @pl.when(n == 0)
    def _():
        for source, first in ((mine, place[1] * block), (other, (1 - place[1]) * block)):
            for r in range(block // strip):
                wide = source[pl.ds(r * strip, strip), :].astype(jnp.float32)
                centred = wide - jnp.mean(wide, axis=1, keepdims=True)
                inverse_std = lax.rsqrt(
                    jnp.mean(centred * centred, axis=1, keepdims=True) + EPSILON
                )
                rows = pl.ds(pl.multiple_of(first + r * strip, strip), strip)
                even = centred * inverse_std
                unit[rows, :] = even.astype(jnp.bfloat16)
                normed[rows, :] = (even * gain[...] + shift[...]).astype(jnp.bfloat16)
        for rows in strips:
            for j in range(3):
                columns = slice(j * width, (j + 1) * width)
                y = jnp.dot(normed[rows, :], w_qkv[j], preferred_element_type=jnp.float32)
                y = y + b_qkv[:, columns]
                if j < 2:
                    parts = []
                    for part in range(width // 128):
                        piece = y[:, part * 128 : (part + 1) * 128]
                        parts.append(piece * cosine[rows, :] + swap_pairs(piece) * sine[rows, :])
                    y = jnp.concatenate(parts, axis=1)
                mixed[rows, columns] = y.astype(jnp.bfloat16)

    @pl.when(n > 0)
    def _():
        for rows in strips:
            u = jnp.dot(normed[rows, :], w_up[...], preferred_element_type=jnp.float32) + b_up[...]
            high, tilt = gelu_pair(u)
            activated[rows, :] = high.astype(jnp.bfloat16)
            slope[rows, :] = tilt.astype(jnp.bfloat16)


def project(line, place, mine, other, weights, tables, length, carried, cost=0):
    gain, shift, w_qkv, b_qkv, w_up, b_up = weights
    block, width = mine.shape
    local_width = w_qkv.shape[2]
    hidden = w_up.shape[1]
    tile = min(512, hidden)
    up = lambda n, place: (0, jnp.maximum(n - 1, 0))
    here = lambda n, place: (place[0], 0)
    up_here = lambda n, place: (place[0], jnp.maximum(n - 1, 0))
    operands = [place, mine, other, gain, shift, w_qkv, b_qkv, w_up, b_up, *tables, *carried]
    return line.call(
        project_kernel,
        "project",
        (1 + hidden // tile,),
        operands,
        [
            pl.BlockSpec((block, width), whole),
            pl.BlockSpec((block, width), whole),
            pl.BlockSpec((1, width), whole),
            pl.BlockSpec((1, width), whole),
            pl.BlockSpec((3, width, local_width), lambda n, place: (0, 0, 0)),
            pl.BlockSpec((1, 3 * local_width), whole),
            pl.BlockSpec((width, tile), up),
            pl.BlockSpec((1, tile), up),
            pl.BlockSpec((2 * block, 128), here),
            pl.BlockSpec((2 * block, 128), here),
            *[pl.BlockSpec(memory_space=pl.ANY)] * len(carried),
        ],
        [
            ((length, columns), jnp.bfloat16, pl.BlockSpec((2 * block, wide), index))
            for columns, wide, index in (
                (width, width, here),
                (width, width, here),
                (3 * local_width, 3 * local_width, here),
                (hidden, tile, up_here),
                (hidden, tile, up_here),
            )
        ],
        scalars=1,
        aliases={len(operands) - 5 + i: i for i in range(len(carried))},
        cost=cost,
    )


def backward_products_kernel(layout, *refs):
    grads = refs[:layout]
    w_down, w_out, slope, grad_up, grad_context, total = refs[layout:]
    columns = grads[0].shape[1]
    up, context = 0.0, 0.0
    for c in range(layout):
        part = slice(c * columns, (c + 1) * columns)
        piece = grads[c][...]
        up = up + lax.dot_general(piece, w_down[:, part], NT, preferred_element_type=jnp.float32)
        context = context + lax.dot_general(
            piece, w_out[:, part], NT, preferred_element_type=jnp.float32
        )
    low = (up * slope[...].astype(jnp.float32)).astype(jnp.bfloat16)
    grad_up[...] = low
    grad_context[...] = context.astype(jnp.bfloat16)

    @pl.when(pl.program_id(0) == 0)
    def _():
        total[...] = jnp.zeros_like(total)

    total[...] += jnp.sum(low.astype(jnp.float32), axis=0, keepdims=True)


def backward_products(line, grads, w_down, w_out, slope):
    length, columns = grads[0].shape
    hidden, width = w_down.shape
    local_width = w_out.shape[0]
    tile = min(256, length)
    return line.call(
        partial(backward_products_kernel, len(grads)),
        "backward_products",
        (length // tile,),
        [*grads, w_down, w_out, slope],
        [pl.BlockSpec((tile, columns), row) for _ in grads]
        + [
            pl.BlockSpec((hidden, width), whole),
            pl.BlockSpec((local_width, width), whole),
            pl.BlockSpec((tile, hidden), row),
        ],
        [
            ((length, hidden), jnp.bfloat16, pl.BlockSpec((tile, hidden), row)),
            ((length, local_width), jnp.bfloat16, pl.BlockSpec((tile, local_width), row)),
            ((1, hidden), jnp.float32, pl.BlockSpec((1, hidden), whole)),
        ],
    )


def branch_kernel(context, activated, w_out, w_down, out):
    total = jnp.dot(context[...], w_out[...], preferred_element_type=jnp.float32)
    total = total + jnp.dot(activated[...], w_down[...], preferred_element_type=jnp.float32)
    out[...] = total.astype(jnp.bfloat16)


def branch_sum(line, context, activated, w_out, w_down):
    length, local_width = context.shape
    hidden, width = w_down.shape
    tile = min(256, length)
    return line.call(
        branch_kernel,
        "branch_sum",
        (length // tile,),
        [context, activated, w_out, w_down],
        [
            pl.BlockSpec((tile, local_width), row),
            pl.BlockSpec((tile, hidden), row),
            pl.BlockSpec((local_width, width), whole),
            pl.BlockSpec((hidden, width), whole),
        ],
        [((length, width), jnp.bfloat16, pl.BlockSpec((tile, width), row))],
    )[0]


def normed_kernel(mixed, up, unit, w_qkv, w_up, out, gain, shift):
    width = w_qkv.shape[2]
    total = lax.dot_general(up[...], w_up[...], NT, preferred_element_type=jnp.float32)
    for j in range(3):
        total = total + lax.dot_general(
            mixed[:, j * width : (j + 1) * width],
            w_qkv[j],
            NT,
            preferred_element_type=jnp.float32,
        )
    out[...] = total.astype(jnp.bfloat16)

    @pl.when(pl.program_id(0) == 0)
    def _():
        gain[...] = jnp.zeros_like(gain)
        shift[...] = jnp.zeros_like(shift)

    gain[...] += jnp.sum(total * unit[...].astype(jnp.float32), axis=0, keepdims=True)
    shift[...] += jnp.sum(total, axis=0, keepdims=True)


def normed_sum(line, grad_mixed, grad_up, unit, w_qkv, w_up):
    length, triple = grad_mixed.shape
    width, hidden = w_up.shape
    tile = min(256, length)
    return line.call(
        normed_kernel,
        "normed_sum",
        (length // tile,),
        [grad_mixed, grad_up, unit, w_qkv, w_up],
        [
            pl.BlockSpec((tile, triple), row),
            pl.BlockSpec((tile, hidden), row),
            pl.BlockSpec((tile, width), row),
            pl.BlockSpec(w_qkv.shape, lambda i: (0, 0, 0)),
            pl.BlockSpec((width, hidden), whole),
        ],
        [
            ((length, width), jnp.bfloat16, pl.BlockSpec((tile, width), row)),
            ((1, width), jnp.float32, pl.BlockSpec((1, width), whole)),
            ((1, width), jnp.float32, pl.BlockSpec((1, width), whole)),
        ],
    )


def finish_kernel(layout, order, *refs):
    s = pl.program_id(0)
    outs = refs[-1:] if isinstance(layout, int) else refs[-len(layout) :]
    for index, source in enumerate(refs[:4]):

        @pl.when(s == index)
        def _(source=source):
            if isinstance(layout, int):
                group = outs[0].shape[2]
                for j in range(layout):
                    columns = slice(j * group, (j + 1) * group)
                    outs[0][j] = source[:, columns].astype(jnp.float32)
            else:
                start = 0
                columns = source.shape[1]
                for out in outs:
                    rows, spread = out.shape
                    for j in range(spread // columns):
                        out[:, j * columns : (j + 1) * columns] = source[
                            start : start + rows, :
                        ].astype(jnp.float32)
                        start += rows


def finish(line, order, pieces, layout, carried=(), cost=0):
    rows, columns = pieces[0].shape
    in_specs = [pl.BlockSpec(pieces[0].shape, whole) for _ in range(4)]
    in_specs += [pl.BlockSpec(memory_space=pl.ANY)] * len(carried)
    if isinstance(layout, int):
        group = columns // layout
        spec = pl.BlockSpec((layout, rows, group), lambda s, order: (0, order[s], 0))
        outs = [((layout, 4 * rows, group), jnp.float32, spec)]
    else:
        outs = [
            (
                (4 * tall, spread),
                jnp.float32,
                pl.BlockSpec((tall, wide), lambda s, order, place=place: (order[s], place)),
            )
            for tall, wide, spread, place in layout
        ]
    return line.call(
        partial(finish_kernel, layout),
        "finish",
        (4,),
        [order, *pieces, *carried],
        in_specs,
        outs,
        scalars=1,
        aliases={5 + i: i for i in range(len(carried))},
        cost=cost,
    )


def add_low(one, other):
    return (one.astype(jnp.float32) + other.astype(jnp.float32)).astype(jnp.bfloat16)


def swap_rows(array, bit):
    return lax.ppermute(array, "rows", [(i, i ^ bit) for i in range(4)])


def outer_kernel(extra, order, left, right, *refs):
    s = pl.program_id(0)
    dims = (((0,), (0,)), ((), ()))
    low = lax.dot_general(left[...], right[...], dims, preferred_element_type=jnp.float32)
    parts = [low.astype(jnp.bfloat16)]
    outs = refs[extra : 4 + extra]
    if extra:
        second, held = refs[0], refs[-1]

        @pl.when(s == 0)
        def _():
            held[...] = lax.dot_general(
                second[...], right[...], dims, preferred_element_type=jnp.float32
            ).astype(jnp.bfloat16)

        rows = held.shape[0] // 4
        parts.append(held[pl.ds(pl.multiple_of(order[s] * rows, rows), rows), :])
    for index, out in enumerate(outs):

        @pl.when(s == index)
        def _(out=out):
            start = 0
            for part in parts:
                out[start : start + part.shape[0], :] = part
                start += part.shape[0]


def outer_parts(line, order, left, right, second=None):
    length, tall = left.shape
    columns = right.shape[1]
    extra = [] if second is None else [second]
    rows = (tall + sum(array.shape[1] for array in extra)) // 4
    return line.call(
        partial(outer_kernel, len(extra)),
        "outer_parts",
        (4,),
        [order, left, right, *extra],
        [
            pl.BlockSpec((length, tall // 4), lambda s, order: (0, order[s])),
            *(pl.BlockSpec(array.shape, whole) for array in (right, *extra)),
        ],
        [((rows, columns), jnp.bfloat16, pl.BlockSpec((rows, columns), whole)) for _ in range(4)],
        scalars=1,
        scratch=[pltpu.VMEM((array.shape[1], columns), jnp.bfloat16) for array in extra],
    )


class RowsSum:
    def __init__(self, rows, line, left, right, second=None, between=None):
        self.rows, self.line, self.phase = rows, line, 0
        if rows != 4:
            self.order = jnp.arange(4, dtype=jnp.int32)
            self.pieces = lax.psum(outer_parts(line, self.order, left, right, second), "rows")
            return
        place = lax.axis_index("rows")
        x, y = place % 2, place // 2
        away = jnp.stack([1 - x, 3 - y, x, 2 + y]).astype(jnp.int32)
        self.order = jnp.stack([x, 1 - x, 2 + y, 3 - y]).astype(jnp.int32)
        self.bits = ((1, 2), (2, 1))
        *away, keep_a, keep_b = outer_parts(line, away, left, right, second)
        self.keep = [keep_a, keep_b]
        if between is not None:
            between()
        self.send(0, away)

    def send(self, which, arrays):
        arrays = self.line.join(*arrays)
        self.came = [swap_rows(a, bits[which]) for a, bits in zip(arrays, self.bits)]
        return arrays

    def advance(self):
        if self.rows != 4:
            return
        self.phase += 1
        came = self.line.join(*self.came)
        if self.phase < 3:
            self.keep = [add_low(k, c) for k, c in zip(self.keep, came)]
            self.keep = self.send(2 - self.phase, self.keep)
        else:
            self.pieces = [self.keep[0], came[0], self.keep[1], came[1]]

    def finish(self, *layout, **more):
        if self.phase < 3:
            self.advance()
        return finish(self.line, self.order, self.pieces, *layout, **more)


class SmallSum:
    def __init__(self, line, array, more, rows, tp):
        self.line, self.array, self.more = line, array, more
        self.steps = [("tp", 1 << i, tp) for i in range(tp.bit_length() - 1)]
        self.steps += [("rows", 1 << i, rows) for i in range(rows.bit_length() - 1)]
        self.send()

    def send(self):
        if self.steps:
            axis, step, size = self.steps.pop(0)
            if axis == "rows" and self.more is not None:
                self.array, self.more = jnp.concatenate([self.array, self.more]), None
            (self.array,) = self.line.join(self.array)
            self.came = lax.ppermute(self.array, axis, [(i, i ^ step) for i in range(size)])
        else:
            self.came = None

    def step(self):
        if self.came is not None:
            (came,) = self.line.join(self.came)
            self.array = self.array + came
            self.send()

    def rest(self):
        while self.came is not None:
            self.step()
        return self.array


class SmallGather:
    def __init__(self, line, array, me, tp):
        self.line, self.me, self.step = line, me, 1
        while 2 * self.step < tp:
            other = lax.ppermute(array, "tp", [(i, i ^ self.step) for i in range(tp)])
            array = self.laid(array, other)
            self.step *= 2
        (self.array,) = line.join(array)
        self.other = lax.ppermute(self.array, "tp", [(i, i ^ self.step) for i in range(tp)])

    def laid(self, array, other):
        return jnp.where(
            (self.me // self.step) % 2 == 0,
            jnp.concatenate([array, other]),
            jnp.concatenate([other, array]),
        )

    def whole(self):
        return self.line.join(self.laid(self.array, *self.line.join(self.other)))[0]


def token_sum(matrix):
    ones_row = jnp.ones((1, matrix.shape[0]), matrix.dtype)
    return jnp.dot(ones_row, matrix, preferred_element_type=jnp.float32)[0]


def local(
    rows,
    tp,
    hidden_in,
    segment_ids,
    ln_gain,
    ln_bias,
    w_qkv,
    b_qkv,
    w_out,
    out_bias,
    w_up,
    b_up,
    w_down,
    cotangent,
):
    x = hidden_in[0]
    block, width = x.shape
    length = block * tp
    local_width = w_qkv.shape[2]
    hidden = w_up.shape[1]
    chips = tp // 2
    me = lax.axis_index("tp")
    chip, core = me // 2, me % 2
    line = Line()

    around = [(i, (i + 2) % tp) for i in range(tp)]
    sibling = [(i, i ^ 1) for i in range(tp)]
    mine, others = [x], [lax.ppermute(x, "tp", sibling)]
    coming = lax.ppermute(x, "tp", around)
    ids = SmallGather(line, segment_ids[0], me, tp)

    def serve():
        nonlocal coming
        (arrived,) = line.join(coming)
        mine.append(arrived)
        if len(mine) < chips:
            coming = lax.ppermute(arrived, "tp", around)
        others.append(lax.ppermute(arrived, "tp", sibling))
    columns = width // 2
    serve()
    segments = ids.whole()
    starts = positions_of(segments)
    tables = rotary_tables(jnp.arange(length, dtype=jnp.int32) - starts)
    lows = starts[::block] // block
    starts = jnp.broadcast_to(starts[None], (8, length))
    w_three = jnp.transpose(w_qkv, (1, 0, 2))
    weights = (
        ln_gain.reshape(1, width),
        ln_bias.reshape(1, width),
        w_three,
        b_qkv.reshape(1, 3 * local_width),
        w_up,
        b_up.reshape(1, hidden),
    )
    carried = ()

    def project_slot(s, cost=0):
        place = jnp.stack([(chip - s + chips) % chips, core]).astype(jnp.int32)
        pair = line.join(mine[s], others[s])
        return project(line, place, *pair, weights, tables[:2], length, carried, cost)

    carried = project_slot(0)
    for s in range(1, chips):
        if s > 1:
            serve()
        if s != 1 or chips == 2:
            for t in (1, 2) if s == 2 else (s,):
                carried = project_slot(t, cost=920 * 10**8)
                if t == max(chips - 3, 1):
                    halves = line.join(cotangent[0, :, :columns], cotangent[0, :, columns:])
                    grads = [lax.all_gather(half, "tp", axis=0, tiled=True) for half in halves]
    normed, unit, mixed, activated, slope = carried

    hidden_parts, local_parts = hidden // 4, local_width // 4
    sums = partial(RowsSum, rows, line)
    context, lse = attend_forward(line, lows, starts, mixed, block)
    d0 = sums(activated, grads[0], context)
    branch = branch_sum(line, context, activated, w_out, w_down)
    d0.advance()
    (branch,) = line.join(branch)
    branch_total = lax.psum_scatter(branch, "tp", scatter_dimension=0, tiled=True)
    d1 = sums(activated, grads[1], context)
    d0.advance()
    grad_up, grad_context, grad_b_up = backward_products(line, grads, w_down, w_out, slope)
    d1.advance()
    up = sums(normed, grad_up, between=d0.advance)
    d1.advance()
    grad_mixed = attend_backward(
        line, lows, starts, lse, mixed, context, grad_context, *tables, block
    )
    up.advance()
    d1.advance()
    (branch_total,) = line.join(branch_total)
    part, gain_part, shift_part = normed_sum(line, grad_mixed, grad_up, unit, w_three, w_up)
    grad_normed = lax.psum_scatter(part, "tp", scatter_dimension=0, tiled=True).astype(jnp.float32)
    up.advance()
    three = sums(normed, grad_mixed)
    small = SmallSum(
        line,
        jnp.concatenate([gain_part, shift_part, token_sum(cotangent[0])[None]], axis=1)[0],
        jnp.concatenate([token_sum(grad_mixed), grad_b_up[0]]),
        rows,
        tp,
    )
    down = d0.finish([(hidden_parts, columns, width, 0), (local_parts, columns, width, 0)])
    small.step()
    down = d1.finish(
        [(hidden_parts, columns, width, 1), (local_parts, columns, width, 1)], carried=down
    )
    up.advance()
    three.advance()
    small.step()
    up = up.finish([(width // 4, hidden, hidden, 0)], cost=1035 * 10**8)
    three.advance()
    small.step()
    small.step()
    three = three.finish(3, cost=230 * 10**8)
    small = small.rest()
    grad_w_down, grad_w_out = down
    grad_w_up = up[0]
    grad_w_qkv = jnp.transpose(three[0], (1, 0, 2))

    inputs = x.astype(jnp.float32)
    hidden_out = (inputs + branch_total.astype(jnp.float32) + out_bias).astype(jnp.bfloat16)
    average = jnp.mean(inputs, axis=-1, keepdims=True)
    centred = inputs - average
    inverse_std = lax.rsqrt(jnp.mean(centred * centred, axis=-1, keepdims=True) + EPSILON)
    unit_rows = centred * inverse_std
    grad_unit = grad_normed * ln_gain
    grad_input = cotangent[0].astype(jnp.float32) + inverse_std * (
        grad_unit
        - jnp.mean(grad_unit, axis=-1, keepdims=True)
        - unit_rows * jnp.mean(grad_unit * unit_rows, axis=-1, keepdims=True)
    )
    tail = small[: 3 * width].reshape(3, width)
    grad_b_qkv = small[3 * width : 3 * (width + local_width)].reshape(3, local_width)
    grad_b_up = small[3 * (width + local_width) :]
    return (
        hidden_out[None],
        grad_input.astype(jnp.bfloat16)[None],
        tail[0],
        tail[1],
        grad_w_qkv,
        grad_b_qkv,
        grad_w_out,
        tail[2],
        grad_w_up,
        grad_b_up,
        grad_w_down,
    )


def solution(mesh):
    in_specs = (
        P("rows", "tp", None),
        P("rows", "tp"),
        P(),
        P(),
        P(None, None, "tp"),
        P(None, "tp"),
        P("tp", None),
        P(),
        P(None, "tp"),
        P("tp"),
        P("tp", None),
        P("rows", "tp", None),
    )
    out_specs = (
        P("rows", "tp", None),
        P("rows", "tp", None),
        P(),
        P(),
        P(None, None, "tp"),
        P(None, "tp"),
        P("tp", None),
        P(),
        P(None, "tp"),
        P("tp"),
        P("tp", None),
    )
    return jax.shard_map(
        partial(local, mesh.shape["rows"], mesh.shape["tp"]),
        mesh=mesh,
        in_specs=in_specs,
        out_specs=out_specs,
        check_vma=False,
    )
```

```python
from functools import partial
import math

import jax
import jax.numpy as jnp
from jax import lax
from jax.experimental import pallas as pl
from jax.experimental.pallas import tpu as pltpu
from jax.sharding import PartitionSpec as P

HEAD_DIM = 64
ROT = 32
EPSILON = 1e-05
NEGATIVE = -1e30
VMEM_BYTES = 56 * 2**20
NT = (((1,), (1,)), ((), ()))


class Line:
    def __init__(self):
        self.token = jnp.zeros((8, 128), jnp.float32)

    def join(self, *arrays):
        *arrays, self.token = lax.optimization_barrier((*arrays, self.token))
        return arrays

    def call(
        self, body, name, grid, operands, in_specs, outs, scalars=0, scratch=(), aliases=None, cost=0
    ):
        inputs = len(operands)

        def whole_body(*refs):
            refs = list(refs)
            token = refs.pop(inputs + 1 + len(outs))
            refs.pop(inputs)
            token[...] = jnp.zeros_like(token)
            body(*refs)

        *results, self.token = pl.pallas_call(
            whole_body,
            grid_spec=pltpu.PrefetchScalarGridSpec(
                num_scalar_prefetch=scalars,
                grid=grid,
                in_specs=[*in_specs, pl.BlockSpec(memory_space=pl.ANY)],
                out_specs=[
                    *(spec for _, _, spec in outs),
                    pl.BlockSpec((8, 128), lambda *index: (0, 0)),
                ],
                scratch_shapes=list(scratch),
            ),
            out_shape=[
                *(jax.ShapeDtypeStruct(shape, dtype) for shape, dtype, _ in outs),
                jax.ShapeDtypeStruct((8, 128), jnp.float32),
            ],
            input_output_aliases=aliases or {},
            compiler_params=pltpu.CompilerParams(vmem_limit_bytes=VMEM_BYTES),
            cost_estimate=pl.CostEstimate(
                flops=2**20 + cost, bytes_accessed=2**16, transcendentals=0
            ),
            name=name,
        )(*operands, self.token)
        return results


def whole(*index):
    return (0, 0)


def row(i, *scalars):
    return (i, 0)


def lane_heads(rows, width):
    return lax.broadcasted_iota(jnp.int32, (rows, width), 1) // HEAD_DIM


def swap_pairs(x):
    width = x.shape[1]
    lane = lax.broadcasted_iota(jnp.int32, x.shape, 1) % HEAD_DIM
    up = pltpu.roll(x, width - ROT // 2, 1)
    down = pltpu.roll(x, ROT // 2, 1)
    return jnp.where(lane < ROT // 2, up, down)


def mask_bias(starts, key_first, query_first, block):
    key_index = key_first + lax.broadcasted_iota(jnp.int32, (block, block), 0)
    query_index = query_first + lax.broadcasted_iota(jnp.int32, (block, block), 1)
    allowed = (key_index >= starts) & (key_index <= query_index)
    return jnp.where(allowed, 0.0, NEGATIVE).astype(jnp.float32)


def stack_heads(source, stacked, block):
    length, width = source.shape
    row_heads = lane_heads(block, width)
    for j in range(length // block):
        rows = pl.ds(j * block, block)
        piece = source[rows, :]
        for h in range(width // HEAD_DIM):
            stacked[j, pl.ds(h * block, block), :] = jnp.where(row_heads == h, piece, 0).astype(
                jnp.bfloat16
            )


def forward_kernel(lows, starts, q, k, v, context, lse, v_t, k_heads, acc):
    block, width = q.shape
    heads = width // HEAD_DIM
    length = k.shape[0]
    i = pl.program_id(0)

    @pl.when(i == 0)
    def _():
        stack_heads(k, k_heads, block)
        for j in range(length // block):
            rows = pl.ds(j * block, block)
            v_t[:, rows] = v[rows, :].T

    turned = (q[...] * 0.125).T
    acc[...] = jnp.zeros_like(acc)

    def step(j, carry):
        tops, sums = carry
        first = pl.multiple_of(j * block, block)
        all_scores = jnp.dot(k_heads[j], turned, preferred_element_type=jnp.float32)
        bias = mask_bias(starts[0:1, :], first, i * block, block)
        new_tops, new_sums = [], []
        for h in range(heads):
            rows = pl.ds(h * HEAD_DIM, HEAD_DIM)
            scores = all_scores[h * block : (h + 1) * block, :] + bias
            top = jnp.maximum(tops[h], jnp.max(scores, axis=0, keepdims=True))
            weights = jnp.exp(scores - top)
            keep = jnp.exp(tops[h] - top)
            new_tops.append(top)
            new_sums.append(sums[h] * keep + jnp.sum(weights, axis=0, keepdims=True))
            acc[rows, :] = acc[rows, :] * keep + jnp.dot(
                v_t[rows, pl.ds(first, block)],
                weights.astype(jnp.bfloat16),
                preferred_element_type=jnp.float32,
            )
        return tuple(new_tops), tuple(new_sums)

    empty = tuple(jnp.full((1, block), NEGATIVE, jnp.float32) for _ in range(heads))
    nothing = tuple(jnp.zeros((1, block), jnp.float32) for _ in range(heads))
    tops, sums = lax.fori_loop(lows[i], i + 1, step, (empty, nothing))
    for h in range(heads):
        rows = pl.ds(h * HEAD_DIM, HEAD_DIM)
        acc[rows, :] = acc[rows, :] / sums[h]
        lse[h : h + 1, :] = tops[h] + jnp.log(sums[h])
    context[...] = acc[...].astype(jnp.bfloat16).T


def attend_forward(line, lows, starts, mixed, block):
    length, triple = mixed.shape
    local_width = triple // 3
    blocks = length // block
    stack = (blocks, local_width // HEAD_DIM * block, local_width)
    column = lambda i, lows: (0, i)
    return line.call(
        forward_kernel,
        "attend_forward",
        (blocks,),
        [lows, starts, mixed, mixed, mixed],
        [
            pl.BlockSpec((8, block), column),
            pl.BlockSpec((block, local_width), row),
            pl.BlockSpec((length, local_width), lambda i, lows: (0, 1)),
            pl.BlockSpec((length, local_width), lambda i, lows: (0, 2)),
        ],
        [
            ((length, local_width), jnp.bfloat16, pl.BlockSpec((block, local_width), row)),
            ((8, length), jnp.float32, pl.BlockSpec((8, block), column)),
        ],
        scalars=1,
        scratch=[
            pltpu.VMEM((local_width, length), jnp.bfloat16),
            pltpu.VMEM(stack, jnp.bfloat16),
            pltpu.VMEM((local_width, block), jnp.float32),
        ],
    )


def backward_kernel(
    lows, starts, lse, q, k, v, context, grad, cosine, sine, turned_tables, grad_mixed, k_t, k_heads, v_heads, grad_q, grad_k, grad_v
):
    block, width = q.shape
    heads = width // HEAD_DIM
    length = k.shape[0]
    i = pl.program_id(0)
    blocks = length // block

    @pl.when(i == 0)
    def _():
        grad_k[...] = jnp.zeros_like(grad_k)
        grad_v[...] = jnp.zeros_like(grad_v)
        stack_heads(k, k_heads, block)
        stack_heads(v, v_heads, block)
        for j in range(blocks):
            rows = pl.ds(j * block, block)
            k_t[:, rows] = k[rows, :].T

    row_heads = lane_heads(block, width)
    scaled = q[...] * 0.125
    grads = grad[...]
    masked_q = [jnp.where(row_heads == h, scaled, 0).astype(jnp.bfloat16) for h in range(heads)]
    masked_g = [jnp.where(row_heads == h, grads, 0).astype(jnp.bfloat16) for h in range(heads)]
    turned_q = scaled.T
    turned_g = grads.T
    products = grads.astype(jnp.float32) * context[...].astype(jnp.float32)
    high = products.astype(jnp.bfloat16)
    low = (products - high.astype(jnp.float32)).astype(jnp.bfloat16)
    chooser = lax.broadcasted_iota(jnp.int32, (8, width), 0) == lane_heads(8, width)
    chooser = jnp.where(chooser, 1.0, 0.0).astype(jnp.bfloat16)
    sums = lax.dot_general(chooser, high, NT, preferred_element_type=jnp.float32)
    sums = sums + lax.dot_general(chooser, low, NT, preferred_element_type=jnp.float32)
    inner = [sums[h : h + 1, :] for h in range(heads)]
    grad_q[...] = jnp.zeros_like(grad_q)

    def step(j, carry):
        first = pl.multiple_of(j * block, block)
        here = pl.ds(first, block)
        all_scores = jnp.dot(k_heads[j], turned_q, preferred_element_type=jnp.float32)
        all_grads = jnp.dot(v_heads[j], turned_g, preferred_element_type=jnp.float32)
        bias = mask_bias(starts[0:1, :], first, i * block, block)
        probs, slopes = [], []
        for h in range(heads):
            rows = pl.ds(h * HEAD_DIM, HEAD_DIM)
            part = slice(h * block, (h + 1) * block)
            scores = all_scores[part, :]
            soft = jnp.exp(scores + bias - lse[h : h + 1, :])
            grad_probs = all_grads[part, :]
            slope = (soft * (grad_probs - inner[h])).astype(jnp.bfloat16)
            grad_q[rows, :] += jnp.dot(k_t[rows, here], slope, preferred_element_type=jnp.float32)
            probs.append(soft.astype(jnp.bfloat16))
            slopes.append(slope)
        grad_v[here, :] += jnp.dot(
            jnp.concatenate(probs, axis=1),
            jnp.concatenate(masked_g, axis=0),
            preferred_element_type=jnp.float32,
        )
        grad_k[here, :] += jnp.dot(
            jnp.concatenate(slopes, axis=1),
            jnp.concatenate(masked_q, axis=0),
            preferred_element_type=jnp.float32,
        )
        return carry

    lax.fori_loop(lows[i], i + 1, step, 0)

    def unrotate(x, rows):
        parts = []
        for part in range(width // 128):
            piece = x[:, part * 128 : (part + 1) * 128]
            parts.append(piece * cosine[rows, :] - swap_pairs(piece) * sine[rows, :])
        return jnp.concatenate(parts, axis=1).astype(jnp.bfloat16)

    mine = pl.ds(pl.multiple_of(i * block, block), block)
    cos_t, sin_t = turned_tables[0 : ROT // 2, :], turned_tables[ROT // 2 : ROT, :]
    for h in range(heads):
        top = pl.ds(h * HEAD_DIM, ROT // 2)
        bottom = pl.ds(h * HEAD_DIM + ROT // 2, ROT // 2)
        one, two = grad_q[top, :], grad_q[bottom, :]
        grad_q[top, :] = one * cos_t + two * sin_t
        grad_q[bottom, :] = two * cos_t - one * sin_t
    grad_mixed[mine, 0:width] = (grad_q[...] * 0.125).astype(jnp.bfloat16).T

    @pl.when(i == blocks - 1)
    def _():
        def finish(j, carry):
            rows = pl.ds(pl.multiple_of(j * block, block), block)
            grad_mixed[rows, width : 2 * width] = unrotate(grad_k[rows, :], rows)
            grad_mixed[rows, 2 * width : 3 * width] = grad_v[rows, :].astype(jnp.bfloat16)
            return carry

        lax.fori_loop(0, blocks, finish, 0)


def attend_backward(line, lows, starts, lse, mixed, context, grad_context, cosine, sine, turned, block):
    length, triple = mixed.shape
    local_width = triple // 3
    blocks = length // block
    stack = (blocks, local_width // HEAD_DIM * block, local_width)
    column = lambda i, lows: (0, i)
    return line.call(
        backward_kernel,
        "attend_backward",
        (blocks,),
        [lows, starts, lse, mixed, mixed, mixed, context, grad_context, cosine, sine, turned],
        [
            pl.BlockSpec((8, block), column),
            pl.BlockSpec((8, block), column),
            pl.BlockSpec((block, local_width), row),
            pl.BlockSpec((length, local_width), lambda i, lows: (0, 1)),
            pl.BlockSpec((length, local_width), lambda i, lows: (0, 2)),
            pl.BlockSpec((block, local_width), row),
            pl.BlockSpec((block, local_width), row),
            pl.BlockSpec((length, 128), whole),
            pl.BlockSpec((length, 128), whole),
            pl.BlockSpec((ROT, block), column),
        ],
        [((length, triple), jnp.bfloat16, pl.BlockSpec((length, triple), whole))],
        scalars=1,
        scratch=[
            pltpu.VMEM((local_width, length), jnp.bfloat16),
            pltpu.VMEM(stack, jnp.bfloat16),
            pltpu.VMEM(stack, jnp.bfloat16),
            pltpu.VMEM((local_width, block), jnp.float32),
            pltpu.VMEM((length, local_width), jnp.float32),
            pltpu.VMEM((length, local_width), jnp.float32),
        ],
        cost=632 * 10**8,
    )[0]


def positions_of(segments):
    ids = jnp.arange(8, dtype=jnp.int32)
    counts = jnp.sum((segments[None, :] < ids[:, None]).astype(jnp.int32), axis=1)
    return jnp.sum(jnp.where(segments[None, :] == ids[:, None], counts[:, None], 0), axis=0)


def rotary_tables(positions):
    lane = jnp.arange(128, dtype=jnp.int32) % HEAD_DIM
    step = (lane % (ROT // 2)).astype(jnp.float32)
    inverse = jnp.exp(step * (-2.0 * math.log(10000.0) / ROT))
    angles = positions.astype(jnp.float32)[:, None] * inverse[None, :]
    rotated = (lane < ROT)[None, :]
    cosine = jnp.where(rotated, jnp.cos(angles), 1.0)
    sine = jnp.where(rotated, jnp.where((lane < ROT // 2)[None, :], -1.0, 1.0) * jnp.sin(angles), 0.0)
    turned = jnp.concatenate([cosine[:, : ROT // 2], sine[:, ROT // 2 : ROT]], axis=1).T
    return cosine, sine, turned


def gelu_pair(u):
    scale = math.sqrt(2.0 / math.pi)
    square = u * u
    bent = jnp.tanh(scale * u * (1.0 + 0.044715 * square))
    half = 0.5 * (1.0 + bent)
    slope = half + 0.5 * u * (1.0 - bent * bent) * (scale * (1.0 + 3 * 0.044715 * square))
    return u * half, slope


def project_kernel(place, mine, other, gain, shift, w_qkv, b_qkv, w_up, b_up, cosine, sine, *refs):
    normed, unit, mixed, activated, slope = refs[-5:]
    n = pl.program_id(0)
    block = mine.shape[0]
    width = w_qkv.shape[2]
    strip = min(128, block)
    strips = [pl.ds(r * strip, strip) for r in range(2 * block // strip)]

    @pl.when(n == 0)
    def _():
        for source, first in ((mine, place[1] * block), (other, (1 - place[1]) * block)):
            for r in range(block // strip):
                wide = source[pl.ds(r * strip, strip), :].astype(jnp.float32)
                centred = wide - jnp.mean(wide, axis=1, keepdims=True)
                inverse_std = lax.rsqrt(
                    jnp.mean(centred * centred, axis=1, keepdims=True) + EPSILON
                )
                rows = pl.ds(pl.multiple_of(first + r * strip, strip), strip)
                even = centred * inverse_std
                unit[rows, :] = even.astype(jnp.bfloat16)
                normed[rows, :] = (even * gain[...] + shift[...]).astype(jnp.bfloat16)
        for rows in strips:
            for j in range(3):
                columns = slice(j * width, (j + 1) * width)
                y = jnp.dot(normed[rows, :], w_qkv[j], preferred_element_type=jnp.float32)
                y = y + b_qkv[:, columns]
                if j < 2:
                    parts = []
                    for part in range(width // 128):
                        piece = y[:, part * 128 : (part + 1) * 128]
                        parts.append(piece * cosine[rows, :] + swap_pairs(piece) * sine[rows, :])
                    y = jnp.concatenate(parts, axis=1)
                mixed[rows, columns] = y.astype(jnp.bfloat16)

    @pl.when(n > 0)
    def _():
        for rows in strips:
            u = jnp.dot(normed[rows, :], w_up[...], preferred_element_type=jnp.float32) + b_up[...]
            high, tilt = gelu_pair(u)
            activated[rows, :] = high.astype(jnp.bfloat16)
            slope[rows, :] = tilt.astype(jnp.bfloat16)


def project(line, place, mine, other, weights, tables, length, carried, cost=0):
    gain, shift, w_qkv, b_qkv, w_up, b_up = weights
    block, width = mine.shape
    local_width = w_qkv.shape[2]
    hidden = w_up.shape[1]
    tile = min(512, hidden)
    up = lambda n, place: (0, jnp.maximum(n - 1, 0))
    here = lambda n, place: (place[0], 0)
    up_here = lambda n, place: (place[0], jnp.maximum(n - 1, 0))
    operands = [place, mine, other, gain, shift, w_qkv, b_qkv, w_up, b_up, *tables, *carried]
    return line.call(
        project_kernel,
        "project",
        (1 + hidden // tile,),
        operands,
        [
            pl.BlockSpec((block, width), whole),
            pl.BlockSpec((block, width), whole),
            pl.BlockSpec((1, width), whole),
            pl.BlockSpec((1, width), whole),
            pl.BlockSpec((3, width, local_width), lambda n, place: (0, 0, 0)),
            pl.BlockSpec((1, 3 * local_width), whole),
            pl.BlockSpec((width, tile), up),
            pl.BlockSpec((1, tile), up),
            pl.BlockSpec((2 * block, 128), here),
            pl.BlockSpec((2 * block, 128), here),
            *[pl.BlockSpec(memory_space=pl.ANY)] * len(carried),
        ],
        [
            ((length, columns), jnp.bfloat16, pl.BlockSpec((2 * block, wide), index))
            for columns, wide, index in (
                (width, width, here),
                (width, width, here),
                (3 * local_width, 3 * local_width, here),
                (hidden, tile, up_here),
                (hidden, tile, up_here),
            )
        ],
        scalars=1,
        aliases={len(operands) - 5 + i: i for i in range(len(carried))},
        cost=cost,
    )


def backward_products_kernel(layout, *refs):
    grads = refs[:layout]
    w_down, w_out, slope, grad_up, grad_context, total = refs[layout:]
    columns = grads[0].shape[1]
    up, context = 0.0, 0.0
    for c in range(layout):
        part = slice(c * columns, (c + 1) * columns)
        piece = grads[c][...]
        up = up + lax.dot_general(piece, w_down[:, part], NT, preferred_element_type=jnp.float32)
        context = context + lax.dot_general(
            piece, w_out[:, part], NT, preferred_element_type=jnp.float32
        )
    low = (up * slope[...].astype(jnp.float32)).astype(jnp.bfloat16)
    grad_up[...] = low
    grad_context[...] = context.astype(jnp.bfloat16)

    @pl.when(pl.program_id(0) == 0)
    def _():
        total[...] = jnp.zeros_like(total)

    total[...] += jnp.sum(low.astype(jnp.float32), axis=0, keepdims=True)


def backward_products(line, grads, w_down, w_out, slope):
    length, columns = grads[0].shape
    hidden, width = w_down.shape
    local_width = w_out.shape[0]
    tile = min(256, length)
    return line.call(
        partial(backward_products_kernel, len(grads)),
        "backward_products",
        (length // tile,),
        [*grads, w_down, w_out, slope],
        [pl.BlockSpec((tile, columns), row) for _ in grads]
        + [
            pl.BlockSpec((hidden, width), whole),
            pl.BlockSpec((local_width, width), whole),
            pl.BlockSpec((tile, hidden), row),
        ],
        [
            ((length, hidden), jnp.bfloat16, pl.BlockSpec((tile, hidden), row)),
            ((length, local_width), jnp.bfloat16, pl.BlockSpec((tile, local_width), row)),
            ((1, hidden), jnp.float32, pl.BlockSpec((1, hidden), whole)),
        ],
    )


def branch_kernel(context, activated, w_out, w_down, out):
    total = jnp.dot(context[...], w_out[...], preferred_element_type=jnp.float32)
    total = total + jnp.dot(activated[...], w_down[...], preferred_element_type=jnp.float32)
    out[...] = total.astype(jnp.bfloat16)


def branch_sum(line, context, activated, w_out, w_down):
    length, local_width = context.shape
    hidden, width = w_down.shape
    tile = min(256, length)
    return line.call(
        branch_kernel,
        "branch_sum",
        (length // tile,),
        [context, activated, w_out, w_down],
        [
            pl.BlockSpec((tile, local_width), row),
            pl.BlockSpec((tile, hidden), row),
            pl.BlockSpec((local_width, width), whole),
            pl.BlockSpec((hidden, width), whole),
        ],
        [((length, width), jnp.bfloat16, pl.BlockSpec((tile, width), row))],
    )[0]


def normed_kernel(mixed, up, unit, w_qkv, w_up, out, gain, shift):
    width = w_qkv.shape[2]
    total = lax.dot_general(up[...], w_up[...], NT, preferred_element_type=jnp.float32)
    for j in range(3):
        total = total + lax.dot_general(
            mixed[:, j * width : (j + 1) * width],
            w_qkv[j],
            NT,
            preferred_element_type=jnp.float32,
        )
    out[...] = total.astype(jnp.bfloat16)

    @pl.when(pl.program_id(0) == 0)
    def _():
        gain[...] = jnp.zeros_like(gain)
        shift[...] = jnp.zeros_like(shift)

    gain[...] += jnp.sum(total * unit[...].astype(jnp.float32), axis=0, keepdims=True)
    shift[...] += jnp.sum(total, axis=0, keepdims=True)


def normed_sum(line, grad_mixed, grad_up, unit, w_qkv, w_up):
    length, triple = grad_mixed.shape
    width, hidden = w_up.shape
    tile = min(256, length)
    return line.call(
        normed_kernel,
        "normed_sum",
        (length // tile,),
        [grad_mixed, grad_up, unit, w_qkv, w_up],
        [
            pl.BlockSpec((tile, triple), row),
            pl.BlockSpec((tile, hidden), row),
            pl.BlockSpec((tile, width), row),
            pl.BlockSpec(w_qkv.shape, lambda i: (0, 0, 0)),
            pl.BlockSpec((width, hidden), whole),
        ],
        [
            ((length, width), jnp.bfloat16, pl.BlockSpec((tile, width), row)),
            ((1, width), jnp.float32, pl.BlockSpec((1, width), whole)),
            ((1, width), jnp.float32, pl.BlockSpec((1, width), whole)),
        ],
    )


def norm_back_kernel(grad_normed, x, grad, gain, out):
    wide = x[...].astype(jnp.float32)
    centred = wide - jnp.mean(wide, axis=1, keepdims=True)
    inverse_std = lax.rsqrt(jnp.mean(centred * centred, axis=1, keepdims=True) + EPSILON)
    unit = centred * inverse_std
    slope = grad_normed[...].astype(jnp.float32) * gain[...]
    inner = jnp.mean(slope * unit, axis=1, keepdims=True)
    slope = slope - jnp.mean(slope, axis=1, keepdims=True) - unit * inner
    out[...] = (grad[...].astype(jnp.float32) + inverse_std * slope).astype(jnp.bfloat16)


def norm_back(line, grad_normed, x, grad, gain):
    block, width = x.shape
    tile = min(128, block)
    spec = pl.BlockSpec((tile, width), row)
    return line.call(
        norm_back_kernel,
        "norm_back",
        (block // tile,),
        [grad_normed, x, grad, gain],
        [spec, spec, spec, pl.BlockSpec((1, width), whole)],
        [((block, width), jnp.bfloat16, spec)],
    )[0]


def finish_kernel(layout, order, *refs):
    s = pl.program_id(0)
    outs = refs[-1:] if isinstance(layout, int) else refs[-len(layout) :]
    for index, source in enumerate(refs[:4]):

        @pl.when(s == index)
        def _(source=source):
            if isinstance(layout, int):
                group = outs[0].shape[2]
                for j in range(layout):
                    columns = slice(j * group, (j + 1) * group)
                    outs[0][j] = source[:, columns].astype(jnp.float32)
            else:
                start = 0
                columns = source.shape[1]
                for out in outs:
                    rows, spread = out.shape
                    for j in range(spread // columns):
                        out[:, j * columns : (j + 1) * columns] = source[
                            start : start + rows, :
                        ].astype(jnp.float32)
                        start += rows


def finish(line, order, pieces, layout, carried=(), cost=0):
    rows, columns = pieces[0].shape
    in_specs = [pl.BlockSpec(pieces[0].shape, whole) for _ in range(4)]
    in_specs += [pl.BlockSpec(memory_space=pl.ANY)] * len(carried)
    if isinstance(layout, int):
        group = columns // layout
        spec = pl.BlockSpec((layout, rows, group), lambda s, order: (0, order[s], 0))
        outs = [((layout, 4 * rows, group), jnp.float32, spec)]
    else:
        outs = [
            (
                (4 * tall, spread),
                jnp.float32,
                pl.BlockSpec((tall, wide), lambda s, order, place=place: (order[s], place)),
            )
            for tall, wide, spread, place in layout
        ]
    return line.call(
        partial(finish_kernel, layout),
        "finish",
        (4,),
        [order, *pieces, *carried],
        in_specs,
        outs,
        scalars=1,
        aliases={5 + i: i for i in range(len(carried))},
        cost=cost,
    )


def add_low(one, other):
    return (one.astype(jnp.float32) + other.astype(jnp.float32)).astype(jnp.bfloat16)


def swap_rows(array, bit):
    return lax.ppermute(array, "rows", [(i, i ^ bit) for i in range(4)])


def outer_kernel(extra, order, left, right, *refs):
    s = pl.program_id(0)
    dims = (((0,), (0,)), ((), ()))
    low = lax.dot_general(left[...], right[...], dims, preferred_element_type=jnp.float32)
    parts = [low.astype(jnp.bfloat16)]
    outs = refs[extra : 4 + extra]
    if extra:
        second, held = refs[0], refs[-1]

        @pl.when(s == 0)
        def _():
            held[...] = lax.dot_general(
                second[...], right[...], dims, preferred_element_type=jnp.float32
            ).astype(jnp.bfloat16)

        rows = held.shape[0] // 4
        parts.append(held[pl.ds(pl.multiple_of(order[s] * rows, rows), rows), :])
    for index, out in enumerate(outs):

        @pl.when(s == index)
        def _(out=out):
            start = 0
            for part in parts:
                out[start : start + part.shape[0], :] = part
                start += part.shape[0]


def outer_parts(line, order, left, right, second=None):
    length, tall = left.shape
    columns = right.shape[1]
    extra = [] if second is None else [second]
    rows = (tall + sum(array.shape[1] for array in extra)) // 4
    return line.call(
        partial(outer_kernel, len(extra)),
        "outer_parts",
        (4,),
        [order, left, right, *extra],
        [
            pl.BlockSpec((length, tall // 4), lambda s, order: (0, order[s])),
            *(pl.BlockSpec(array.shape, whole) for array in (right, *extra)),
        ],
        [((rows, columns), jnp.bfloat16, pl.BlockSpec((rows, columns), whole)) for _ in range(4)],
        scalars=1,
        scratch=[pltpu.VMEM((array.shape[1], columns), jnp.bfloat16) for array in extra],
    )


class RowsSum:
    def __init__(self, rows, line, left, right, second=None, between=None):
        self.rows, self.line, self.phase = rows, line, 0
        if rows != 4:
            self.order = jnp.arange(4, dtype=jnp.int32)
            self.pieces = lax.psum(outer_parts(line, self.order, left, right, second), "rows")
            return
        place = lax.axis_index("rows")
        x, y = place % 2, place // 2
        away = jnp.stack([1 - x, 3 - y, x, 2 + y]).astype(jnp.int32)
        self.order = jnp.stack([x, 1 - x, 2 + y, 3 - y]).astype(jnp.int32)
        self.bits = ((1, 2), (2, 1))
        *away, keep_a, keep_b = outer_parts(line, away, left, right, second)
        self.keep = [keep_a, keep_b]
        if between is not None:
            between()
        self.send(0, away)

    def send(self, which, arrays):
        arrays = self.line.join(*arrays)
        self.came = [swap_rows(a, bits[which]) for a, bits in zip(arrays, self.bits)]
        return arrays

    def advance(self):
        if self.rows != 4:
            return
        self.phase += 1
        came = self.line.join(*self.came)
        if self.phase < 3:
            self.keep = [add_low(k, c) for k, c in zip(self.keep, came)]
            self.keep = self.send(2 - self.phase, self.keep)
        else:
            self.pieces = [self.keep[0], came[0], self.keep[1], came[1]]

    def finish(self, *layout, **more):
        if self.phase < 3:
            self.advance()
        return finish(self.line, self.order, self.pieces, *layout, **more)


class SmallSum:
    def __init__(self, line, array, more, rows, tp):
        self.line, self.array, self.more = line, array, more
        self.steps = [("tp", 1 << i, tp) for i in range(tp.bit_length() - 1)]
        self.steps += [("rows", 1 << i, rows) for i in range(rows.bit_length() - 1)]
        self.send()

    def send(self):
        if self.steps:
            axis, step, size = self.steps.pop(0)
            if axis == "rows" and self.more is not None:
                self.array, self.more = jnp.concatenate([self.array, self.more]), None
            (self.array,) = self.line.join(self.array)
            self.came = lax.ppermute(self.array, axis, [(i, i ^ step) for i in range(size)])
        else:
            self.came = None

    def step(self):
        if self.came is not None:
            (came,) = self.line.join(self.came)
            self.array = self.array + came
            self.send()

    def rest(self):
        while self.came is not None:
            self.step()
        return self.array


class SmallGather:
    def __init__(self, line, array, me, tp):
        self.line, self.me, self.step = line, me, 1
        while 2 * self.step < tp:
            other = lax.ppermute(array, "tp", [(i, i ^ self.step) for i in range(tp)])
            array = self.laid(array, other)
            self.step *= 2
        (self.array,) = line.join(array)
        self.other = lax.ppermute(self.array, "tp", [(i, i ^ self.step) for i in range(tp)])

    def laid(self, array, other):
        return jnp.where(
            (self.me // self.step) % 2 == 0,
            jnp.concatenate([array, other]),
            jnp.concatenate([other, array]),
        )

    def whole(self):
        return self.line.join(self.laid(self.array, *self.line.join(self.other)))[0]


def token_sum(matrix):
    ones_row = jnp.ones((1, matrix.shape[0]), matrix.dtype)
    return jnp.dot(ones_row, matrix, preferred_element_type=jnp.float32)[0]


def local(
    rows,
    tp,
    hidden_in,
    segment_ids,
    ln_gain,
    ln_bias,
    w_qkv,
    b_qkv,
    w_out,
    out_bias,
    w_up,
    b_up,
    w_down,
    cotangent,
):
    x = hidden_in[0]
    block, width = x.shape
    length = block * tp
    local_width = w_qkv.shape[2]
    hidden = w_up.shape[1]
    chips = tp // 2
    me = lax.axis_index("tp")
    chip, core = me // 2, me % 2
    line = Line()

    around = [(i, (i + 2) % tp) for i in range(tp)]
    sibling = [(i, i ^ 1) for i in range(tp)]
    mine, others = [x], [lax.ppermute(x, "tp", sibling)]
    coming = lax.ppermute(x, "tp", around)
    ids = SmallGather(line, segment_ids[0], me, tp)

    def serve():
        nonlocal coming
        (arrived,) = line.join(coming)
        mine.append(arrived)
        if len(mine) < chips:
            coming = lax.ppermute(arrived, "tp", around)
        others.append(lax.ppermute(arrived, "tp", sibling))
    columns = width // 2
    serve()
    segments = ids.whole()
    starts = positions_of(segments)
    tables = rotary_tables(jnp.arange(length, dtype=jnp.int32) - starts)
    lows = starts[::block] // block
    starts = jnp.broadcast_to(starts[None], (8, length))
    w_three = jnp.transpose(w_qkv, (1, 0, 2))
    weights = (
        ln_gain.reshape(1, width),
        ln_bias.reshape(1, width),
        w_three,
        b_qkv.reshape(1, 3 * local_width),
        w_up,
        b_up.reshape(1, hidden),
    )
    carried = ()

    def project_slot(s, cost=0):
        place = jnp.stack([(chip - s + chips) % chips, core]).astype(jnp.int32)
        pair = line.join(mine[s], others[s])
        return project(line, place, *pair, weights, tables[:2], length, carried, cost)

    carried = project_slot(0)
    for s in range(1, chips):
        if s > 1:
            serve()
        if s != 1 or chips == 2:
            for t in (1, 2) if s == 2 else (s,):
                carried = project_slot(t, cost=920 * 10**8)
                if t == max(chips - 3, 1):
                    halves = line.join(cotangent[0, :, :columns], cotangent[0, :, columns:])
                    grads = [lax.all_gather(half, "tp", axis=0, tiled=True) for half in halves]
    normed, unit, mixed, activated, slope = carried

    hidden_parts, local_parts = hidden // 4, local_width // 4
    sums = partial(RowsSum, rows, line)
    context, lse = attend_forward(line, lows, starts, mixed, block)
    d0 = sums(activated, grads[0], context)
    branch = branch_sum(line, context, activated, w_out, w_down)
    d0.advance()
    (branch,) = line.join(branch)
    branch_total = lax.psum_scatter(branch, "tp", scatter_dimension=0, tiled=True)
    d1 = sums(activated, grads[1], context)
    d0.advance()
    grad_up, grad_context, grad_b_up = backward_products(line, grads, w_down, w_out, slope)
    d1.advance()
    up = sums(normed, grad_up, between=d0.advance)
    grad_mixed = attend_backward(
        line, lows, starts, lse, mixed, context, grad_context, *tables, block
    )
    d1.advance()
    up.advance()
    (branch_total,) = line.join(branch_total)
    part, gain_part, shift_part = normed_sum(line, grad_mixed, grad_up, unit, w_three, w_up)
    grad_normed = lax.psum_scatter(part, "tp", scatter_dimension=0, tiled=True)
    up.advance()
    three = sums(normed, grad_mixed, between=d1.advance)
    small = SmallSum(
        line,
        jnp.concatenate([gain_part, shift_part, token_sum(cotangent[0])[None]], axis=1)[0],
        jnp.concatenate([token_sum(grad_mixed), grad_b_up[0]]),
        rows,
        tp,
    )
    down = d0.finish([(hidden_parts, columns, width, 0), (local_parts, columns, width, 0)])
    small.step()
    down = d1.finish(
        [(hidden_parts, columns, width, 1), (local_parts, columns, width, 1)], carried=down
    )
    up.advance()
    three.advance()
    small.step()
    up = up.finish([(width // 4, hidden, hidden, 0)], cost=1092 * 10**8)
    three.advance()
    small.step()
    small.step()
    three = three.finish(3, cost=287 * 10**8)
    small = small.rest()
    grad_w_down, grad_w_out = down
    grad_w_up = up[0]
    grad_w_qkv = jnp.transpose(three[0], (1, 0, 2))

    inputs = x.astype(jnp.float32)
    hidden_out = (inputs + branch_total.astype(jnp.float32) + out_bias).astype(jnp.bfloat16)
    grad_input = norm_back(line, grad_normed, x, cotangent[0], ln_gain.reshape(1, width))
    tail = small[: 3 * width].reshape(3, width)
    grad_b_qkv = small[3 * width : 3 * (width + local_width)].reshape(3, local_width)
    grad_b_up = small[3 * (width + local_width) :]
    return (
        hidden_out[None],
        grad_input[None],
        tail[0],
        tail[1],
        grad_w_qkv,
        grad_b_qkv,
        grad_w_out,
        tail[2],
        grad_w_up,
        grad_b_up,
        grad_w_down,
    )


def solution(mesh):
    in_specs = (
        P("rows", "tp", None),
        P("rows", "tp"),
        P(),
        P(),
        P(None, None, "tp"),
        P(None, "tp"),
        P("tp", None),
        P(),
        P(None, "tp"),
        P("tp"),
        P("tp", None),
        P("rows", "tp", None),
    )
    out_specs = (
        P("rows", "tp", None),
        P("rows", "tp", None),
        P(),
        P(),
        P(None, None, "tp"),
        P(None, "tp"),
        P("tp", None),
        P(),
        P(None, "tp"),
        P("tp"),
        P("tp", None),
    )
    return jax.shard_map(
        partial(local, mesh.shape["rows"], mesh.shape["tp"]),
        mesh=mesh,
        in_specs=in_specs,
        out_specs=out_specs,
        check_vma=False,
    )
```

```python
from functools import partial
import math

import jax
import jax.numpy as jnp
from jax import lax
from jax.experimental import pallas as pl
from jax.experimental.pallas import tpu as pltpu
from jax.sharding import PartitionSpec as P

HEAD_DIM = 64
ROT = 32
EPSILON = 1e-05
NEGATIVE = -1e30
VMEM_BYTES = 56 * 2**20
NT = (((1,), (1,)), ((), ()))


class Line:
    def __init__(self):
        self.token = jnp.zeros((8, 128), jnp.float32)

    def join(self, *arrays):
        *arrays, self.token = lax.optimization_barrier((*arrays, self.token))
        return arrays

    def call(
        self, body, name, grid, operands, in_specs, outs, scalars=0, scratch=(), aliases=None, cost=0
    ):
        inputs = len(operands)

        def whole_body(*refs):
            refs = list(refs)
            token = refs.pop(inputs + 1 + len(outs))
            refs.pop(inputs)
            token[...] = jnp.zeros_like(token)
            body(*refs)

        *results, self.token = pl.pallas_call(
            whole_body,
            grid_spec=pltpu.PrefetchScalarGridSpec(
                num_scalar_prefetch=scalars,
                grid=grid,
                in_specs=[*in_specs, pl.BlockSpec(memory_space=pl.ANY)],
                out_specs=[
                    *(spec for _, _, spec in outs),
                    pl.BlockSpec((8, 128), lambda *index: (0, 0)),
                ],
                scratch_shapes=list(scratch),
            ),
            out_shape=[
                *(jax.ShapeDtypeStruct(shape, dtype) for shape, dtype, _ in outs),
                jax.ShapeDtypeStruct((8, 128), jnp.float32),
            ],
            input_output_aliases=aliases or {},
            compiler_params=pltpu.CompilerParams(vmem_limit_bytes=VMEM_BYTES),
            cost_estimate=pl.CostEstimate(
                flops=2**20 + cost, bytes_accessed=2**16, transcendentals=0
            ),
            name=name,
        )(*operands, self.token)
        return results


def whole(*index):
    return (0, 0)


def row(i, *scalars):
    return (i, 0)


def lane_heads(rows, width):
    return lax.broadcasted_iota(jnp.int32, (rows, width), 1) // HEAD_DIM


def swap_pairs(x):
    width = x.shape[1]
    lane = lax.broadcasted_iota(jnp.int32, x.shape, 1) % HEAD_DIM
    up = pltpu.roll(x, width - ROT // 2, 1)
    down = pltpu.roll(x, ROT // 2, 1)
    return jnp.where(lane < ROT // 2, up, down)


def mask_bias(starts, key_first, query_first, block):
    key_index = key_first + lax.broadcasted_iota(jnp.int32, (block, block), 0)
    query_index = query_first + lax.broadcasted_iota(jnp.int32, (block, block), 1)
    allowed = (key_index >= starts) & (key_index <= query_index)
    return jnp.where(allowed, 0.0, NEGATIVE).astype(jnp.float32)


def stack_heads(source, stacked, block):
    length, width = source.shape
    row_heads = lane_heads(block, width)
    for j in range(length // block):
        rows = pl.ds(j * block, block)
        piece = source[rows, :]
        for h in range(width // HEAD_DIM):
            stacked[j, pl.ds(h * block, block), :] = jnp.where(row_heads == h, piece, 0).astype(
                jnp.bfloat16
            )


def forward_kernel(lows, starts, q, k, v, context, lse, v_t, k_heads, acc):
    block, width = q.shape
    heads = width // HEAD_DIM
    length = k.shape[0]
    i = pl.program_id(0)

    @pl.when(i == 0)
    def _():
        stack_heads(k, k_heads, block)
        for j in range(length // block):
            rows = pl.ds(j * block, block)
            v_t[:, rows] = v[rows, :].T

    turned = (q[...] * 0.125).T
    acc[...] = jnp.zeros_like(acc)

    def step(j, carry):
        tops, sums = carry
        first = pl.multiple_of(j * block, block)
        all_scores = jnp.dot(k_heads[j], turned, preferred_element_type=jnp.float32)
        bias = mask_bias(starts[0:1, :], first, i * block, block)
        new_tops, new_sums = [], []
        for h in range(heads):
            rows = pl.ds(h * HEAD_DIM, HEAD_DIM)
            scores = all_scores[h * block : (h + 1) * block, :] + bias
            top = jnp.maximum(tops[h], jnp.max(scores, axis=0, keepdims=True))
            weights = jnp.exp(scores - top)
            keep = jnp.exp(tops[h] - top)
            new_tops.append(top)
            new_sums.append(sums[h] * keep + jnp.sum(weights, axis=0, keepdims=True))
            acc[rows, :] = acc[rows, :] * keep + jnp.dot(
                v_t[rows, pl.ds(first, block)],
                weights.astype(jnp.bfloat16),
                preferred_element_type=jnp.float32,
            )
        return tuple(new_tops), tuple(new_sums)

    empty = tuple(jnp.full((1, block), NEGATIVE, jnp.float32) for _ in range(heads))
    nothing = tuple(jnp.zeros((1, block), jnp.float32) for _ in range(heads))
    tops, sums = lax.fori_loop(lows[i], i + 1, step, (empty, nothing))
    for h in range(heads):
        rows = pl.ds(h * HEAD_DIM, HEAD_DIM)
        acc[rows, :] = acc[rows, :] / sums[h]
        lse[h : h + 1, :] = tops[h] + jnp.log(sums[h])
    context[...] = acc[...].astype(jnp.bfloat16).T


def attend_forward(line, lows, starts, mixed, block):
    length, triple = mixed.shape
    local_width = triple // 3
    blocks = length // block
    stack = (blocks, local_width // HEAD_DIM * block, local_width)
    column = lambda i, lows: (0, i)
    return line.call(
        forward_kernel,
        "attend_forward",
        (blocks,),
        [lows, starts, mixed, mixed, mixed],
        [
            pl.BlockSpec((8, block), column),
            pl.BlockSpec((block, local_width), row),
            pl.BlockSpec((length, local_width), lambda i, lows: (0, 1)),
            pl.BlockSpec((length, local_width), lambda i, lows: (0, 2)),
        ],
        [
            ((length, local_width), jnp.bfloat16, pl.BlockSpec((block, local_width), row)),
            ((8, length), jnp.float32, pl.BlockSpec((8, block), column)),
        ],
        scalars=1,
        scratch=[
            pltpu.VMEM((local_width, length), jnp.bfloat16),
            pltpu.VMEM(stack, jnp.bfloat16),
            pltpu.VMEM((local_width, block), jnp.float32),
        ],
    )


def backward_kernel(
    lows, starts, lse, q, k, v, context, grad, cosine, sine, turned_tables, grad_mixed, k_t, k_heads, v_heads, grad_q, grad_k, grad_v
):
    block, width = q.shape
    heads = width // HEAD_DIM
    length = k.shape[0]
    i = pl.program_id(0)
    blocks = length // block

    @pl.when(i == 0)
    def _():
        grad_k[...] = jnp.zeros_like(grad_k)
        grad_v[...] = jnp.zeros_like(grad_v)
        stack_heads(k, k_heads, block)
        stack_heads(v, v_heads, block)
        for j in range(blocks):
            rows = pl.ds(j * block, block)
            k_t[:, rows] = k[rows, :].T

    row_heads = lane_heads(block, width)
    scaled = q[...] * 0.125
    grads = grad[...]
    masked_q = [jnp.where(row_heads == h, scaled, 0).astype(jnp.bfloat16) for h in range(heads)]
    masked_g = [jnp.where(row_heads == h, grads, 0).astype(jnp.bfloat16) for h in range(heads)]
    turned_q = scaled.T
    turned_g = grads.T
    products = grads.astype(jnp.float32) * context[...].astype(jnp.float32)
    high = products.astype(jnp.bfloat16)
    low = (products - high.astype(jnp.float32)).astype(jnp.bfloat16)
    chooser = lax.broadcasted_iota(jnp.int32, (8, width), 0) == lane_heads(8, width)
    chooser = jnp.where(chooser, 1.0, 0.0).astype(jnp.bfloat16)
    sums = lax.dot_general(chooser, high, NT, preferred_element_type=jnp.float32)
    sums = sums + lax.dot_general(chooser, low, NT, preferred_element_type=jnp.float32)
    inner = [sums[h : h + 1, :] for h in range(heads)]
    grad_q[...] = jnp.zeros_like(grad_q)

    def step(j, carry):
        first = pl.multiple_of(j * block, block)
        here = pl.ds(first, block)
        all_scores = jnp.dot(k_heads[j], turned_q, preferred_element_type=jnp.float32)
        all_grads = jnp.dot(v_heads[j], turned_g, preferred_element_type=jnp.float32)
        bias = mask_bias(starts[0:1, :], first, i * block, block)
        probs, slopes = [], []
        for h in range(heads):
            rows = pl.ds(h * HEAD_DIM, HEAD_DIM)
            part = slice(h * block, (h + 1) * block)
            scores = all_scores[part, :]
            soft = jnp.exp(scores + bias - lse[h : h + 1, :])
            grad_probs = all_grads[part, :]
            slope = (soft * (grad_probs - inner[h])).astype(jnp.bfloat16)
            grad_q[rows, :] += jnp.dot(k_t[rows, here], slope, preferred_element_type=jnp.float32)
            probs.append(soft.astype(jnp.bfloat16))
            slopes.append(slope)
        grad_v[here, :] += jnp.dot(
            jnp.concatenate(probs, axis=1),
            jnp.concatenate(masked_g, axis=0),
            preferred_element_type=jnp.float32,
        )
        grad_k[here, :] += jnp.dot(
            jnp.concatenate(slopes, axis=1),
            jnp.concatenate(masked_q, axis=0),
            preferred_element_type=jnp.float32,
        )
        return carry

    lax.fori_loop(lows[i], i + 1, step, 0)

    def unrotate(x, rows):
        parts = []
        for part in range(width // 128):
            piece = x[:, part * 128 : (part + 1) * 128]
            parts.append(piece * cosine[rows, :] - swap_pairs(piece) * sine[rows, :])
        return jnp.concatenate(parts, axis=1).astype(jnp.bfloat16)

    mine = pl.ds(pl.multiple_of(i * block, block), block)
    cos_t, sin_t = turned_tables[0 : ROT // 2, :], turned_tables[ROT // 2 : ROT, :]
    for h in range(heads):
        top = pl.ds(h * HEAD_DIM, ROT // 2)
        bottom = pl.ds(h * HEAD_DIM + ROT // 2, ROT // 2)
        one, two = grad_q[top, :], grad_q[bottom, :]
        grad_q[top, :] = one * cos_t + two * sin_t
        grad_q[bottom, :] = two * cos_t - one * sin_t
    grad_mixed[mine, 0:width] = (grad_q[...] * 0.125).astype(jnp.bfloat16).T

    @pl.when(i == blocks - 1)
    def _():
        def finish(j, carry):
            rows = pl.ds(pl.multiple_of(j * block, block), block)
            grad_mixed[rows, width : 2 * width] = unrotate(grad_k[rows, :], rows)
            grad_mixed[rows, 2 * width : 3 * width] = grad_v[rows, :].astype(jnp.bfloat16)
            return carry

        lax.fori_loop(0, blocks, finish, 0)


def attend_backward(line, lows, starts, lse, mixed, context, grad_context, cosine, sine, turned, block):
    length, triple = mixed.shape
    local_width = triple // 3
    blocks = length // block
    stack = (blocks, local_width // HEAD_DIM * block, local_width)
    column = lambda i, lows: (0, i)
    return line.call(
        backward_kernel,
        "attend_backward",
        (blocks,),
        [lows, starts, lse, mixed, mixed, mixed, context, grad_context, cosine, sine, turned],
        [
            pl.BlockSpec((8, block), column),
            pl.BlockSpec((8, block), column),
            pl.BlockSpec((block, local_width), row),
            pl.BlockSpec((length, local_width), lambda i, lows: (0, 1)),
            pl.BlockSpec((length, local_width), lambda i, lows: (0, 2)),
            pl.BlockSpec((block, local_width), row),
            pl.BlockSpec((block, local_width), row),
            pl.BlockSpec((length, 128), whole),
            pl.BlockSpec((length, 128), whole),
            pl.BlockSpec((ROT, block), column),
        ],
        [((length, triple), jnp.bfloat16, pl.BlockSpec((length, triple), whole))],
        scalars=1,
        scratch=[
            pltpu.VMEM((local_width, length), jnp.bfloat16),
            pltpu.VMEM(stack, jnp.bfloat16),
            pltpu.VMEM(stack, jnp.bfloat16),
            pltpu.VMEM((local_width, block), jnp.float32),
            pltpu.VMEM((length, local_width), jnp.float32),
            pltpu.VMEM((length, local_width), jnp.float32),
        ],
        cost=632 * 10**8,
    )[0]


def positions_of(segments):
    ids = jnp.arange(8, dtype=jnp.int32)
    counts = jnp.sum((segments[None, :] < ids[:, None]).astype(jnp.int32), axis=1)
    return jnp.sum(jnp.where(segments[None, :] == ids[:, None], counts[:, None], 0), axis=0)


def rotary_tables(positions):
    lane = jnp.arange(128, dtype=jnp.int32) % HEAD_DIM
    step = (lane % (ROT // 2)).astype(jnp.float32)
    inverse = jnp.exp(step * (-2.0 * math.log(10000.0) / ROT))
    angles = positions.astype(jnp.float32)[:, None] * inverse[None, :]
    rotated = (lane < ROT)[None, :]
    cosine = jnp.where(rotated, jnp.cos(angles), 1.0)
    sine = jnp.where(rotated, jnp.where((lane < ROT // 2)[None, :], -1.0, 1.0) * jnp.sin(angles), 0.0)
    turned = jnp.concatenate([cosine[:, : ROT // 2], sine[:, ROT // 2 : ROT]], axis=1).T
    return cosine, sine, turned


def gelu_pair(u):
    scale = math.sqrt(2.0 / math.pi)
    square = u * u
    bent = jnp.tanh(scale * u * (1.0 + 0.044715 * square))
    half = 0.5 * (1.0 + bent)
    slope = half + 0.5 * u * (1.0 - bent * bent) * (scale * (1.0 + 3 * 0.044715 * square))
    return u * half, slope


def project_kernel(place, mine, other, gain, shift, w_qkv, b_qkv, w_up, b_up, cosine, sine, *refs):
    normed, unit, mixed, activated, slope = refs[-5:]
    n = pl.program_id(0)
    block = mine.shape[0]
    width = w_qkv.shape[2]
    strip = min(128, block)
    strips = [pl.ds(r * strip, strip) for r in range(2 * block // strip)]

    @pl.when(n == 0)
    def _():
        for source, first in ((mine, place[1] * block), (other, (1 - place[1]) * block)):
            for r in range(block // strip):
                wide = source[pl.ds(r * strip, strip), :].astype(jnp.float32)
                centred = wide - jnp.mean(wide, axis=1, keepdims=True)
                inverse_std = lax.rsqrt(
                    jnp.mean(centred * centred, axis=1, keepdims=True) + EPSILON
                )
                rows = pl.ds(pl.multiple_of(first + r * strip, strip), strip)
                even = centred * inverse_std
                unit[rows, :] = even.astype(jnp.bfloat16)
                normed[rows, :] = (even * gain[...] + shift[...]).astype(jnp.bfloat16)
        for rows in strips:
            for j in range(3):
                columns = slice(j * width, (j + 1) * width)
                y = jnp.dot(normed[rows, :], w_qkv[j], preferred_element_type=jnp.float32)
                y = y + b_qkv[:, columns]
                if j < 2:
                    parts = []
                    for part in range(width // 128):
                        piece = y[:, part * 128 : (part + 1) * 128]
                        parts.append(piece * cosine[rows, :] + swap_pairs(piece) * sine[rows, :])
                    y = jnp.concatenate(parts, axis=1)
                mixed[rows, columns] = y.astype(jnp.bfloat16)

    @pl.when(n > 0)
    def _():
        for rows in strips:
            u = jnp.dot(normed[rows, :], w_up[...], preferred_element_type=jnp.float32) + b_up[...]
            high, tilt = gelu_pair(u)
            activated[rows, :] = high.astype(jnp.bfloat16)
            slope[rows, :] = tilt.astype(jnp.bfloat16)


def project(line, place, mine, other, weights, tables, length, carried, cost=0):
    gain, shift, w_qkv, b_qkv, w_up, b_up = weights
    block, width = mine.shape
    local_width = w_qkv.shape[2]
    hidden = w_up.shape[1]
    tile = min(512, hidden)
    up = lambda n, place: (0, jnp.maximum(n - 1, 0))
    here = lambda n, place: (place[0], 0)
    up_here = lambda n, place: (place[0], jnp.maximum(n - 1, 0))
    operands = [place, mine, other, gain, shift, w_qkv, b_qkv, w_up, b_up, *tables, *carried]
    return line.call(
        project_kernel,
        "project",
        (1 + hidden // tile,),
        operands,
        [
            pl.BlockSpec((block, width), whole),
            pl.BlockSpec((block, width), whole),
            pl.BlockSpec((1, width), whole),
            pl.BlockSpec((1, width), whole),
            pl.BlockSpec((3, width, local_width), lambda n, place: (0, 0, 0)),
            pl.BlockSpec((1, 3 * local_width), whole),
            pl.BlockSpec((width, tile), up),
            pl.BlockSpec((1, tile), up),
            pl.BlockSpec((2 * block, 128), here),
            pl.BlockSpec((2 * block, 128), here),
            *[pl.BlockSpec(memory_space=pl.ANY)] * len(carried),
        ],
        [
            ((length, columns), jnp.bfloat16, pl.BlockSpec((2 * block, wide), index))
            for columns, wide, index in (
                (width, width, here),
                (width, width, here),
                (3 * local_width, 3 * local_width, here),
                (hidden, tile, up_here),
                (hidden, tile, up_here),
            )
        ],
        scalars=1,
        aliases={len(operands) - 5 + i: i for i in range(len(carried))},
        cost=cost,
    )


def backward_products_kernel(layout, *refs):
    grads = refs[:layout]
    w_down, w_out, slope, grad_up, grad_context, total = refs[layout:]
    columns = grads[0].shape[1]
    up, context = 0.0, 0.0
    for c in range(layout):
        part = slice(c * columns, (c + 1) * columns)
        piece = grads[c][...]
        up = up + lax.dot_general(piece, w_down[:, part], NT, preferred_element_type=jnp.float32)
        context = context + lax.dot_general(
            piece, w_out[:, part], NT, preferred_element_type=jnp.float32
        )
    low = (up * slope[...].astype(jnp.float32)).astype(jnp.bfloat16)
    grad_up[...] = low
    grad_context[...] = context.astype(jnp.bfloat16)

    @pl.when(pl.program_id(0) == 0)
    def _():
        total[...] = jnp.zeros_like(total)

    total[...] += jnp.sum(low.astype(jnp.float32), axis=0, keepdims=True)


def backward_products(line, grads, w_down, w_out, slope):
    length, columns = grads[0].shape
    hidden, width = w_down.shape
    local_width = w_out.shape[0]
    tile = min(256, length)
    return line.call(
        partial(backward_products_kernel, len(grads)),
        "backward_products",
        (length // tile,),
        [*grads, w_down, w_out, slope],
        [pl.BlockSpec((tile, columns), row) for _ in grads]
        + [
            pl.BlockSpec((hidden, width), whole),
            pl.BlockSpec((local_width, width), whole),
            pl.BlockSpec((tile, hidden), row),
        ],
        [
            ((length, hidden), jnp.bfloat16, pl.BlockSpec((tile, hidden), row)),
            ((length, local_width), jnp.bfloat16, pl.BlockSpec((tile, local_width), row)),
            ((1, hidden), jnp.float32, pl.BlockSpec((1, hidden), whole)),
        ],
    )


def branch_kernel(context, activated, w_out, w_down, out):
    total = jnp.dot(context[...], w_out[...], preferred_element_type=jnp.float32)
    total = total + jnp.dot(activated[...], w_down[...], preferred_element_type=jnp.float32)
    out[...] = total.astype(jnp.bfloat16)


def branch_sum(line, context, activated, w_out, w_down):
    length, local_width = context.shape
    hidden, width = w_down.shape
    tile = min(256, length)
    return line.call(
        branch_kernel,
        "branch_sum",
        (length // tile,),
        [context, activated, w_out, w_down],
        [
            pl.BlockSpec((tile, local_width), row),
            pl.BlockSpec((tile, hidden), row),
            pl.BlockSpec((local_width, width), whole),
            pl.BlockSpec((hidden, width), whole),
        ],
        [((length, width), jnp.bfloat16, pl.BlockSpec((tile, width), row))],
    )[0]


def normed_kernel(mixed, up, unit, w_qkv, w_up, out, gain, shift):
    width = w_qkv.shape[2]
    total = lax.dot_general(up[...], w_up[...], NT, preferred_element_type=jnp.float32)
    for j in range(3):
        total = total + lax.dot_general(
            mixed[:, j * width : (j + 1) * width],
            w_qkv[j],
            NT,
            preferred_element_type=jnp.float32,
        )
    out[...] = total.astype(jnp.bfloat16)

    @pl.when(pl.program_id(0) == 0)
    def _():
        gain[...] = jnp.zeros_like(gain)
        shift[...] = jnp.zeros_like(shift)

    gain[...] += jnp.sum(total * unit[...].astype(jnp.float32), axis=0, keepdims=True)
    shift[...] += jnp.sum(total, axis=0, keepdims=True)


def normed_sum(line, grad_mixed, grad_up, unit, w_qkv, w_up):
    length, triple = grad_mixed.shape
    width, hidden = w_up.shape
    tile = min(256, length)
    return line.call(
        normed_kernel,
        "normed_sum",
        (length // tile,),
        [grad_mixed, grad_up, unit, w_qkv, w_up],
        [
            pl.BlockSpec((tile, triple), row),
            pl.BlockSpec((tile, hidden), row),
            pl.BlockSpec((tile, width), row),
            pl.BlockSpec(w_qkv.shape, lambda i: (0, 0, 0)),
            pl.BlockSpec((width, hidden), whole),
        ],
        [
            ((length, width), jnp.bfloat16, pl.BlockSpec((tile, width), row)),
            ((1, width), jnp.float32, pl.BlockSpec((1, width), whole)),
            ((1, width), jnp.float32, pl.BlockSpec((1, width), whole)),
        ],
    )


def norm_back_kernel(grad_normed, x, grad, gain, out):
    wide = x[...].astype(jnp.float32)
    centred = wide - jnp.mean(wide, axis=1, keepdims=True)
    inverse_std = lax.rsqrt(jnp.mean(centred * centred, axis=1, keepdims=True) + EPSILON)
    unit = centred * inverse_std
    slope = grad_normed[...].astype(jnp.float32) * gain[...]
    inner = jnp.mean(slope * unit, axis=1, keepdims=True)
    slope = slope - jnp.mean(slope, axis=1, keepdims=True) - unit * inner
    out[...] = (grad[...].astype(jnp.float32) + inverse_std * slope).astype(jnp.bfloat16)


def norm_back(line, grad_normed, x, grad, gain):
    block, width = x.shape
    tile = min(128, block)
    spec = pl.BlockSpec((tile, width), row)
    return line.call(
        norm_back_kernel,
        "norm_back",
        (block // tile,),
        [grad_normed, x, grad, gain],
        [spec, spec, spec, pl.BlockSpec((1, width), whole)],
        [((block, width), jnp.bfloat16, spec)],
    )[0]


def finish_kernel(layout, count, order, *refs):
    s = pl.program_id(0)
    outs = refs[-1:] if isinstance(layout, int) else refs[-len(layout) :]
    for index, source in enumerate(refs[:count]):

        @pl.when(s == index)
        def _(source=source):
            if isinstance(layout, int):
                group = outs[0].shape[2]
                for j in range(layout):
                    columns = slice(j * group, (j + 1) * group)
                    outs[0][j] = source[:, columns].astype(jnp.float32)
            else:
                start = 0
                columns = source.shape[1]
                for out in outs:
                    rows, spread = out.shape
                    for j in range(spread // columns):
                        out[:, j * columns : (j + 1) * columns] = source[
                            start : start + rows, :
                        ].astype(jnp.float32)
                        start += rows


def finish(line, order, pieces, layout, carried=(), cost=0):
    rows, columns = pieces[0].shape
    in_specs = [pl.BlockSpec(pieces[0].shape, whole) for _ in pieces]
    in_specs += [pl.BlockSpec(memory_space=pl.ANY)] * len(carried)
    if isinstance(layout, int):
        group = columns // layout
        spec = pl.BlockSpec((layout, rows, group), lambda s, order: (0, order[s], 0))
        outs = [((layout, 4 * rows, group), jnp.float32, spec)]
    else:
        outs = [
            (
                (4 * tall, spread),
                jnp.float32,
                pl.BlockSpec((tall, wide), lambda s, order, place=place: (order[s], place)),
            )
            for tall, wide, spread, place in layout
        ]
    return line.call(
        partial(finish_kernel, layout, len(pieces)),
        "finish",
        (len(pieces),),
        [order, *pieces, *carried],
        in_specs,
        outs,
        scalars=1,
        aliases={1 + len(pieces) + i: i for i in range(len(carried))},
        cost=cost,
    )


def add_low(one, other):
    return (one.astype(jnp.float32) + other.astype(jnp.float32)).astype(jnp.bfloat16)


def swap_rows(array, bit):
    return lax.ppermute(array, "rows", [(i, i ^ bit) for i in range(4)])


def outer_kernel(extra, order, left, right, *refs):
    s = pl.program_id(0)
    dims = (((0,), (0,)), ((), ()))
    low = lax.dot_general(left[...], right[...], dims, preferred_element_type=jnp.float32)
    parts = [low.astype(jnp.bfloat16)]
    outs = refs[extra : 4 + extra]
    if extra:
        second, held = refs[0], refs[-1]

        @pl.when(s == 0)
        def _():
            held[...] = lax.dot_general(
                second[...], right[...], dims, preferred_element_type=jnp.float32
            ).astype(jnp.bfloat16)

        rows = held.shape[0] // 4
        parts.append(held[pl.ds(pl.multiple_of(order[s] * rows, rows), rows), :])
    for index, out in enumerate(outs):

        @pl.when(s == index)
        def _(out=out):
            start = 0
            for part in parts:
                out[start : start + part.shape[0], :] = part
                start += part.shape[0]


def outer_parts(line, order, left, right, second=None):
    length, tall = left.shape
    columns = right.shape[1]
    extra = [] if second is None else [second]
    rows = (tall + sum(array.shape[1] for array in extra)) // 4
    return line.call(
        partial(outer_kernel, len(extra)),
        "outer_parts",
        (4,),
        [order, left, right, *extra],
        [
            pl.BlockSpec((length, tall // 4), lambda s, order: (0, order[s])),
            *(pl.BlockSpec(array.shape, whole) for array in (right, *extra)),
        ],
        [((rows, columns), jnp.bfloat16, pl.BlockSpec((rows, columns), whole)) for _ in range(4)],
        scalars=1,
        scratch=[pltpu.VMEM((array.shape[1], columns), jnp.bfloat16) for array in extra],
    )


class RowsSum:
    def __init__(self, rows, line, left, right, second=None, between=None):
        self.rows, self.line, self.phase, self.own = rows, line, 0, False
        if rows != 4:
            self.order = jnp.arange(4, dtype=jnp.int32)
            self.pieces = lax.psum(outer_parts(line, self.order, left, right, second), "rows")
            return
        place = lax.axis_index("rows")
        x, y = place % 2, place // 2
        away = jnp.stack([1 - x, 3 - y, x, 2 + y]).astype(jnp.int32)
        self.order = jnp.stack([x, 1 - x, 2 + y, 3 - y]).astype(jnp.int32)
        self.bits = ((1, 2), (2, 1))
        *away, keep_a, keep_b = outer_parts(line, away, left, right, second)
        self.keep = [keep_a, keep_b]
        if between is not None:
            between()
        self.send(0, away)

    def send(self, which, arrays):
        arrays = self.line.join(*arrays)
        self.came = [swap_rows(a, bits[which]) for a, bits in zip(arrays, self.bits)]
        return arrays

    def advance(self):
        if self.rows != 4:
            return
        self.phase += 1
        came = self.line.join(*self.came)
        if self.phase < 3:
            self.keep = [add_low(k, c) for k, c in zip(self.keep, came)]
            self.keep = self.send(2 - self.phase, self.keep)
        else:
            self.pieces = [self.keep[0], came[0], self.keep[1], came[1]]

    def finish_own(self, *layout):
        if self.rows != 4:
            return ()
        self.own = True
        return finish(self.line, self.order[::2], self.keep, *layout)

    def finish(self, *layout, **more):
        if self.phase < 3:
            self.advance()
        if self.own:
            return finish(self.line, self.order[1::2], self.pieces[1::2], *layout, **more)
        return finish(self.line, self.order, self.pieces, *layout, **more)


class SmallSum:
    def __init__(self, line, array, more, rows, tp):
        self.line, self.array, self.more = line, array, more
        self.steps = [("tp", 1 << i, tp) for i in range(tp.bit_length() - 1)]
        self.steps += [("rows", 1 << i, rows) for i in range(rows.bit_length() - 1)]
        self.send()

    def send(self):
        if self.steps:
            axis, step, size = self.steps.pop(0)
            if axis == "rows" and self.more is not None:
                self.array, self.more = jnp.concatenate([self.array, self.more]), None
            (self.array,) = self.line.join(self.array)
            self.came = lax.ppermute(self.array, axis, [(i, i ^ step) for i in range(size)])
        else:
            self.came = None

    def step(self):
        if self.came is not None:
            (came,) = self.line.join(self.came)
            self.array = self.array + came
            self.send()

    def rest(self):
        while self.came is not None:
            self.step()
        return self.array


class SmallGather:
    def __init__(self, line, array, me, tp):
        self.line, self.me, self.step = line, me, 1
        while 2 * self.step < tp:
            other = lax.ppermute(array, "tp", [(i, i ^ self.step) for i in range(tp)])
            array = self.laid(array, other)
            self.step *= 2
        (self.array,) = line.join(array)
        self.other = lax.ppermute(self.array, "tp", [(i, i ^ self.step) for i in range(tp)])

    def laid(self, array, other):
        return jnp.where(
            (self.me // self.step) % 2 == 0,
            jnp.concatenate([array, other]),
            jnp.concatenate([other, array]),
        )

    def whole(self):
        return self.line.join(self.laid(self.array, *self.line.join(self.other)))[0]


def token_sum(matrix):
    ones_row = jnp.ones((1, matrix.shape[0]), matrix.dtype)
    return jnp.dot(ones_row, matrix, preferred_element_type=jnp.float32)[0]


def local(
    rows,
    tp,
    hidden_in,
    segment_ids,
    ln_gain,
    ln_bias,
    w_qkv,
    b_qkv,
    w_out,
    out_bias,
    w_up,
    b_up,
    w_down,
    cotangent,
):
    x = hidden_in[0]
    block, width = x.shape
    length = block * tp
    local_width = w_qkv.shape[2]
    hidden = w_up.shape[1]
    chips = tp // 2
    me = lax.axis_index("tp")
    chip, core = me // 2, me % 2
    line = Line()

    around = [(i, (i + 2) % tp) for i in range(tp)]
    sibling = [(i, i ^ 1) for i in range(tp)]
    mine, others = [x], [lax.ppermute(x, "tp", sibling)]
    coming = lax.ppermute(x, "tp", around)
    ids = SmallGather(line, segment_ids[0], me, tp)

    def serve():
        nonlocal coming
        (arrived,) = line.join(coming)
        mine.append(arrived)
        if len(mine) < chips:
            coming = lax.ppermute(arrived, "tp", around)
        others.append(lax.ppermute(arrived, "tp", sibling))
    columns = width // 2
    serve()
    segments = ids.whole()
    starts = positions_of(segments)
    tables = rotary_tables(jnp.arange(length, dtype=jnp.int32) - starts)
    lows = starts[::block] // block
    starts = jnp.broadcast_to(starts[None], (8, length))
    w_three = jnp.transpose(w_qkv, (1, 0, 2))
    weights = (
        ln_gain.reshape(1, width),
        ln_bias.reshape(1, width),
        w_three,
        b_qkv.reshape(1, 3 * local_width),
        w_up,
        b_up.reshape(1, hidden),
    )
    carried = ()

    def project_slot(s, cost=0):
        place = jnp.stack([(chip - s + chips) % chips, core]).astype(jnp.int32)
        pair = line.join(mine[s], others[s])
        return project(line, place, *pair, weights, tables[:2], length, carried, cost)

    carried = project_slot(0)
    for s in range(1, chips):
        if s > 1:
            serve()
        if s != 1 or chips == 2:
            for t in (1, 2) if s == 2 else (s,):
                carried = project_slot(t, cost=920 * 10**8)
                if t == max(chips - 3, 1):
                    halves = line.join(cotangent[0, :, :columns], cotangent[0, :, columns:])
                    grads = [lax.all_gather(half, "tp", axis=0, tiled=True) for half in halves]
    normed, unit, mixed, activated, slope = carried

    hidden_parts, local_parts = hidden // 4, local_width // 4
    sums = partial(RowsSum, rows, line)
    context, lse = attend_forward(line, lows, starts, mixed, block)
    d0 = sums(activated, grads[0], context)
    branch = branch_sum(line, context, activated, w_out, w_down)
    d0.advance()
    (branch,) = line.join(branch)
    branch_total = lax.psum_scatter(branch, "tp", scatter_dimension=0, tiled=True)
    d1 = sums(activated, grads[1], context)
    d0.advance()
    grad_up, grad_context, grad_b_up = backward_products(line, grads, w_down, w_out, slope)
    d1.advance()
    up = sums(normed, grad_up, between=d0.advance)
    grad_mixed = attend_backward(
        line, lows, starts, lse, mixed, context, grad_context, *tables, block
    )
    d1.advance()
    up.advance()
    (branch_total,) = line.join(branch_total)
    part, gain_part, shift_part = normed_sum(line, grad_mixed, grad_up, unit, w_three, w_up)
    grad_normed = lax.psum_scatter(part, "tp", scatter_dimension=0, tiled=True)
    up.advance()
    three = sums(normed, grad_mixed, between=d1.advance)
    small = SmallSum(
        line,
        jnp.concatenate([gain_part, shift_part, token_sum(cotangent[0])[None]], axis=1)[0],
        jnp.concatenate([token_sum(grad_mixed), grad_b_up[0]]),
        rows,
        tp,
    )
    down = d0.finish([(hidden_parts, columns, width, 0), (local_parts, columns, width, 0)])
    small.step()
    down = d1.finish(
        [(hidden_parts, columns, width, 1), (local_parts, columns, width, 1)], carried=down
    )
    up.advance()
    three.advance()
    small.step()
    up = up.finish([(width // 4, hidden, hidden, 0)], cost=1092 * 10**8)
    three.advance()
    own = three.finish_own(3)
    small.step()
    small.step()
    three = three.finish(3, carried=own, cost=287 * 10**8)
    small = small.rest()
    grad_w_down, grad_w_out = down
    grad_w_up = up[0]
    grad_w_qkv = jnp.transpose(three[0], (1, 0, 2))

    inputs = x.astype(jnp.float32)
    hidden_out = (inputs + branch_total.astype(jnp.float32) + out_bias).astype(jnp.bfloat16)
    grad_input = norm_back(line, grad_normed, x, cotangent[0], ln_gain.reshape(1, width))
    tail = small[: 3 * width].reshape(3, width)
    grad_b_qkv = small[3 * width : 3 * (width + local_width)].reshape(3, local_width)
    grad_b_up = small[3 * (width + local_width) :]
    return (
        hidden_out[None],
        grad_input[None],
        tail[0],
        tail[1],
        grad_w_qkv,
        grad_b_qkv,
        grad_w_out,
        tail[2],
        grad_w_up,
        grad_b_up,
        grad_w_down,
    )


def solution(mesh):
    in_specs = (
        P("rows", "tp", None),
        P("rows", "tp"),
        P(),
        P(),
        P(None, None, "tp"),
        P(None, "tp"),
        P("tp", None),
        P(),
        P(None, "tp"),
        P("tp"),
        P("tp", None),
        P("rows", "tp", None),
    )
    out_specs = (
        P("rows", "tp", None),
        P("rows", "tp", None),
        P(),
        P(),
        P(None, None, "tp"),
        P(None, "tp"),
        P("tp", None),
        P(),
        P(None, "tp"),
        P("tp"),
        P("tp", None),
    )
    return jax.shard_map(
        partial(local, mesh.shape["rows"], mesh.shape["tp"]),
        mesh=mesh,
        in_specs=in_specs,
        out_specs=out_specs,
        check_vma=False,
    )
```

```python
from functools import partial
import math

import jax
import jax.numpy as jnp
from jax import lax
from jax.experimental import pallas as pl
from jax.experimental.pallas import tpu as pltpu
from jax.sharding import PartitionSpec as P

HEAD_DIM = 64
ROT = 32
EPSILON = 1e-05
NEGATIVE = -1e30
VMEM_BYTES = 56 * 2**20
NT = (((1,), (1,)), ((), ()))


class Line:
    def __init__(self):
        self.token = jnp.zeros((8, 128), jnp.float32)

    def join(self, *arrays):
        *arrays, self.token = lax.optimization_barrier((*arrays, self.token))
        return arrays

    def call(
        self, body, name, grid, operands, in_specs, outs, scalars=0, scratch=(), aliases=None, cost=0
    ):
        inputs = len(operands)

        def whole_body(*refs):
            refs = list(refs)
            token = refs.pop(inputs + 1 + len(outs))
            refs.pop(inputs)
            token[...] = jnp.zeros_like(token)
            body(*refs)

        *results, self.token = pl.pallas_call(
            whole_body,
            grid_spec=pltpu.PrefetchScalarGridSpec(
                num_scalar_prefetch=scalars,
                grid=grid,
                in_specs=[*in_specs, pl.BlockSpec(memory_space=pl.ANY)],
                out_specs=[
                    *(spec for _, _, spec in outs),
                    pl.BlockSpec((8, 128), lambda *index: (0, 0)),
                ],
                scratch_shapes=list(scratch),
            ),
            out_shape=[
                *(jax.ShapeDtypeStruct(shape, dtype) for shape, dtype, _ in outs),
                jax.ShapeDtypeStruct((8, 128), jnp.float32),
            ],
            input_output_aliases=aliases or {},
            compiler_params=pltpu.CompilerParams(vmem_limit_bytes=VMEM_BYTES),
            cost_estimate=pl.CostEstimate(
                flops=2**20 + cost, bytes_accessed=2**16, transcendentals=0
            ),
            name=name,
        )(*operands, self.token)
        return results


def whole(*index):
    return (0, 0)


def row(i, *scalars):
    return (i, 0)


def lane_heads(rows, width):
    return lax.broadcasted_iota(jnp.int32, (rows, width), 1) // HEAD_DIM


def swap_pairs(x):
    width = x.shape[1]
    lane = lax.broadcasted_iota(jnp.int32, x.shape, 1) % HEAD_DIM
    up = pltpu.roll(x, width - ROT // 2, 1)
    down = pltpu.roll(x, ROT // 2, 1)
    return jnp.where(lane < ROT // 2, up, down)


def mask_bias(starts, key_first, query_first, block):
    key_index = key_first + lax.broadcasted_iota(jnp.int32, (block, block), 0)
    query_index = query_first + lax.broadcasted_iota(jnp.int32, (block, block), 1)
    allowed = (key_index >= starts) & (key_index <= query_index)
    return jnp.where(allowed, 0.0, NEGATIVE).astype(jnp.float32)


def stack_heads(source, stacked, block):
    length, width = source.shape
    row_heads = lane_heads(block, width)
    for j in range(length // block):
        rows = pl.ds(j * block, block)
        piece = source[rows, :]
        for h in range(width // HEAD_DIM):
            stacked[j, pl.ds(h * block, block), :] = jnp.where(row_heads == h, piece, 0).astype(
                jnp.bfloat16
            )


def forward_kernel(lows, starts, q, k, v, context, lse, v_t, k_heads, acc):
    block, width = q.shape
    heads = width // HEAD_DIM
    length = k.shape[0]
    i = pl.program_id(0)

    @pl.when(i == 0)
    def _():
        stack_heads(k, k_heads, block)
        for j in range(length // block):
            rows = pl.ds(j * block, block)
            v_t[:, rows] = v[rows, :].T

    turned = (q[...] * 0.125).T
    acc[...] = jnp.zeros_like(acc)

    def step(j, carry):
        tops, sums = carry
        first = pl.multiple_of(j * block, block)
        all_scores = jnp.dot(k_heads[j], turned, preferred_element_type=jnp.float32)
        bias = mask_bias(starts[0:1, :], first, i * block, block)
        new_tops, new_sums = [], []
        for h in range(heads):
            rows = pl.ds(h * HEAD_DIM, HEAD_DIM)
            scores = all_scores[h * block : (h + 1) * block, :] + bias
            top = jnp.maximum(tops[h], jnp.max(scores, axis=0, keepdims=True))
            weights = jnp.exp(scores - top)
            keep = jnp.exp(tops[h] - top)
            new_tops.append(top)
            new_sums.append(sums[h] * keep + jnp.sum(weights, axis=0, keepdims=True))
            acc[rows, :] = acc[rows, :] * keep + jnp.dot(
                v_t[rows, pl.ds(first, block)],
                weights.astype(jnp.bfloat16),
                preferred_element_type=jnp.float32,
            )
        return tuple(new_tops), tuple(new_sums)

    empty = tuple(jnp.full((1, block), NEGATIVE, jnp.float32) for _ in range(heads))
    nothing = tuple(jnp.zeros((1, block), jnp.float32) for _ in range(heads))
    tops, sums = lax.fori_loop(lows[i], i + 1, step, (empty, nothing))
    for h in range(heads):
        rows = pl.ds(h * HEAD_DIM, HEAD_DIM)
        acc[rows, :] = acc[rows, :] / sums[h]
        lse[h : h + 1, :] = tops[h] + jnp.log(sums[h])
    context[...] = acc[...].astype(jnp.bfloat16).T


def attend_forward(line, lows, starts, mixed, block):
    length, triple = mixed.shape
    local_width = triple // 3
    blocks = length // block
    stack = (blocks, local_width // HEAD_DIM * block, local_width)
    column = lambda i, lows: (0, i)
    return line.call(
        forward_kernel,
        "attend_forward",
        (blocks,),
        [lows, starts, mixed, mixed, mixed],
        [
            pl.BlockSpec((8, block), column),
            pl.BlockSpec((block, local_width), row),
            pl.BlockSpec((length, local_width), lambda i, lows: (0, 1)),
            pl.BlockSpec((length, local_width), lambda i, lows: (0, 2)),
        ],
        [
            ((length, local_width), jnp.bfloat16, pl.BlockSpec((block, local_width), row)),
            ((8, length), jnp.float32, pl.BlockSpec((8, block), column)),
        ],
        scalars=1,
        scratch=[
            pltpu.VMEM((local_width, length), jnp.bfloat16),
            pltpu.VMEM(stack, jnp.bfloat16),
            pltpu.VMEM((local_width, block), jnp.float32),
        ],
    )


def backward_kernel(
    lows, starts, lse, q, k, v, context, grad, cosine, sine, turned_tables, grad_mixed, k_t, k_heads, v_heads, grad_q, grad_k, grad_v
):
    block, width = q.shape
    heads = width // HEAD_DIM
    length = k.shape[0]
    i = pl.program_id(0)
    blocks = length // block

    @pl.when(i == 0)
    def _():
        grad_k[...] = jnp.zeros_like(grad_k)
        grad_v[...] = jnp.zeros_like(grad_v)
        stack_heads(k, k_heads, block)
        stack_heads(v, v_heads, block)
        for j in range(blocks):
            rows = pl.ds(j * block, block)
            k_t[:, rows] = k[rows, :].T

    row_heads = lane_heads(block, width)
    scaled = q[...] * 0.125
    grads = grad[...]
    masked_q = [jnp.where(row_heads == h, scaled, 0).astype(jnp.bfloat16) for h in range(heads)]
    masked_g = [jnp.where(row_heads == h, grads, 0).astype(jnp.bfloat16) for h in range(heads)]
    turned_q = scaled.T
    turned_g = grads.T
    products = grads.astype(jnp.float32) * context[...].astype(jnp.float32)
    high = products.astype(jnp.bfloat16)
    low = (products - high.astype(jnp.float32)).astype(jnp.bfloat16)
    chooser = lax.broadcasted_iota(jnp.int32, (8, width), 0) == lane_heads(8, width)
    chooser = jnp.where(chooser, 1.0, 0.0).astype(jnp.bfloat16)
    sums = lax.dot_general(chooser, high, NT, preferred_element_type=jnp.float32)
    sums = sums + lax.dot_general(chooser, low, NT, preferred_element_type=jnp.float32)
    inner = [sums[h : h + 1, :] for h in range(heads)]
    grad_q[...] = jnp.zeros_like(grad_q)

    def step(j, carry):
        first = pl.multiple_of(j * block, block)
        here = pl.ds(first, block)
        all_scores = jnp.dot(k_heads[j], turned_q, preferred_element_type=jnp.float32)
        all_grads = jnp.dot(v_heads[j], turned_g, preferred_element_type=jnp.float32)
        bias = mask_bias(starts[0:1, :], first, i * block, block)
        probs, slopes = [], []
        for h in range(heads):
            rows = pl.ds(h * HEAD_DIM, HEAD_DIM)
            part = slice(h * block, (h + 1) * block)
            scores = all_scores[part, :]
            soft = jnp.exp(scores + bias - lse[h : h + 1, :])
            grad_probs = all_grads[part, :]
            slope = (soft * (grad_probs - inner[h])).astype(jnp.bfloat16)
            grad_q[rows, :] += jnp.dot(k_t[rows, here], slope, preferred_element_type=jnp.float32)
            probs.append(soft.astype(jnp.bfloat16))
            slopes.append(slope)
        grad_v[here, :] += jnp.dot(
            jnp.concatenate(probs, axis=1),
            jnp.concatenate(masked_g, axis=0),
            preferred_element_type=jnp.float32,
        )
        grad_k[here, :] += jnp.dot(
            jnp.concatenate(slopes, axis=1),
            jnp.concatenate(masked_q, axis=0),
            preferred_element_type=jnp.float32,
        )
        return carry

    lax.fori_loop(lows[i], i + 1, step, 0)

    def unrotate(x, rows):
        parts = []
        for part in range(width // 128):
            piece = x[:, part * 128 : (part + 1) * 128]
            parts.append(piece * cosine[rows, :] - swap_pairs(piece) * sine[rows, :])
        return jnp.concatenate(parts, axis=1).astype(jnp.bfloat16)

    mine = pl.ds(pl.multiple_of(i * block, block), block)
    cos_t, sin_t = turned_tables[0 : ROT // 2, :], turned_tables[ROT // 2 : ROT, :]
    for h in range(heads):
        top = pl.ds(h * HEAD_DIM, ROT // 2)
        bottom = pl.ds(h * HEAD_DIM + ROT // 2, ROT // 2)
        one, two = grad_q[top, :], grad_q[bottom, :]
        grad_q[top, :] = one * cos_t + two * sin_t
        grad_q[bottom, :] = two * cos_t - one * sin_t
    grad_mixed[mine, 0:width] = (grad_q[...] * 0.125).astype(jnp.bfloat16).T

    @pl.when(i == blocks - 1)
    def _():
        def finish(j, carry):
            rows = pl.ds(pl.multiple_of(j * block, block), block)
            grad_mixed[rows, width : 2 * width] = unrotate(grad_k[rows, :], rows)
            grad_mixed[rows, 2 * width : 3 * width] = grad_v[rows, :].astype(jnp.bfloat16)
            return carry

        lax.fori_loop(0, blocks, finish, 0)


def attend_backward(line, lows, starts, lse, mixed, context, grad_context, cosine, sine, turned, block):
    length, triple = mixed.shape
    local_width = triple // 3
    blocks = length // block
    stack = (blocks, local_width // HEAD_DIM * block, local_width)
    column = lambda i, lows: (0, i)
    return line.call(
        backward_kernel,
        "attend_backward",
        (blocks,),
        [lows, starts, lse, mixed, mixed, mixed, context, grad_context, cosine, sine, turned],
        [
            pl.BlockSpec((8, block), column),
            pl.BlockSpec((8, block), column),
            pl.BlockSpec((block, local_width), row),
            pl.BlockSpec((length, local_width), lambda i, lows: (0, 1)),
            pl.BlockSpec((length, local_width), lambda i, lows: (0, 2)),
            pl.BlockSpec((block, local_width), row),
            pl.BlockSpec((block, local_width), row),
            pl.BlockSpec((length, 128), whole),
            pl.BlockSpec((length, 128), whole),
            pl.BlockSpec((ROT, block), column),
        ],
        [((length, triple), jnp.bfloat16, pl.BlockSpec((length, triple), whole))],
        scalars=1,
        scratch=[
            pltpu.VMEM((local_width, length), jnp.bfloat16),
            pltpu.VMEM(stack, jnp.bfloat16),
            pltpu.VMEM(stack, jnp.bfloat16),
            pltpu.VMEM((local_width, block), jnp.float32),
            pltpu.VMEM((length, local_width), jnp.float32),
            pltpu.VMEM((length, local_width), jnp.float32),
        ],
        cost=632 * 10**8,
    )[0]


def positions_of(segments):
    ids = jnp.arange(8, dtype=jnp.int32)
    counts = jnp.sum((segments[None, :] < ids[:, None]).astype(jnp.int32), axis=1)
    return jnp.sum(jnp.where(segments[None, :] == ids[:, None], counts[:, None], 0), axis=0)


def rotary_tables(positions):
    lane = jnp.arange(128, dtype=jnp.int32) % HEAD_DIM
    step = (lane % (ROT // 2)).astype(jnp.float32)
    inverse = jnp.exp(step * (-2.0 * math.log(10000.0) / ROT))
    angles = positions.astype(jnp.float32)[:, None] * inverse[None, :]
    rotated = (lane < ROT)[None, :]
    cosine = jnp.where(rotated, jnp.cos(angles), 1.0)
    sine = jnp.where(rotated, jnp.where((lane < ROT // 2)[None, :], -1.0, 1.0) * jnp.sin(angles), 0.0)
    turned = jnp.concatenate([cosine[:, : ROT // 2], sine[:, ROT // 2 : ROT]], axis=1).T
    return cosine, sine, turned


def gelu_pair(u):
    scale = math.sqrt(2.0 / math.pi)
    square = u * u
    bent = jnp.tanh(scale * u * (1.0 + 0.044715 * square))
    half = 0.5 * (1.0 + bent)
    slope = half + 0.5 * u * (1.0 - bent * bent) * (scale * (1.0 + 3 * 0.044715 * square))
    return u * half, slope


def project_kernel(place, mine, other, gain, shift, w_qkv, b_qkv, w_up, b_up, cosine, sine, *refs):
    normed, unit, mixed, activated, slope = refs[-5:]
    n = pl.program_id(0)
    block = mine.shape[0]
    width = w_qkv.shape[2]
    strip = min(128, block)
    strips = [pl.ds(r * strip, strip) for r in range(2 * block // strip)]

    @pl.when(n == 0)
    def _():
        for source, first in ((mine, place[1] * block), (other, (1 - place[1]) * block)):
            for r in range(block // strip):
                wide = source[pl.ds(r * strip, strip), :].astype(jnp.float32)
                centred = wide - jnp.mean(wide, axis=1, keepdims=True)
                inverse_std = lax.rsqrt(
                    jnp.mean(centred * centred, axis=1, keepdims=True) + EPSILON
                )
                rows = pl.ds(pl.multiple_of(first + r * strip, strip), strip)
                even = centred * inverse_std
                unit[rows, :] = even.astype(jnp.bfloat16)
                normed[rows, :] = (even * gain[...] + shift[...]).astype(jnp.bfloat16)
        for rows in strips:
            for j in range(3):
                columns = slice(j * width, (j + 1) * width)
                y = jnp.dot(normed[rows, :], w_qkv[j], preferred_element_type=jnp.float32)
                y = y + b_qkv[:, columns]
                if j < 2:
                    parts = []
                    for part in range(width // 128):
                        piece = y[:, part * 128 : (part + 1) * 128]
                        parts.append(piece * cosine[rows, :] + swap_pairs(piece) * sine[rows, :])
                    y = jnp.concatenate(parts, axis=1)
                mixed[rows, columns] = y.astype(jnp.bfloat16)

    @pl.when(n > 0)
    def _():
        for rows in strips:
            u = jnp.dot(normed[rows, :], w_up[...], preferred_element_type=jnp.float32) + b_up[...]
            high, tilt = gelu_pair(u)
            activated[rows, :] = high.astype(jnp.bfloat16)
            slope[rows, :] = tilt.astype(jnp.bfloat16)


def project(line, place, mine, other, weights, tables, length, carried, cost=0):
    gain, shift, w_qkv, b_qkv, w_up, b_up = weights
    block, width = mine.shape
    local_width = w_qkv.shape[2]
    hidden = w_up.shape[1]
    tile = min(512, hidden)
    up = lambda n, place: (0, jnp.maximum(n - 1, 0))
    here = lambda n, place: (place[0], 0)
    up_here = lambda n, place: (place[0], jnp.maximum(n - 1, 0))
    operands = [place, mine, other, gain, shift, w_qkv, b_qkv, w_up, b_up, *tables, *carried]
    return line.call(
        project_kernel,
        "project",
        (1 + hidden // tile,),
        operands,
        [
            pl.BlockSpec((block, width), whole),
            pl.BlockSpec((block, width), whole),
            pl.BlockSpec((1, width), whole),
            pl.BlockSpec((1, width), whole),
            pl.BlockSpec((3, width, local_width), lambda n, place: (0, 0, 0)),
            pl.BlockSpec((1, 3 * local_width), whole),
            pl.BlockSpec((width, tile), up),
            pl.BlockSpec((1, tile), up),
            pl.BlockSpec((2 * block, 128), here),
            pl.BlockSpec((2 * block, 128), here),
            *[pl.BlockSpec(memory_space=pl.ANY)] * len(carried),
        ],
        [
            ((length, columns), jnp.bfloat16, pl.BlockSpec((2 * block, wide), index))
            for columns, wide, index in (
                (width, width, here),
                (width, width, here),
                (3 * local_width, 3 * local_width, here),
                (hidden, tile, up_here),
                (hidden, tile, up_here),
            )
        ],
        scalars=1,
        aliases={len(operands) - 5 + i: i for i in range(len(carried))},
        cost=cost,
    )


def backward_products_kernel(layout, *refs):
    grads = refs[:layout]
    w_down, w_out, slope, grad_up, grad_context, total = refs[layout:]
    columns = grads[0].shape[1]
    up, context = 0.0, 0.0
    for c in range(layout):
        part = slice(c * columns, (c + 1) * columns)
        piece = grads[c][...]
        up = up + lax.dot_general(piece, w_down[:, part], NT, preferred_element_type=jnp.float32)
        context = context + lax.dot_general(
            piece, w_out[:, part], NT, preferred_element_type=jnp.float32
        )
    low = (up * slope[...].astype(jnp.float32)).astype(jnp.bfloat16)
    grad_up[...] = low
    grad_context[...] = context.astype(jnp.bfloat16)

    @pl.when(pl.program_id(0) == 0)
    def _():
        total[...] = jnp.zeros_like(total)

    total[...] += jnp.sum(low.astype(jnp.float32), axis=0, keepdims=True)


def backward_products(line, grads, w_down, w_out, slope):
    length, columns = grads[0].shape
    hidden, width = w_down.shape
    local_width = w_out.shape[0]
    tile = min(256, length)
    return line.call(
        partial(backward_products_kernel, len(grads)),
        "backward_products",
        (length // tile,),
        [*grads, w_down, w_out, slope],
        [pl.BlockSpec((tile, columns), row) for _ in grads]
        + [
            pl.BlockSpec((hidden, width), whole),
            pl.BlockSpec((local_width, width), whole),
            pl.BlockSpec((tile, hidden), row),
        ],
        [
            ((length, hidden), jnp.bfloat16, pl.BlockSpec((tile, hidden), row)),
            ((length, local_width), jnp.bfloat16, pl.BlockSpec((tile, local_width), row)),
            ((1, hidden), jnp.float32, pl.BlockSpec((1, hidden), whole)),
        ],
    )


def branch_kernel(context, activated, w_out, w_down, out):
    total = jnp.dot(context[...], w_out[...], preferred_element_type=jnp.float32)
    total = total + jnp.dot(activated[...], w_down[...], preferred_element_type=jnp.float32)
    out[...] = total.astype(jnp.bfloat16)


def branch_sum(line, context, activated, w_out, w_down):
    length, local_width = context.shape
    hidden, width = w_down.shape
    tile = min(256, length)
    return line.call(
        branch_kernel,
        "branch_sum",
        (length // tile,),
        [context, activated, w_out, w_down],
        [
            pl.BlockSpec((tile, local_width), row),
            pl.BlockSpec((tile, hidden), row),
            pl.BlockSpec((local_width, width), whole),
            pl.BlockSpec((hidden, width), whole),
        ],
        [((length, width), jnp.bfloat16, pl.BlockSpec((tile, width), row))],
    )[0]


def normed_kernel(mixed, up, unit, w_qkv, w_up, out, gain, shift):
    width = w_qkv.shape[2]
    total = lax.dot_general(up[...], w_up[...], NT, preferred_element_type=jnp.float32)
    for j in range(3):
        total = total + lax.dot_general(
            mixed[:, j * width : (j + 1) * width],
            w_qkv[j],
            NT,
            preferred_element_type=jnp.float32,
        )
    out[...] = total.astype(jnp.bfloat16)

    @pl.when(pl.program_id(0) == 0)
    def _():
        gain[...] = jnp.zeros_like(gain)
        shift[...] = jnp.zeros_like(shift)

    gain[...] += jnp.sum(total * unit[...].astype(jnp.float32), axis=0, keepdims=True)
    shift[...] += jnp.sum(total, axis=0, keepdims=True)


def normed_sum(line, grad_mixed, grad_up, unit, w_qkv, w_up):
    length, triple = grad_mixed.shape
    width, hidden = w_up.shape
    tile = min(256, length)
    return line.call(
        normed_kernel,
        "normed_sum",
        (length // tile,),
        [grad_mixed, grad_up, unit, w_qkv, w_up],
        [
            pl.BlockSpec((tile, triple), row),
            pl.BlockSpec((tile, hidden), row),
            pl.BlockSpec((tile, width), row),
            pl.BlockSpec(w_qkv.shape, lambda i: (0, 0, 0)),
            pl.BlockSpec((width, hidden), whole),
        ],
        [
            ((length, width), jnp.bfloat16, pl.BlockSpec((tile, width), row)),
            ((1, width), jnp.float32, pl.BlockSpec((1, width), whole)),
            ((1, width), jnp.float32, pl.BlockSpec((1, width), whole)),
        ],
    )


def norm_back_kernel(grad_normed, x, grad, gain, out):
    wide = x[...].astype(jnp.float32)
    centred = wide - jnp.mean(wide, axis=1, keepdims=True)
    inverse_std = lax.rsqrt(jnp.mean(centred * centred, axis=1, keepdims=True) + EPSILON)
    unit = centred * inverse_std
    slope = grad_normed[...].astype(jnp.float32) * gain[...]
    inner = jnp.mean(slope * unit, axis=1, keepdims=True)
    slope = slope - jnp.mean(slope, axis=1, keepdims=True) - unit * inner
    out[...] = (grad[...].astype(jnp.float32) + inverse_std * slope).astype(jnp.bfloat16)


def norm_back(line, grad_normed, x, grad, gain):
    block, width = x.shape
    tile = block
    spec = pl.BlockSpec((tile, width), row)
    return line.call(
        norm_back_kernel,
        "norm_back",
        (block // tile,),
        [grad_normed, x, grad, gain],
        [spec, spec, spec, pl.BlockSpec((1, width), whole)],
        [((block, width), jnp.bfloat16, spec)],
    )[0]


def finish_kernel(layout, count, order, *refs):
    s = pl.program_id(0)
    outs = refs[-1:] if isinstance(layout, int) else refs[-len(layout) :]
    for index, source in enumerate(refs[:count]):

        @pl.when(s == index)
        def _(source=source):
            if isinstance(layout, int):
                group = outs[0].shape[2]
                for j in range(layout):
                    columns = slice(j * group, (j + 1) * group)
                    outs[0][j] = source[:, columns].astype(jnp.float32)
            else:
                start = 0
                columns = source.shape[1]
                for out in outs:
                    rows, spread = out.shape
                    for j in range(spread // columns):
                        out[:, j * columns : (j + 1) * columns] = source[
                            start : start + rows, :
                        ].astype(jnp.float32)
                        start += rows


def finish(line, order, pieces, layout, carried=(), cost=0):
    rows, columns = pieces[0].shape
    in_specs = [pl.BlockSpec(pieces[0].shape, whole) for _ in pieces]
    in_specs += [pl.BlockSpec(memory_space=pl.ANY)] * len(carried)
    if isinstance(layout, int):
        group = columns // layout
        spec = pl.BlockSpec((layout, rows, group), lambda s, order: (0, order[s], 0))
        outs = [((layout, 4 * rows, group), jnp.float32, spec)]
    else:
        outs = [
            (
                (4 * tall, spread),
                jnp.float32,
                pl.BlockSpec((tall, wide), lambda s, order, place=place: (order[s], place)),
            )
            for tall, wide, spread, place in layout
        ]
    return line.call(
        partial(finish_kernel, layout, len(pieces)),
        "finish",
        (len(pieces),),
        [order, *pieces, *carried],
        in_specs,
        outs,
        scalars=1,
        aliases={1 + len(pieces) + i: i for i in range(len(carried))},
        cost=cost,
    )


def add_low(one, other):
    return (one.astype(jnp.float32) + other.astype(jnp.float32)).astype(jnp.bfloat16)


def swap_rows(array, bit):
    return lax.ppermute(array, "rows", [(i, i ^ bit) for i in range(4)])


def outer_kernel(extra, order, left, right, *refs):
    s = pl.program_id(0)
    dims = (((0,), (0,)), ((), ()))
    low = lax.dot_general(left[...], right[...], dims, preferred_element_type=jnp.float32)
    parts = [low.astype(jnp.bfloat16)]
    outs = refs[extra : 4 + extra]
    if extra:
        second, held = refs[0], refs[-1]

        @pl.when(s == 0)
        def _():
            held[...] = lax.dot_general(
                second[...], right[...], dims, preferred_element_type=jnp.float32
            ).astype(jnp.bfloat16)

        rows = held.shape[0] // 4
        parts.append(held[pl.ds(pl.multiple_of(order[s] * rows, rows), rows), :])
    for index, out in enumerate(outs):

        @pl.when(s == index)
        def _(out=out):
            start = 0
            for part in parts:
                out[start : start + part.shape[0], :] = part
                start += part.shape[0]


def outer_parts(line, order, left, right, second=None):
    length, tall = left.shape
    columns = right.shape[1]
    extra = [] if second is None else [second]
    rows = (tall + sum(array.shape[1] for array in extra)) // 4
    return line.call(
        partial(outer_kernel, len(extra)),
        "outer_parts",
        (4,),
        [order, left, right, *extra],
        [
            pl.BlockSpec((length, tall // 4), lambda s, order: (0, order[s])),
            *(pl.BlockSpec(array.shape, whole) for array in (right, *extra)),
        ],
        [((rows, columns), jnp.bfloat16, pl.BlockSpec((rows, columns), whole)) for _ in range(4)],
        scalars=1,
        scratch=[pltpu.VMEM((array.shape[1], columns), jnp.bfloat16) for array in extra],
    )


class RowsSum:
    def __init__(self, rows, line, left, right, second=None, between=None):
        self.rows, self.line, self.phase, self.own = rows, line, 0, False
        if rows != 4:
            self.order = jnp.arange(4, dtype=jnp.int32)
            self.pieces = lax.psum(outer_parts(line, self.order, left, right, second), "rows")
            return
        place = lax.axis_index("rows")
        x, y = place % 2, place // 2
        away = jnp.stack([1 - x, 3 - y, x, 2 + y]).astype(jnp.int32)
        self.order = jnp.stack([x, 1 - x, 2 + y, 3 - y]).astype(jnp.int32)
        self.bits = ((1, 2), (2, 1))
        *away, keep_a, keep_b = outer_parts(line, away, left, right, second)
        self.keep = [keep_a, keep_b]
        if between is not None:
            between()
        self.send(0, away)

    def send(self, which, arrays):
        arrays = self.line.join(*arrays)
        self.came = [swap_rows(a, bits[which]) for a, bits in zip(arrays, self.bits)]
        return arrays

    def advance(self):
        if self.rows != 4:
            return
        self.phase += 1
        came = self.line.join(*self.came)
        if self.phase < 3:
            self.keep = [add_low(k, c) for k, c in zip(self.keep, came)]
            self.keep = self.send(2 - self.phase, self.keep)
        else:
            self.pieces = [self.keep[0], came[0], self.keep[1], came[1]]

    def finish_own(self, *layout):
        if self.rows != 4:
            return ()
        self.own = True
        return finish(self.line, self.order[::2], self.keep, *layout)

    def finish(self, *layout, **more):
        if self.phase < 3:
            self.advance()
        if self.own:
            return finish(self.line, self.order[1::2], self.pieces[1::2], *layout, **more)
        return finish(self.line, self.order, self.pieces, *layout, **more)


class SmallSum:
    def __init__(self, line, array, more, rows, tp):
        self.line, self.array, self.more = line, array, more
        self.steps = [("tp", 1 << i, tp) for i in range(tp.bit_length() - 1)]
        self.steps += [("rows", 1 << i, rows) for i in range(rows.bit_length() - 1)]
        self.send()

    def send(self):
        if self.steps:
            axis, step, size = self.steps.pop(0)
            if axis == "rows" and self.more is not None:
                self.array, self.more = jnp.concatenate([self.array, self.more]), None
            (self.array,) = self.line.join(self.array)
            self.came = lax.ppermute(self.array, axis, [(i, i ^ step) for i in range(size)])
        else:
            self.came = None

    def step(self):
        if self.came is not None:
            (came,) = self.line.join(self.came)
            self.array = self.array + came
            self.send()

    def rest(self):
        while self.came is not None:
            self.step()
        return self.array


class SmallGather:
    def __init__(self, line, array, me, tp):
        self.line, self.me, self.step = line, me, 1
        while 2 * self.step < tp:
            other = lax.ppermute(array, "tp", [(i, i ^ self.step) for i in range(tp)])
            array = self.laid(array, other)
            self.step *= 2
        (self.array,) = line.join(array)
        self.other = lax.ppermute(self.array, "tp", [(i, i ^ self.step) for i in range(tp)])

    def laid(self, array, other):
        return jnp.where(
            (self.me // self.step) % 2 == 0,
            jnp.concatenate([array, other]),
            jnp.concatenate([other, array]),
        )

    def whole(self):
        return self.line.join(self.laid(self.array, *self.line.join(self.other)))[0]


def token_sum(matrix):
    ones_row = jnp.ones((1, matrix.shape[0]), matrix.dtype)
    return jnp.dot(ones_row, matrix, preferred_element_type=jnp.float32)[0]


def local(
    rows,
    tp,
    hidden_in,
    segment_ids,
    ln_gain,
    ln_bias,
    w_qkv,
    b_qkv,
    w_out,
    out_bias,
    w_up,
    b_up,
    w_down,
    cotangent,
):
    x = hidden_in[0]
    block, width = x.shape
    length = block * tp
    local_width = w_qkv.shape[2]
    hidden = w_up.shape[1]
    chips = tp // 2
    me = lax.axis_index("tp")
    chip, core = me // 2, me % 2
    line = Line()

    around = [(i, (i + 2) % tp) for i in range(tp)]
    sibling = [(i, i ^ 1) for i in range(tp)]
    mine, others = [x], [lax.ppermute(x, "tp", sibling)]
    coming = lax.ppermute(x, "tp", around)
    ids = SmallGather(line, segment_ids[0], me, tp)

    def serve():
        nonlocal coming
        (arrived,) = line.join(coming)
        mine.append(arrived)
        if len(mine) < chips:
            coming = lax.ppermute(arrived, "tp", around)
        others.append(lax.ppermute(arrived, "tp", sibling))
    columns = width // 2
    serve()
    segments = ids.whole()
    starts = positions_of(segments)
    tables = rotary_tables(jnp.arange(length, dtype=jnp.int32) - starts)
    lows = starts[::block] // block
    starts = jnp.broadcast_to(starts[None], (8, length))
    w_three = jnp.transpose(w_qkv, (1, 0, 2))
    weights = (
        ln_gain.reshape(1, width),
        ln_bias.reshape(1, width),
        w_three,
        b_qkv.reshape(1, 3 * local_width),
        w_up,
        b_up.reshape(1, hidden),
    )
    carried = ()

    def project_slot(s, cost=0):
        place = jnp.stack([(chip - s + chips) % chips, core]).astype(jnp.int32)
        pair = line.join(mine[s], others[s])
        return project(line, place, *pair, weights, tables[:2], length, carried, cost)

    carried = project_slot(0)
    for s in range(1, chips):
        if s > 1:
            serve()
        if s != 1 or chips == 2:
            for t in (1, 2) if s == 2 else (s,):
                carried = project_slot(t, cost=920 * 10**8)
                if t == max(chips - 3, 1):
                    halves = line.join(cotangent[0, :, :columns], cotangent[0, :, columns:])
                    grads = [lax.all_gather(half, "tp", axis=0, tiled=True) for half in halves]
    normed, unit, mixed, activated, slope = carried

    hidden_parts, local_parts = hidden // 4, local_width // 4
    sums = partial(RowsSum, rows, line)
    context, lse = attend_forward(line, lows, starts, mixed, block)
    d0 = sums(activated, grads[0], context)
    branch = branch_sum(line, context, activated, w_out, w_down)
    d0.advance()
    (branch,) = line.join(branch)
    branch_total = lax.psum_scatter(branch, "tp", scatter_dimension=0, tiled=True)
    d1 = sums(activated, grads[1], context)
    d0.advance()
    grad_up, grad_context, grad_b_up = backward_products(line, grads, w_down, w_out, slope)
    d1.advance()
    up = sums(normed, grad_up, between=d0.advance)
    grad_mixed = attend_backward(
        line, lows, starts, lse, mixed, context, grad_context, *tables, block
    )
    d1.advance()
    up.advance()
    (branch_total,) = line.join(branch_total)
    part, gain_part, shift_part = normed_sum(line, grad_mixed, grad_up, unit, w_three, w_up)
    grad_normed = lax.psum_scatter(part, "tp", scatter_dimension=0, tiled=True)
    up.advance()
    three = sums(normed, grad_mixed, between=d1.advance)
    small = SmallSum(
        line,
        jnp.concatenate([gain_part, shift_part, token_sum(cotangent[0])[None]], axis=1)[0],
        jnp.concatenate([token_sum(grad_mixed), grad_b_up[0]]),
        rows,
        tp,
    )
    down = d0.finish([(hidden_parts, columns, width, 0), (local_parts, columns, width, 0)])
    small.step()
    down = d1.finish(
        [(hidden_parts, columns, width, 1), (local_parts, columns, width, 1)], carried=down
    )
    up.advance()
    three.advance()
    small.step()
    up = up.finish([(width // 4, hidden, hidden, 0)], cost=1092 * 10**8)
    three.advance()
    own = three.finish_own(3)
    small.step()
    small.step()
    three = three.finish(3, carried=own, cost=287 * 10**8)
    small = small.rest()
    grad_w_down, grad_w_out = down
    grad_w_up = up[0]
    grad_w_qkv = jnp.transpose(three[0], (1, 0, 2))

    inputs = x.astype(jnp.float32)
    hidden_out = (inputs + branch_total.astype(jnp.float32) + out_bias).astype(jnp.bfloat16)
    grad_input = norm_back(line, grad_normed, x, cotangent[0], ln_gain.reshape(1, width))
    tail = small[: 3 * width].reshape(3, width)
    grad_b_qkv = small[3 * width : 3 * (width + local_width)].reshape(3, local_width)
    grad_b_up = small[3 * (width + local_width) :]
    return (
        hidden_out[None],
        grad_input[None],
        tail[0],
        tail[1],
        grad_w_qkv,
        grad_b_qkv,
        grad_w_out,
        tail[2],
        grad_w_up,
        grad_b_up,
        grad_w_down,
    )


def solution(mesh):
    in_specs = (
        P("rows", "tp", None),
        P("rows", "tp"),
        P(),
        P(),
        P(None, None, "tp"),
        P(None, "tp"),
        P("tp", None),
        P(),
        P(None, "tp"),
        P("tp"),
        P("tp", None),
        P("rows", "tp", None),
    )
    out_specs = (
        P("rows", "tp", None),
        P("rows", "tp", None),
        P(),
        P(),
        P(None, None, "tp"),
        P(None, "tp"),
        P("tp", None),
        P(),
        P(None, "tp"),
        P("tp"),
        P("tp", None),
    )
    return jax.shard_map(
        partial(local, mesh.shape["rows"], mesh.shape["tp"]),
        mesh=mesh,
        in_specs=in_specs,
        out_specs=out_specs,
        check_vma=False,
    )
```
